32 devices in a mesh: group: 8 (over y, x, core), local: 4 (over z).
Axes of the slice: x: 2, y: 2, z: 4, core: 2. Of those that a mesh axis runs over, the one named last changes fastest.
Arguments:
- inputs: bfloat16 [8192, 768], P(('group', 'local')), may hold values from -6 to 6
- norm_one: bfloat16 [768], P(('group', 'local')), may hold values from 0.25 to 1.75
- w_query: bfloat16 [768, 768], P(('group', 'local')), may hold values from -0.21875 to 0.21875
- w_key: bfloat16 [768, 768], P(('group', 'local')), may hold values from -0.21875 to 0.21875
- w_value: bfloat16 [768, 768], P(('group', 'local')), may hold values from -0.21875 to 0.21875
- w_output: bfloat16 [768, 768], P(('group', 'local')), may hold values from -4 to 4
- norm_two: bfloat16 [768], P(('group', 'local')), may hold values from 0.25 to 1.75
- w_router: bfloat16 [768, 32], P(('group', 'local')), may hold values from -0.109375 to 0.109375
- expert_in: bfloat16 [32, 768, 3072], P(('group', 'local')), may hold values from -0.21875 to 0.21875
- expert_out: bfloat16 [32, 3072, 768], P(('group', 'local')), may hold values from -6 to 6
- routes: int32 [8192, 1], P(('group', 'local')), may hold values from 0 to 31; in each aligned block of 256 rows (0 to 255, 256 to 511, ...) at most 16 rows name the same one
- cotangent: bfloat16 [8192, 768], P(('group', 'local')), may hold values from -6 to 6
Outputs:
- output: bfloat16 [8192, 768], P(('group', 'local'))
- grad_input: float32 [8192, 768], P(('group', 'local'))
- grad_norm_one: float32 [768], P(('group', 'local'))
- grad_w_query: float32 [768, 768], P(('group', 'local'))
- grad_w_key: float32 [768, 768], P(('group', 'local'))
- grad_w_value: float32 [768, 768], P(('group', 'local'))
- grad_w_output: float32 [768, 768], P(('group', 'local'))
- grad_norm_two: float32 [768], P(('group', 'local'))
- grad_w_router: float32 [768, 32], P(('group', 'local'))
- grad_expert_in: float32 [32, 768, 3072], P(('group', 'local'))
- grad_expert_out: float32 [32, 3072, 768], P(('group', 'local'))
The draws below stay inside these ranges and needn't reach their ends.
Inputs may be any that keep to these rules, and one draw needn't show every extreme that they name: `routes`: in each aligned block of 256 rows (the rows of one device) no expert is named by more than 16 rows, a bound that some block reaches.
All inputs are finite; a program needn't handle non-finite values.
Results may differ from the reference program's by a relative error of at most 0.017.
Values may be sent and summed in bfloat16 or wider, within the bound.
No kernel may reach another device: no remote copies, remote signals or barrier semaphores. Data moves between devices by JAX's collectives and lax.ppermute only.
A program may use at most 128 MiB of HBM per device.

```python
import math
import jax
import jax.numpy as jnp
import numpy as np
from jax import lax

D = 768
HEADS = 12
HEAD_DIM = 64
FF = 3072
TOK_DEV = 256
EXPERTS = 32
TOKENS = 8192
SEQ_LEN = 1024
MOST = 16
CAP = 320


def steps_of(key, extent, cuts, least, top_value):
    factor_of = 1.0
    for dim, parts in cuts:
        heights = jax.random.uniform(jax.random.fold_in(jax.random.fold_in(key, 6), dim), (parts,), jnp.float32, least / len(cuts), top_value / len(cuts))
        factor_of = factor_of * jnp.repeat(jnp.exp(heights), extent[dim] // parts).reshape((-1,) + (1,) * (len(extent) - 1 - dim))
    return factor_of


def assign_block(key, own, number, rows, number_of, top, limit, slope):
    order = jax.random.permutation(key, number_of)
    crowded, common = shares(number_of, rows * top, limit, slope, True), shares(number_of, rows * top, limit, slope, False)
    places = jnp.arange(number_of)

    def named(tallies, turn):
        used = int((tallies > 0).sum())
        fixed = max(1, used // 4)
        passed = fixed + (places - fixed + turn * (used - fixed)) % max(1, number_of - fixed)
        return jnp.zeros((number_of,), jnp.int32).at[order[jnp.where(places < fixed, places, passed)]].set(jnp.asarray(tallies, jnp.int32))

    tallies = jnp.where(number % 4 == 0, named(crowded, number // 4), named(common, number - number // 4 - 1))
    mixed = jax.random.permutation(jax.random.fold_in(own, 3), number_of)
    source_of, receiver = mixed[0:number_of // 2 * 2:2], mixed[1:number_of // 2 * 2:2]
    room = jnp.minimum(tallies[source_of] - 1, limit - tallies[receiver]) // 2
    room = jnp.where((source_of == order[0]) | (receiver == order[0]) | (tallies[receiver] == 0), 0, jnp.maximum(room, 0))
    passed = jax.random.randint(jax.random.fold_in(own, 4), (number_of // 2,), 0, 1 << 20) % (room + 1)
    tallies = tallies.at[source_of].add(-passed).at[receiver].add(passed)
    labels = jnp.searchsorted(jnp.cumsum(tallies), jnp.arange(rows * top), side="right").astype(jnp.int32)
    grid = labels.reshape(top, rows).T
    grid = grid[jax.random.permutation(jax.random.fold_in(own, 1), rows)]
    turn = jax.random.randint(jax.random.fold_in(own, 2), (rows, 1), 0, top)
    return jnp.take_along_axis(grid, (jnp.arange(top)[None, :] + turn) % top, axis=1)


def shares(amount, total, bound, skew, full):
    weights = [(1 << 20) // math.isqrt(standing ** skew) + 1 for standing in range(1, amount + 1)]
    largest = bound if full else min(bound, max(-(-total // amount), total * weights[0] // sum(weights)))
    least = 1 if total - largest >= amount - 1 else 0
    counts, surplus = [largest] + [least] * (amount - 1), total - largest - least * (amount - 1)
    while surplus > 0:
        movable = [i for i in range(1, amount) if counts[i] < largest] or [i for i in range(1, amount) if counts[i] < bound]
        mass, left = sum([weights[i] for i in movable]), surplus
        for i in movable:
            addition = min(bound - counts[i], max(1, left * weights[i] // mass), surplus)
            counts[i] = counts[i] + addition
            surplus = surplus - addition
    return np.array(counts)


def noise(key, dims, scale, reach, split=(), held_as=jnp.bfloat16):
    values = scale * jax.random.normal(key, dims, jnp.float32)
    if split:
        values = values * steps_of(key, dims, split, -0.22, 0.18)
    return jnp.clip(values, -reach, reach).astype(held_as)


def setup_inputs(seed: int = 0) -> dict:
    keys = jax.random.split(jax.random.key(seed), 13)
    inputs = noise(keys[0], (TOKENS, D), 1.0, 6.0, ((0, 32),))
    norm_one = jnp.clip(1.0 + 0.15 * jax.random.normal(keys[1], (D,), jnp.float32), 0.25, 1.75).astype(jnp.bfloat16)
    w_query = noise(keys[2], (D, D), D ** -0.5, 0.21875, ((0, 32),))
    w_key = noise(keys[3], (D, D), D ** -0.5, 0.21875, ((0, 32),))
    w_value = noise(keys[4], (D, D), D ** -0.5, 0.21875, ((0, 32),))
    w_output = noise(keys[5], (D, D), 2 ** -0.5, 4.0, ((0, 32),))
    norm_two = jnp.clip(1.0 + 0.15 * jax.random.normal(keys[6], (D,), jnp.float32), 0.25, 1.75).astype(jnp.bfloat16)
    w_router = noise(keys[7], (D, EXPERTS), (4 * D) ** -0.5, 0.109375, ((0, 32),))
    expert_in = noise(keys[8], (EXPERTS, D, FF), D ** -0.5, 0.21875, ((0, 32),))
    expert_out = noise(keys[9], (EXPERTS, FF, D), (5 * EXPERTS * (4 * FF) ** -0.5), 6.0, ((0, 32),))
    routes_keys = jax.random.split(jax.random.fold_in(keys[10], 1), TOKENS // TOK_DEV)
    routes_turns = jax.random.permutation(jax.random.fold_in(keys[10], 3), TOKENS // TOK_DEV)
    routes = jax.vmap(lambda own, number: assign_block(jax.random.fold_in(keys[10], 2), own, number, TOK_DEV, EXPERTS, 1, MOST, 2))(routes_keys, routes_turns).reshape((TOKENS, 1))
    cotangent = noise(keys[11], (TOKENS, D), 1.0, 6.0, ((0, 32),))
    return dict(inputs=inputs, norm_one=norm_one, w_query=w_query, w_key=w_key, w_value=w_value, w_output=w_output, norm_two=norm_two, w_router=w_router, expert_in=expert_in, expert_out=expert_out, routes=routes, cotangent=cotangent)


@jax.custom_vjp
def low(v):
    return lax.optimization_barrier(v.astype(jnp.bfloat16)).astype(jnp.float32)

@jax.custom_vjp
def low_back(v):
    return v

def low_keep(v):
    return (low(v), None)

def low_pass(kept, grad):
    return (grad,)

def back_keep(v):
    return (v, None)

def back_low(kept, grad):
    return (low(grad),)
low.defvjp(low_keep, low_pass)
low_back.defvjp(back_keep, back_low)
epsilon = 1e-06
highest = lax.Precision.HIGHEST

def rms_normed(values, gain):
    return values * lax.rsqrt(lax.optimization_barrier(jnp.mean(values * values, axis=-1, keepdims=True)) + epsilon) * gain

def attend_sequence(packed):
    queries, keys_all, values_all = packed
    scores = jnp.einsum('qhd,khd->hqk', queries, keys_all, precision=highest) * HEAD_DIM ** (-0.5)
    scores = low_back(scores)
    probs = low(jax.nn.softmax(scores, axis=-1))
    return jnp.einsum('hqk,khd->qhd', probs, values_all, precision=highest)

def expert_apply(packed):
    rows_in, weight_in, weight_out = packed
    inner = low_back(jnp.dot(rows_in, weight_in, precision=highest))
    hidden = low(jax.nn.gelu(inner, approximate=True))
    return low(low_back(jnp.dot(hidden, weight_out, precision=highest)))

def forward(source, norm_one, w_query, w_key, w_value, w_output, norm_two, w_router, expert_in, expert_out, routes):
    first = low(rms_normed(source, norm_one))

    def project(weight):
        return low(low_back(jnp.dot(first, weight, precision=highest)))
    seq_shape = (TOKENS // SEQ_LEN, SEQ_LEN, HEADS, HEAD_DIM)
    queries = project(w_query).reshape(seq_shape)
    keys_all = project(w_key).reshape(seq_shape)
    values_all = project(w_value).reshape(seq_shape)
    mixed = lax.map(jax.checkpoint(attend_sequence), (queries, keys_all, values_all))
    mixed = low(low_back(mixed.reshape(TOKENS, D)))
    middle = source + low_back(jnp.dot(mixed, w_output, precision=highest))
    second = low(rms_normed(middle, norm_two))
    logits = low_back(jnp.dot(second, w_router, precision=highest))
    router_probs = jax.nn.softmax(logits, axis=-1)
    chosen = routes[:, 0].astype(jnp.int32)
    onehot = chosen[:, None] == jnp.arange(EXPERTS, dtype=jnp.int32)[None, :]
    gate = lax.optimization_barrier(jnp.sum(jnp.where(onehot, router_probs, jnp.zeros_like(router_probs)), axis=1))
    picked = onehot.astype(jnp.int32)
    slot = lax.optimization_barrier(jnp.sum((jnp.cumsum(picked, axis=0) - picked) * picked, axis=1)).astype(jnp.int32)
    slot = jnp.where(slot < CAP, slot, CAP).astype(jnp.int32)
    held = jnp.zeros((EXPERTS, CAP, D), second.dtype).at[chosen, slot].set(second, mode='drop')
    held = low_back(held)
    result = lax.map(jax.checkpoint(expert_apply), (held, expert_in, expert_out))
    taken = result.at[chosen, slot].get(mode='fill', fill_value=0.0)
    return middle + gate[:, None] * taken

def reference(inputs, norm_one, w_query, w_key, w_value, w_output, norm_two, w_router, expert_in, expert_out, routes, cotangent):
    params = tuple((member.astype(jnp.float32) for member in (inputs, norm_one, w_query, w_key, w_value, w_output, norm_two, w_router, expert_in, expert_out)))

    def wrapped(source, gain_one, query_w, key_w, value_w, out_w, gain_two, router_w, first_w, second_w):
        return forward(source, gain_one, query_w, key_w, value_w, out_w, gain_two, router_w, first_w, second_w, routes)
    output, pullback = jax.vjp(wrapped, *params)
    grads = pullback(cotangent.astype(jnp.float32))
    return (output.astype(jnp.bfloat16), grads[0], grads[1], grads[2], grads[3], grads[4], grads[5], grads[6], grads[7], grads[8], grads[9])
```

```python
import jax
import jax.numpy as jnp
from jax import lax
from jax.sharding import PartitionSpec as P

HEAD_DIM = 64
AXES = ("group", "local")
BF = jnp.bfloat16
F32 = jnp.float32
EPSILON = 1e-06


def dot(left, right):
    return jnp.dot(left, right, preferred_element_type=F32)


def dot_tn(left, right):
    return lax.dot_general(left, right, (((0,), (0,)), ((), ())), preferred_element_type=F32)


def dot_nt(left, right):
    return lax.dot_general(left, right, (((1,), (1,)), ((), ())), preferred_element_type=F32)


class Links:
    def __init__(self):
        self.groups = lax.axis_size("group")
        self.levels = lax.axis_size("local")
        self.bits = (self.groups // 2).bit_length() - 1
        self.group = lax.axis_index("group")
        self.level = lax.axis_index("local")
        self.core = self.group % 2

    def permute(self, array, target):
        pairs = []
        for group in range(self.groups):
            for level in range(self.levels):
                other_group, other_level = target(group, level)
                pairs.append((group * self.levels + level, other_group * self.levels + other_level))
        return lax.ppermute(array, AXES, pairs)

    def swap_core(self, array):
        return self.permute(array, lambda g, l: (g ^ 1, l))

    def swap_level(self, array, mask):
        return self.permute(array, lambda g, l: (g, l ^ mask))

    def stage_bit(self, core, stage):
        return 1 + (stage if core == 0 else self.bits - 1 - stage)

    def swap_stage(self, array, stage):
        return self.permute(array, lambda g, l: (g ^ (1 << self.stage_bit(g % 2, stage)), l))

    def my_stage_bit(self, stage):
        first = (self.group >> self.stage_bit(0, stage)) & 1
        second = (self.group >> self.stage_bit(1, stage)) & 1
        return jnp.where(self.core == 0, first, second)


def pick(flag, first, second):
    return jnp.where(flag == 0, first, second)


def joined(flag, mine, other, axis=0):
    return jnp.concatenate([pick(flag, mine, other), pick(flag, other, mine)], axis=axis)


def turned(links, array):
    bits = links.bits
    shape = (2,) * bits + array.shape[1:]
    order = tuple(reversed(range(bits))) + tuple(range(bits, len(shape)))
    grid = array.reshape(shape)
    return pick(links.core, grid, grid.transpose(order)).reshape(array.shape)


def gather_rows(links, piece, halves):
    level = links.level
    if halves:
        other = links.swap_level(pick(level & 1, piece[:, 1], piece[:, 0]), 1)
        piece = pick(level & 1, piece[:, 0], piece[:, 1])
        block = joined(level & 1, piece, other)
    else:
        block = joined(level & 1, piece, links.swap_level(piece, 1))
    block = joined(level >> 1, block, links.swap_level(block, 2))
    rows, width = block.shape
    for stage in range(links.bits):
        block = joined(links.my_stage_bit(stage), block, links.swap_stage(block, stage))
    block = turned(links, block.reshape(-1, rows, width))
    other = links.swap_core(block)
    both = jnp.stack([pick(links.core, block, other), pick(links.core, other, block)], axis=1)
    return both.reshape(-1, width)


def reduce_rows(links, partial, halves):
    level = links.level
    width = partial.shape[1]
    count = links.groups // 2
    grid = partial.reshape(count, 2, -1, width)
    other = links.swap_core(pick(links.core, grid[:, 1], grid[:, 0]).astype(BF))
    grid = pick(links.core, grid[:, 0], grid[:, 1])
    grid = turned(links, grid + other.astype(F32))
    block = grid.reshape(-1, width)
    for stage in reversed(range(links.bits)):
        bit = links.my_stage_bit(stage)
        pair = block.reshape(2, -1, width)
        other = links.swap_stage(pick(bit, pair[1], pair[0]).astype(BF), stage)
        block = pick(bit, pair[0], pair[1]) + other.astype(F32)
    pair = block.reshape(2, -1, width)
    other = links.swap_level(pick(level >> 1, pair[1], pair[0]).astype(BF), 2)
    block = pick(level >> 1, pair[0], pair[1]) + other.astype(F32)
    pair = block.reshape(2, -1, width)
    other = links.swap_level(pick(level & 1, pair[1], pair[0]).astype(BF), 1)
    mine = pick(level & 1, pair[0], pair[1])
    if halves:
        other = other.astype(F32)
        return jnp.stack([pick(level & 1, mine, other), pick(level & 1, other, mine)], axis=1)
    return mine + other.astype(F32)


def owner_to_workers(links, array):
    half = array.shape[0] // 2
    mine = pick(links.core, array[:half], array[half:])
    other = links.swap_core(pick(links.core, array[half:], array[:half]))
    same = (links.level >> 1) ^ links.core
    return pick(same, mine, other), pick(same, other, mine)


def workers_to_owner(links, near, far):
    same = (links.level >> 1) ^ links.core
    mine = pick(same, near, far)
    other = links.swap_core(pick(same, far, near))
    return joined(links.core, mine, other)


def attention_forward(queries, keys, values):
    rows, width = queries.shape
    heads = width // HEAD_DIM
    query_heads = queries.reshape(rows, heads, HEAD_DIM)
    key_heads = keys.reshape(-1, heads, HEAD_DIM)
    value_heads = values.reshape(-1, heads, HEAD_DIM)
    scores = jnp.einsum("qhd,khd->hqk", query_heads, key_heads, preferred_element_type=F32) * (
        HEAD_DIM**-0.5
    )
    top = jnp.max(scores, axis=-1, keepdims=True)
    weights = jnp.exp(scores - top)
    totals = jnp.sum(weights, axis=-1, keepdims=True)
    probs = (weights / totals).astype(BF)
    mixed = jnp.einsum("hqk,khd->qhd", probs, value_heads, preferred_element_type=F32)
    return mixed.reshape(rows, width).astype(BF), top + jnp.log(totals)


def attention_backward(queries, keys, values, log_total, grad_mixed):
    rows, width = queries.shape
    heads = width // HEAD_DIM
    factor = HEAD_DIM**-0.5
    query_heads = queries.reshape(rows, heads, HEAD_DIM)
    key_heads = keys.reshape(-1, heads, HEAD_DIM)
    value_heads = values.reshape(-1, heads, HEAD_DIM)
    grad_heads = grad_mixed.reshape(rows, heads, HEAD_DIM)
    scores = jnp.einsum("qhd,khd->hqk", query_heads, key_heads, preferred_element_type=F32) * factor
    probs = jnp.exp(scores - log_total)
    grad_probs = jnp.einsum("qhd,khd->hqk", grad_heads, value_heads, preferred_element_type=F32)
    row_dots = jnp.sum(probs * grad_probs, axis=-1, keepdims=True)
    grad_scores = (probs * (grad_probs - row_dots)).astype(BF)
    grad_queries = (
        jnp.einsum("hqk,khd->qhd", grad_scores, key_heads, preferred_element_type=F32) * factor
    )
    grad_keys = (
        jnp.einsum("hqk,qhd->khd", grad_scores, query_heads, preferred_element_type=F32) * factor
    )
    grad_values = jnp.einsum(
        "hqk,qhd->khd", probs.astype(BF), grad_heads, preferred_element_type=F32
    )
    return (
        grad_queries.reshape(rows, width).astype(BF),
        grad_keys.reshape(-1, width).astype(BF),
        grad_values.reshape(-1, width).astype(BF),
    )


GELU_SCALE = 0.7978845608028654
GELU_CUBE = 0.044715


def gelu_and_slope(values):
    square = values * values
    bend = jnp.tanh(GELU_SCALE * values * (1.0 + GELU_CUBE * square))
    half = 0.5 + 0.5 * bend
    slope = half + 0.5 * values * (1.0 - bend * bend) * GELU_SCALE * (1.0 + 3 * GELU_CUBE * square)
    return values * half, slope


def all_to_all(array):
    return lax.all_to_all(array, AXES, split_axis=0, concat_axis=0, tiled=True)


def on_device(
    inputs,
    norm_one,
    w_query,
    w_key,
    w_value,
    w_output,
    norm_two,
    w_router,
    expert_in,
    expert_out,
    routes,
    cotangent,
):
    links = Links()
    level, core = links.level, links.core
    device = links.group * links.levels + level
    devices = links.groups * links.levels
    rows, width = inputs.shape
    half_rows = rows // 2
    half_width = width // 2
    experts = w_router.shape[1]
    own_rows = norm_one.shape[0]
    most = 2 * rows // experts
    capacity = 5 * rows // 4
    blocks = links.levels

    chosen = routes[:, 0]
    picked = (chosen[:, None] == jnp.arange(experts, dtype=jnp.int32)[None, :]).astype(jnp.int32)
    rank = jnp.sum((jnp.cumsum(picked, axis=0) - picked) * picked, axis=1)
    tally = jnp.sum(picked, axis=0).astype(BF)
    place = chosen * most + rank
    to_slots = (jnp.arange(experts * most, dtype=jnp.int32)[:, None] == place[None, :]).astype(BF)
    flat = jnp.concatenate([norm_one, norm_two, w_router.reshape(-1)])
    small = jnp.concatenate(
        [jnp.broadcast_to(flat[None], (devices, flat.shape[0])), tally[:, None]], axis=1
    )
    padded = -(-small.shape[1] // 1024) * 1024
    small = jnp.pad(small, ((0, 0), (0, padded - small.shape[1])))
    small = all_to_all(small.reshape(devices, padded // 128, 128)).reshape(devices, padded)
    gain_one = small[:, :own_rows].reshape(width).astype(F32)
    gain_two = small[:, own_rows : 2 * own_rows].reshape(width).astype(F32)
    full_router = small[:, 2 * own_rows : 2 * own_rows + own_rows * experts].reshape(width, experts)
    counts = small[:, 2 * own_rows + own_rows * experts].astype(jnp.int32)

    piece = jnp.stack([w_query, w_key, w_value], axis=1).reshape(own_rows, 3, 2, half_width)
    piece = piece.transpose(0, 2, 1, 3).reshape(own_rows, 2, 3 * half_width)
    weights = gather_rows(links, piece, True)

    near, far = owner_to_workers(links, inputs)
    sources = [
        near,
        links.swap_level(near, 1),
        links.swap_level(far, 2),
        links.swap_level(far, 3),
    ]
    source = jnp.concatenate(sources, axis=0).astype(F32)
    first_low = (
        source * lax.rsqrt(jnp.mean(source * source, axis=-1, keepdims=True) + EPSILON) * gain_one
    ).astype(BF)
    projected = dot(first_low, weights).astype(BF)
    queries = projected[:, :half_width]
    pair_own = projected[:, half_width:]
    pair_all = jnp.concatenate([pair_own, links.swap_core(pair_own)], axis=0)
    keys, values = pair_all[:, :half_width], pair_all[:, half_width:]
    mixed_work, log_total = attention_forward(queries, keys, values)

    full_output = gather_rows(links, w_output, False)
    cot_slots = dot(to_slots, cotangent).astype(BF).reshape(experts, most, width)
    cot_arrived = all_to_all(cot_slots).reshape(-1, width)

    parts = mixed_work.reshape(blocks, half_rows, half_width)
    back = [parts[0]] + [links.swap_level(parts[b], b) for b in (1, 2, 3)]
    near = joined(level & 1, back[0], back[1], axis=1)
    far = joined(level & 1, back[2], back[3], axis=1)
    mixed_low = workers_to_owner(links, near, far)

    source_own = inputs.astype(F32)
    middle = source_own + dot(mixed_low, full_output)
    inverse = lax.rsqrt(jnp.mean(middle * middle, axis=-1, keepdims=True) + EPSILON)
    normed = middle * inverse
    second_low = (normed * gain_two).astype(BF)
    second_slots = dot(to_slots, second_low).astype(BF).reshape(experts, most, width)
    arrived = all_to_all(second_slots).reshape(-1, width)

    offsets = jnp.cumsum(counts) - counts
    within = jnp.arange(most, dtype=jnp.int32)[None, :]
    slot_grid = offsets[:, None] + within
    usable = (within < counts[:, None]) & (slot_grid < capacity)
    slot_flat = jnp.where(usable, slot_grid, -1).reshape(-1)
    compact = (jnp.arange(capacity, dtype=jnp.int32)[:, None] == slot_flat[None, :]).astype(BF)
    held = dot(compact, arrived).astype(BF)
    cot_held = dot(compact, cot_arrived)
    weight_in = expert_in[0]
    weight_out = expert_out[0]
    logits = dot(held, full_router)
    router_probs = jax.nn.softmax(logits, axis=-1)
    mine = (jnp.arange(experts, dtype=jnp.int32) == device).astype(F32)[None, :]
    gate = jnp.sum(router_probs * mine, axis=1, keepdims=True)
    grad_result = (gate * cot_held).astype(BF)
    inner = dot(held, weight_in)
    hidden, slope = gelu_and_slope(inner)
    hidden = hidden.astype(BF)
    result = dot(hidden, weight_out).astype(BF).astype(F32)
    grad_gate = jnp.sum(cot_held * result, axis=1, keepdims=True)
    grad_logits = (grad_gate * router_probs * (mine - gate)).astype(BF)
    grad_router = dot_tn(held, grad_logits)
    grad_inner = (dot_nt(grad_result, weight_out) * slope).astype(BF)
    grad_held = dot_nt(grad_inner, weight_in) + dot_nt(grad_logits, full_router)
    grad_back = dot_tn(compact, grad_held.astype(BF)).astype(BF).reshape(experts, most, width)
    grad_returned = all_to_all(grad_back).reshape(-1, width)
    grad_weight_out = dot_tn(hidden, grad_result)
    grad_weight_in = dot_tn(held, grad_inner)
    taken_back = dot_tn(compact, (gate * result).astype(BF)).astype(BF)
    taken_back = taken_back.reshape(experts, most, width)

    grad_out = cotangent.astype(F32)
    grad_second = dot_tn(to_slots, grad_returned)
    scaled = grad_second * gain_two
    grad_gain_two = jnp.sum(grad_second * normed, axis=0)
    grad_middle = grad_out + inverse * (
        scaled - normed * jnp.mean(scaled * normed, axis=-1, keepdims=True)
    )
    grad_branch = grad_middle.astype(BF)
    grad_mixed = dot_nt(grad_branch, full_output).astype(BF)
    near, far = owner_to_workers(links, grad_mixed)
    half = level & 1
    near_same = pick(half, near[:, :half_width], near[:, half_width:])
    near_other = pick(half, near[:, half_width:], near[:, :half_width])
    far_same = pick(half, far[:, :half_width], far[:, half_width:])
    far_other = pick(half, far[:, half_width:], far[:, :half_width])
    grad_mixed_work = jnp.concatenate(
        [
            near_same,
            links.swap_level(near_other, 1),
            links.swap_level(far_same, 2),
            links.swap_level(far_other, 3),
        ],
        axis=0,
    )
    grad_w_output = reduce_rows(links, dot_tn(mixed_low, grad_branch), False)
    grad_queries, grad_keys, grad_values = attention_backward(
        queries, keys, values, log_total, grad_mixed_work
    )
    grad_pair = jnp.concatenate([grad_keys, grad_values], axis=1)
    work_rows = blocks * half_rows
    grad_pair_other = links.swap_core(grad_pair[work_rows:])
    grad_pair = (grad_pair[:work_rows].astype(F32) + grad_pair_other.astype(F32)).astype(BF)
    grad_projected = jnp.concatenate([grad_queries, grad_pair], axis=1)
    grad_first_work = dot_nt(grad_projected, weights).astype(BF)
    parts = grad_first_work.reshape(blocks, half_rows, width)
    back = [parts[0]] + [links.swap_level(parts[b], b) for b in (1, 2, 3)]
    back = [part.astype(F32) for part in back]
    grad_first = workers_to_owner(
        links, (back[0] + back[1]).astype(BF), (back[2] + back[3]).astype(BF)
    ).astype(F32)
    inverse_one = lax.rsqrt(jnp.mean(source_own * source_own, axis=-1, keepdims=True) + EPSILON)
    normed_one = source_own * inverse_one
    scaled_one = grad_first * gain_one
    grad_input = grad_middle + inverse_one * (
        scaled_one - normed_one * jnp.mean(scaled_one * normed_one, axis=-1, keepdims=True)
    )
    grad_weights = reduce_rows(links, dot_tn(first_low, grad_projected), True)
    grad_weights = grad_weights.reshape(own_rows, 2, 3, half_width).transpose(2, 0, 1, 3)
    grad_weights = grad_weights.reshape(3, own_rows, width)

    taken = dot_tn(to_slots, all_to_all(taken_back).reshape(-1, width))
    output = (middle + taken).astype(BF)

    sums = jnp.concatenate(
        [grad_gain_two.reshape(devices, own_rows), grad_router.reshape(devices, -1)], axis=1
    )
    padded = -(-sums.shape[1] // 1024) * 1024
    sums_in = jnp.pad(sums, ((0, 0), (0, padded - sums.shape[1])))
    sums_in = all_to_all(sums_in.reshape(devices, padded // 128, 128)).reshape(devices, padded)
    sums_own = jnp.sum(sums_in, axis=0)
    grad_norm_two = sums_own[:own_rows]
    grad_w_router = sums_own[own_rows : own_rows + own_rows * experts].reshape(own_rows, experts)
    stacked = jnp.stack([w_query, w_key, w_value]).astype(F32)
    grad_norm_one = jnp.sum(stacked * grad_weights, axis=(0, 2)) / norm_one.astype(F32)
    return (
        output,
        grad_input,
        grad_norm_one,
        grad_weights[0],
        grad_weights[1],
        grad_weights[2],
        grad_w_output,
        grad_norm_two,
        grad_w_router,
        grad_weight_in[None],
        grad_weight_out[None],
    )


def solution(mesh):
    return jax.shard_map(
        on_device,
        mesh=mesh,
        in_specs=(
            P(AXES, None),
            P(AXES),
            P(AXES, None),
            P(AXES, None),
            P(AXES, None),
            P(AXES, None),
            P(AXES),
            P(AXES, None),
            P(AXES, None, None),
            P(AXES, None, None),
            P(AXES, None),
            P(AXES, None),
        ),
        out_specs=(
            P(AXES, None),
            P(AXES, None),
            P(AXES),
            P(AXES, None),
            P(AXES, None),
            P(AXES, None),
            P(AXES, None),
            P(AXES),
            P(AXES, None),
            P(AXES, None, None),
            P(AXES, None, None),
        ),
        check_vma=False,
    )
```

```python
import functools

import jax
import jax.numpy as jnp
from jax import lax
from jax.experimental import pallas as pl
from jax.experimental.pallas import tpu as pltpu
from jax.sharding import PartitionSpec as P

HEAD_DIM = 64
AXES = ("group", "local")
BF = jnp.bfloat16
F32 = jnp.float32
EPSILON = 1e-06
VMEM_BYTES = 58 * 2**20
SMALL_BYTES = 24 * 2**20


def dot(left, right):
    return jnp.dot(left, right, preferred_element_type=F32)


def dot_tn(left, right):
    return lax.dot_general(left, right, (((0,), (0,)), ((), ())), preferred_element_type=F32)


def dot_nt(left, right):
    return lax.dot_general(left, right, (((1,), (1,)), ((), ())), preferred_element_type=F32)


class Links:
    def __init__(self):
        self.groups = lax.axis_size("group")
        self.levels = lax.axis_size("local")
        self.group = lax.axis_index("group")
        self.level = lax.axis_index("local")
        self.core = self.group % 2

    def permute(self, array, target):
        pairs = []
        for group in range(self.groups):
            for level in range(self.levels):
                other_group, other_level = target(group, level)
                pairs.append((group * self.levels + level, other_group * self.levels + other_level))
        return lax.ppermute(array, AXES, pairs)

    def swap_core(self, array):
        return self.permute(array, lambda g, l: (g ^ 1, l))

    def swap_level(self, array, mask):
        return self.permute(array, lambda g, l: (g, l ^ mask))

    def swap_group(self, array, mask):
        return self.permute(array, lambda g, l: (g ^ (2 * mask), l))


def gate(array, *after):
    return lax.optimization_barrier((array, *after))[0]


def tie(*arrays):
    return lax.optimization_barrier(arrays)


def pick(flag, first, second):
    return jnp.where(flag == 0, first, second)


def joined(flag, mine, other, axis=0):
    return jnp.concatenate([pick(flag, mine, other), pick(flag, other, mine)], axis=axis)


def ordered(index, parts):
    count = len(parts)
    if count == 1:
        return parts[0]
    top = count.bit_length() - 2
    half = count // 2
    low = index & (half - 1)
    return joined((index >> top) & 1, ordered(low, parts[:half]), ordered(low, parts[half:]))


def rows_of(array, index, rows):
    return lax.dynamic_slice_in_dim(array, index * rows, rows, axis=0)


def gather_levels(links, pieces):
    got = tie(*[links.swap_level(pieces[b], b) for b in range(1, links.levels)])
    return ordered(links.level, [pieces[0], *got])


def gather_groups(links, block):
    return [block] + [links.swap_group(block, m) for m in range(1, links.groups // 2)]


def in_order(links, own, other):
    pairs = [joined(links.core, mine, far) for mine, far in zip(own, other)]
    return ordered(links.group >> 1, pairs)


def reduce_cores(links, keep, send):
    return keep + links.swap_core(send).astype(F32)


def reduce_groups(links, parts):
    got = [links.swap_group(parts[m].astype(BF), m) for m in range(1, len(parts))]
    total = parts[0]
    for part in tie(*got):
        total = total + part.astype(F32)
    return total


def reduce_levels(links, block):
    rows = block.shape[0] // links.levels
    parts = [rows_of(block, links.level ^ b, rows) for b in range(links.levels)]
    got = tie(*[links.swap_level(parts[b].astype(BF), b) for b in range(1, links.levels)])
    return [parts[0]] + [part.astype(F32) for part in got]


def owner_to_workers(links, array):
    half = array.shape[0] // 2
    mine = pick(links.core, array[:half], array[half:])
    other = links.swap_core(pick(links.core, array[half:], array[:half]))
    same = (links.level >> 1) ^ links.core
    return pick(same, mine, other), pick(same, other, mine)


def workers_to_owner(links, near, far):
    same = (links.level >> 1) ^ links.core
    mine = pick(same, near, far)
    other = links.swap_core(pick(same, far, near))
    return joined(links.core, mine, other)


PAIR = 2 * HEAD_DIM


def head_masks(dtype):
    lanes = lax.broadcasted_iota(jnp.int32, (1, PAIR), 1)
    return [(lanes // HEAD_DIM == head).astype(dtype) for head in range(2)]


def forward_kernel(
    query_ref, key_ref, value_ref, key_far_ref, value_far_ref, zero_ref, one_ref, two_ref, three_ref, probs_ref
):
    rows = query_ref.shape[0]
    query = query_ref[...] * BF(HEAD_DIM**-0.5)
    key = jnp.concatenate([key_ref[...], key_far_ref[...]], axis=0)
    value = jnp.concatenate([value_ref[...], value_far_ref[...]], axis=0)
    mixed = jnp.zeros((rows, PAIR), F32)
    for head, mask in enumerate(head_masks(BF)):
        scores = dot_nt(query * mask, key)
        weights = jnp.exp(scores - jnp.max(scores, axis=1, keepdims=True))
        probs = (weights * (1.0 / jnp.sum(weights, axis=1, keepdims=True))).astype(BF)
        probs_ref[head] = probs
        mixed = mixed + dot(probs, value * mask)
    mixed = mixed.astype(BF)
    part_rows = rows // 4
    for part, ref in enumerate((zero_ref, one_ref, two_ref, three_ref)):
        ref[...] = mixed[part * part_rows : (part + 1) * part_rows]


def pair_column(rows, block=0):
    return pl.BlockSpec((rows, PAIR), lambda i: (0, block + i))


def probs_block(rows):
    return pl.BlockSpec((2, rows, 2 * rows), lambda i: (i, 0, 0))


def attention_forward(queries, pair, pair_far):
    rows, half_width = queries.shape
    pairs = half_width // PAIR
    return pl.pallas_call(
        forward_kernel,
        grid=(pairs,),
        in_specs=[pair_column(rows)] + [pair_column(rows), pair_column(rows, pairs)] * 2,
        out_specs=[pair_column(rows // 4)] * 4 + [probs_block(rows)],
        out_shape=[jax.ShapeDtypeStruct((rows // 4, half_width), BF)] * 4
        + [jax.ShapeDtypeStruct((2 * pairs, rows, 2 * rows), BF)],
        compiler_params=params(),
        cost_estimate=cost(2 * 10**10, 4096),
    )(queries, pair, pair, pair_far, pair_far)


def backward_kernel(query_ref, key_ref, value_ref, key_far_ref, value_far_ref, probs_ref, *refs):
    grad_refs, mixed_refs = refs[:4], refs[4:8]
    grad_query_ref, grad_near_ref, grad_far_ref = refs[8:]
    rows = query_ref.shape[0]
    factor = BF(HEAD_DIM**-0.5)
    query = query_ref[...] * factor
    key = jnp.concatenate([key_ref[...], key_far_ref[...]], axis=0)
    value = jnp.concatenate([value_ref[...], value_far_ref[...]], axis=0)
    grad = jnp.concatenate([ref[...] for ref in grad_refs], axis=0)
    mixed = jnp.concatenate([ref[...] for ref in mixed_refs], axis=0)
    together = grad.astype(F32) * mixed.astype(F32)
    grad_query = jnp.zeros((rows, PAIR), F32)
    grad_key = jnp.zeros((2 * rows, PAIR), F32)
    grad_value = jnp.zeros((2 * rows, PAIR), F32)
    for head, (mask, mask_wide) in enumerate(zip(head_masks(BF), head_masks(F32))):
        probs = probs_ref[head]
        grad_one = grad * mask
        row_dots = jnp.sum(together * mask_wide, axis=1, keepdims=True)
        grad_probs = dot_nt(grad_one, value)
        grad_scores = (probs.astype(F32) * (grad_probs - row_dots)).astype(BF)
        grad_value = grad_value + dot_tn(probs, grad_one)
        grad_key = grad_key + dot_tn(grad_scores, query * mask)
        grad_query = grad_query + dot(grad_scores, key * (mask * factor))
    grad_query_ref[...] = grad_query.astype(BF)
    for index, total in enumerate((grad_key, grad_value)):
        grad_near_ref[index] = total[:rows].astype(BF)
        grad_far_ref[index] = total[rows:].astype(BF)


def attention_backward(queries, pair, pair_far, probs, grads, mixed):
    rows, half_width = queries.shape
    pairs = half_width // PAIR
    return pl.pallas_call(
        backward_kernel,
        grid=(pairs,),
        in_specs=[pair_column(rows)]
        + [pair_column(rows), pair_column(rows, pairs)] * 2
        + [probs_block(rows)]
        + [pair_column(rows // 4)] * 8,
        out_specs=[pair_column(rows)] + [pl.BlockSpec((2, rows, PAIR), lambda i: (0, 0, i))] * 2,
        out_shape=[jax.ShapeDtypeStruct((rows, half_width), BF)]
        + [jax.ShapeDtypeStruct((2, rows, half_width), BF)] * 2,
        compiler_params=params(),
        cost_estimate=cost(2 * 10**10, 4096),
    )(queries, pair, pair, pair_far, pair_far, probs, *grads, *mixed)


GELU_SCALE = 0.7978845608028654
GELU_CUBE = 0.044715


def gelu_and_slope(values):
    square = values * values
    bend = jnp.tanh(GELU_SCALE * values * (1.0 + GELU_CUBE * square))
    half = 0.5 + 0.5 * bend
    slope = half + 0.5 * values * (1.0 - bend * bend) * GELU_SCALE * (1.0 + 3 * GELU_CUBE * square)
    return values * half, slope


def whole(shape):
    return pl.BlockSpec(shape, lambda *_: (0,) * len(shape))


FLAGS = pl.BlockSpec(memory_space=pltpu.SMEM)
CORE, HALF, SAME, DEVICE, PLACE = range(5)


def params(size=VMEM_BYTES):
    return pltpu.CompilerParams(vmem_limit_bytes=size)


def cost(flops, size):
    return pl.CostEstimate(flops=flops, bytes_accessed=size, transcendentals=0)


def one_step(kernel, flags, operands, shapes, scratch=(), size=VMEM_BYTES):
    return pl.pallas_call(
        kernel,
        grid=(1,),
        in_specs=[FLAGS] + [whole(operand.shape) for operand in operands],
        out_specs=[whole(shape.shape) for shape in shapes],
        out_shape=shapes,
        scratch_shapes=list(scratch),
        compiler_params=params(size),
        cost_estimate=cost(0, 2**20),
    )(flags, *operands)


def low_shape(*shape):
    return jax.ShapeDtypeStruct(shape, BF)


def wide_shape(*shape):
    return jax.ShapeDtypeStruct(shape, F32)


def each_case(flags_ref, body):
    for half in range(2):
        for same in range(2):

            @pl.when((flags_ref[HALF] == half) & (flags_ref[SAME] == same))
            def _(half=half, same=same):
                body(half, same)


def project_kernel(count, flags_ref, normed_ref, *refs):
    own_refs, other_refs = refs[:count], refs[count : 2 * count]
    query_ref, pair_ref, weight_ref = refs[2 * count :]
    rows = own_refs[0].shape[0]
    core = flags_ref[CORE]
    for m in range(count):
        place = 2 * (flags_ref[PLACE] ^ m)
        for index, ref in ((place + core, own_refs[m]), (place + 1 - core, other_refs[m])):
            weight_ref[pl.ds(pl.multiple_of(index * rows, 16), rows), :] = ref[...]
    projected = dot(normed_ref[...], weight_ref[...]).astype(BF)
    query_ref[...] = projected[:, : query_ref.shape[1]]
    pair_ref[...] = projected[:, query_ref.shape[1] :]


def project(flags, normed, own, other):
    count = len(own)
    rows, width = normed.shape
    columns = own[0].shape[1]
    shapes = [
        low_shape(rows, columns // 3),
        low_shape(rows, columns * 2 // 3),
        low_shape(width, columns),
    ]
    kernel = functools.partial(project_kernel, count)
    return one_step(kernel, flags, [normed, *own, *other], shapes, size=SMALL_BYTES)


def mixed_route_kernel(flags_ref, zero_ref, one_ref, two_ref, three_ref, mine_ref, sent_ref):
    half_width = zero_ref.shape[1]

    def body(half, same):
        near_ref, far_ref = (mine_ref, sent_ref) if same == 0 else (sent_ref, mine_ref)
        for into_ref, refs in ((near_ref, (zero_ref, one_ref)), (far_ref, (two_ref, three_ref))):
            into_ref[:, :half_width] = refs[half][...]
            into_ref[:, half_width:] = refs[1 - half][...]

    each_case(flags_ref, body)


def mixed_route(flags, parts):
    rows, half_width = parts[0].shape
    shapes = [low_shape(rows, 2 * half_width)] * 2
    return one_step(mixed_route_kernel, flags, parts, shapes, size=SMALL_BYTES)


def grad_route_kernel(flags_ref, mine_ref, got_ref, zero_ref, one_ref, two_ref, three_ref):
    half_width = zero_ref.shape[1]

    def body(half, same):
        near_ref, far_ref = (mine_ref, got_ref) if same == 0 else (got_ref, mine_ref)
        for from_ref, refs in ((near_ref, (zero_ref, one_ref)), (far_ref, (two_ref, three_ref))):
            refs[half][...] = from_ref[:, :half_width]
            refs[1 - half][...] = from_ref[:, half_width:]

    each_case(flags_ref, body)


def grad_route(flags, mine, got):
    rows, width = mine.shape
    shapes = [low_shape(rows, width // 2)] * 4
    return one_step(grad_route_kernel, flags, [mine, got], shapes, size=SMALL_BYTES)


def owner_forward_kernel(
    flags_ref,
    mine_ref,
    got_ref,
    inputs_ref,
    weight_ref,
    gain_ref,
    to_slots_ref,
    mixed_ref,
    middle_ref,
    slots_ref,
):
    half_rows = mine_ref.shape[0]
    for core in range(2):

        @pl.when(flags_ref[CORE] == core)
        def _(core=core):
            refs = (mine_ref, got_ref)
            mixed_ref[:half_rows] = refs[core][...]
            mixed_ref[half_rows:] = refs[1 - core][...]

    weight = weight_ref[:, : mixed_ref.shape[1]]
    middle = inputs_ref[...].astype(F32) + dot(mixed_ref[...], weight)
    middle_ref[...] = middle
    inverse = lax.rsqrt(jnp.mean(middle * middle, axis=1, keepdims=True) + EPSILON)
    second_low = (middle * inverse * gain_ref[...]).astype(BF)
    slots_ref[...] = dot(to_slots_ref[...], second_low).astype(BF)


def owner_forward(flags, mine, got, inputs, full_extra, gain, to_slots):
    rows, width = inputs.shape
    shapes = [
        low_shape(rows, width),
        wide_shape(rows, width),
        low_shape(to_slots.shape[0], width),
    ]
    operands = [mine, got, inputs, full_extra, gain, to_slots]
    return one_step(owner_forward_kernel, flags, operands, shapes)


def expert_kernel(
    flags_ref,
    arrived_ref,
    cot_ref,
    compact_ref,
    expand_ref,
    router_ref,
    weight_in_ref,
    weight_out_ref,
    held_ref,
    grad_result_ref,
    hidden_ref,
    grad_inner_ref,
    grad_back_ref,
    taken_back_ref,
    grad_logits_ref,
    result_sum,
    grad_sum,
    cot_held,
    probs,
    gates,
):
    step = pl.program_id(0)
    experts = router_ref.shape[1]
    lanes = lax.broadcasted_iota(jnp.int32, (1, experts), 1)
    mine = (lanes == flags_ref[DEVICE]).astype(F32)

    @pl.when(step == 0)
    def _():
        held = dot(compact_ref[...], arrived_ref[...]).astype(BF)
        held_ref[...] = held
        cot = dot(compact_ref[...], cot_ref[...])
        cot_held[...] = cot
        logits = dot(held, router_ref[...])
        weights = jnp.exp(logits - jnp.max(logits, axis=1, keepdims=True))
        router_probs = weights / jnp.sum(weights, axis=1, keepdims=True)
        probs[...] = router_probs
        gate = jnp.sum(router_probs * mine, axis=1, keepdims=True)
        gates[...] = gate
        grad_result_ref[...] = (gate * cot).astype(BF)
        result_sum[...] = jnp.zeros_like(result_sum)
        grad_sum[...] = jnp.zeros_like(grad_sum)

    weight_in = weight_in_ref[0]
    weight_out = weight_out_ref[0]
    hidden, slope = gelu_and_slope(dot(held_ref[...], weight_in))
    hidden = hidden.astype(BF)
    hidden_ref[...] = hidden
    grad_inner = (dot_nt(grad_result_ref[...], weight_out) * slope).astype(BF)
    grad_inner_ref[...] = grad_inner
    result_sum[...] += dot(hidden, weight_out)
    grad_sum[...] += dot_nt(grad_inner, weight_in)

    @pl.when(step == pl.num_programs(0) - 1)
    def _():
        result = result_sum[...].astype(BF).astype(F32)
        gate = gates[...]
        grad_gate = jnp.sum(cot_held[...] * result, axis=1, keepdims=True)
        grad_logits = (grad_gate * probs[...] * (mine - gate)).astype(BF)
        grad_logits_ref[...] = grad_logits
        grad_held = grad_sum[...] + dot_nt(grad_logits, router_ref[...])
        grad_back_ref[...] = dot(expand_ref[...], grad_held.astype(BF)).astype(BF)
        taken_back_ref[...] = dot(expand_ref[...], (gate * result).astype(BF)).astype(BF)


def expert_layer(flags, arrived, cot, compact, expand, router, expert_in, expert_out):
    slots, width = arrived.shape
    capacity = compact.shape[0]
    hidden_width = expert_in.shape[2]
    experts = router.shape[1]
    tile = 1024
    wide = whole((capacity, width))
    tall = pl.BlockSpec((capacity, tile), lambda i: (0, i))
    return pl.pallas_call(
        expert_kernel,
        grid=(hidden_width // tile,),
        in_specs=[
            FLAGS,
            whole((slots, width)),
            whole((slots, width)),
            whole((capacity, slots)),
            whole((slots, capacity)),
            whole((width, experts)),
            pl.BlockSpec((1, width, tile), lambda i: (0, 0, i)),
            pl.BlockSpec((1, tile, width), lambda i: (0, i, 0)),
        ],
        out_specs=[wide, wide, tall, tall, whole((slots, width)), whole((slots, width))]
        + [whole((capacity, experts))],
        out_shape=[
            jax.ShapeDtypeStruct((capacity, width), BF),
            jax.ShapeDtypeStruct((capacity, width), BF),
            jax.ShapeDtypeStruct((capacity, hidden_width), BF),
            jax.ShapeDtypeStruct((capacity, hidden_width), BF),
            jax.ShapeDtypeStruct((slots, width), BF),
            jax.ShapeDtypeStruct((slots, width), BF),
            jax.ShapeDtypeStruct((capacity, experts), BF),
        ],
        scratch_shapes=[
            pltpu.VMEM((capacity, width), F32),
            pltpu.VMEM((capacity, width), F32),
            pltpu.VMEM((capacity, width), F32),
            pltpu.VMEM((capacity, experts), F32),
            pltpu.VMEM((capacity, 1), F32),
        ],
        compiler_params=params(),
        cost_estimate=cost(8 * capacity * width * hidden_width, 8 * width * hidden_width),
    )(flags, arrived, cot, compact, expand, router, expert_in, expert_out)


def owner_backward_kernel(
    flags_ref,
    returned_ref,
    to_tokens_ref,
    cotangent_ref,
    middle_ref,
    gain_ref,
    weight_ref,
    grad_middle_ref,
    grad_branch_ref,
    mine_ref,
    sent_ref,
    grad_gain_ref,
):
    half_rows = mine_ref.shape[0]
    middle = middle_ref[...]
    inverse = lax.rsqrt(jnp.mean(middle * middle, axis=1, keepdims=True) + EPSILON)
    normed = middle * inverse
    grad_second = dot(to_tokens_ref[...], returned_ref[...])
    grouped = (grad_second * normed).reshape(-1, GAIN_ROWS, grad_second.shape[1])
    grad_gain_ref[...] = jnp.sum(grouped, axis=0).astype(BF)
    scaled = grad_second * gain_ref[...]
    grad_middle = cotangent_ref[...].astype(F32) + inverse * (
        scaled - normed * jnp.mean(scaled * normed, axis=1, keepdims=True)
    )
    grad_middle_ref[...] = grad_middle
    grad_branch = grad_middle.astype(BF)
    grad_branch_ref[...] = grad_branch
    weight = weight_ref[:, : middle.shape[1]]
    grad_mixed = dot_nt(grad_branch, weight).astype(BF)
    for core in range(2):

        @pl.when(flags_ref[CORE] == core)
        def _(core=core):
            mine_ref[...] = grad_mixed[core * half_rows : (core + 1) * half_rows]
            sent_ref[...] = grad_mixed[(1 - core) * half_rows : (2 - core) * half_rows]


def owner_backward(flags, returned, to_tokens, cotangent, middle, gain, full_extra):
    rows, width = cotangent.shape
    shapes = [
        wide_shape(rows, width),
        low_shape(rows, width),
        low_shape(rows // 2, width),
        low_shape(rows // 2, width),
        low_shape(GAIN_ROWS, width),
    ]
    operands = [returned, to_tokens, cotangent, middle, gain, full_extra]
    return one_step(owner_backward_kernel, flags, operands, shapes)


GAIN_ROWS = 16


def deal_rows(flags_ref, total, keep_ref, send_ref, rows):
    core = flags_ref[CORE]
    for m in range(total.shape[0] // (2 * rows)):
        place = 2 * (flags_ref[PLACE] ^ m)
        keep_ref[m * rows : (m + 1) * rows, :] = total[
            pl.ds(pl.multiple_of((place + core) * rows, 8), rows), :
        ]
        send_ref[m * rows : (m + 1) * rows, :] = total[
            pl.ds(pl.multiple_of((place + 1 - core) * rows, 8), rows), :
        ].astype(BF)


def dealt(width, columns):
    return [wide_shape(width // 2, columns), low_shape(width // 2, columns)]


def output_grads_kernel(
    rows, flags_ref, mixed_ref, branch_ref, router_ref, gain_ref, keep_ref, send_ref, total
):
    width, experts = router_ref.shape
    extra = total.shape[1] - width
    total[:, :width] = dot_tn(mixed_ref[...], branch_ref[...])
    gain = dot_tn(gain_ref[...], jnp.ones((GAIN_ROWS, extra), BF))
    router = router_ref[...]
    router = jnp.concatenate([router, jnp.zeros((width, extra - experts), F32)], axis=1)
    lanes = lax.broadcasted_iota(jnp.int32, (1, extra), 1)
    total[:, width:] = jnp.where(lanes == experts, gain, router)
    deal_rows(flags_ref, total, keep_ref, send_ref, rows)


def output_grads(flags, mixed, branch, router, gain_rows, rows):
    width, experts = router.shape
    columns = width + experts + 1
    columns += -columns % 128
    return one_step(
        functools.partial(output_grads_kernel, rows),
        flags,
        [mixed, branch, router, gain_rows],
        dealt(width, columns),
        [pltpu.VMEM((width, columns), F32)],
        SMALL_BYTES,
    )


def weight_grads_kernel(
    rows,
    flags_ref,
    normed_ref,
    query_ref,
    near_ref,
    got_ref,
    projected_ref,
    keep_ref,
    send_ref,
    total,
):
    part = query_ref.shape[1]
    projected_ref[:, :part] = query_ref[...]
    for index in range(2):
        both = near_ref[index].astype(F32) + got_ref[index].astype(F32)
        projected_ref[:, (index + 1) * part : (index + 2) * part] = both.astype(BF)
    total[...] = dot_tn(normed_ref[...], projected_ref[...])
    deal_rows(flags_ref, total, keep_ref, send_ref, rows)


def weight_grads(flags, normed, query, near, got, rows):
    work_rows, width = normed.shape
    columns = 3 * query.shape[1]
    return one_step(
        functools.partial(weight_grads_kernel, rows),
        flags,
        [normed, query, near, got],
        [low_shape(work_rows, columns)] + dealt(width, columns),
        [pltpu.VMEM((width, columns), F32)],
        SMALL_BYTES,
    )


def all_to_all(array):
    return lax.all_to_all(array, AXES, split_axis=0, concat_axis=0, tiled=True)


def on_device(
    inputs,
    norm_one,
    w_query,
    w_key,
    w_value,
    w_output,
    norm_two,
    w_router,
    expert_in,
    expert_out,
    routes,
    cotangent,
):
    links = Links()
    level, core = links.level, links.core
    device = links.group * links.levels + level
    devices = links.groups * links.levels
    rows, width = inputs.shape
    half_rows = rows // 2
    half_width = width // 2
    experts = w_router.shape[1]
    own_rows = norm_one.shape[0]
    most = 2 * rows // experts
    capacity = 5 * rows // 4
    blocks = links.levels

    same = (level >> 1) ^ core
    flags = jnp.stack([core, level & 1, same, device, links.group >> 1]).astype(jnp.int32)

    mine = pick(core, inputs[:half_rows], inputs[half_rows:])
    got = links.swap_core(pick(core, inputs[half_rows:], inputs[:half_rows]))
    scale = norm_one.astype(F32)[:, None]
    scaled = [(w.astype(F32) * scale).astype(BF) for w in (w_query, w_key, w_value)]
    low = jnp.concatenate([w[:, :half_width] for w in scaled], axis=1)
    high = jnp.concatenate([w[:, half_width:] for w in scaled], axis=1)
    kept, cross = pick(level & 1, low, high), pick(level & 1, high, low)
    chosen = routes[:, 0]
    picked = (chosen[:, None] == jnp.arange(experts, dtype=jnp.int32)[None, :]).astype(jnp.int32)
    tally = jnp.sum(picked, axis=0).astype(BF)
    extra = jnp.concatenate(
        [w_output, w_router, jnp.broadcast_to(tally[None], (own_rows, experts)), norm_two[:, None]],
        axis=1,
    )
    extra = jnp.pad(extra, ((0, 0), (0, -extra.shape[1] % 128)))
    kept = jnp.concatenate([kept, extra], axis=1)
    cross = jnp.concatenate([cross, extra], axis=1)
    level_block = gather_levels(links, [kept, cross, kept, cross])
    level_rows = level_block.shape[0]
    level_weights = level_block[:, : 3 * half_width]
    got = gate(got, kept, cross)
    near, far = pick(same, mine, got), pick(same, got, mine)
    near_first = links.swap_level(near, 1)
    far_first = links.swap_level(far, 2)
    far_second = links.swap_level(far_first, 1)
    own_weights = gather_groups(links, level_weights)
    picked = gate(picked, level_block)
    rank = jnp.sum((jnp.cumsum(picked, axis=0) - picked) * picked, axis=1)
    place = chosen * most + rank
    slot_index = jnp.arange(experts * most, dtype=jnp.int32)
    to_slots = (slot_index[:, None] == place[None, :]).astype(BF)
    to_tokens = (place[:, None] == slot_index[None, :]).astype(BF)
    cot_slots = dot(to_slots, cotangent).astype(BF).reshape(experts, most, width)

    own_weights = tie(*own_weights, near_first, far_first, cot_slots)[:-3]
    other_weights = [links.swap_core(part) for part in own_weights]

    source = jnp.concatenate([near, near_first, far_first, far_second], axis=0).astype(F32)
    normed_work = (
        source * lax.rsqrt(jnp.mean(source * source, axis=-1, keepdims=True) + EPSILON)
    ).astype(BF)
    if level_rows % 16 == 0:
        queries, pair, weights = project(flags, normed_work, own_weights, other_weights)
    else:
        weights = in_order(links, own_weights, other_weights)
        projected = dot(normed_work, weights).astype(BF)
        queries, pair = projected[:, :half_width], projected[:, half_width:]
    pair_far = links.swap_core(pair)
    cot_arrived = all_to_all(gate(cot_slots, far_second, *other_weights)).reshape(-1, width)
    *mixed_parts, probs = attention_forward(queries, pair, pair_far)
    mixed_parts = tie(*mixed_parts, cot_arrived)[:-1]

    back = tie(*[links.swap_level(mixed_parts[b], b) for b in (1, 2, 3)])
    level_extra = gate(level_block[:, 3 * half_width :], queries)
    own_extra = gather_groups(links, level_extra)
    other_extra = [links.swap_core(gate(part, *back)) for part in own_extra]
    full_extra = in_order(links, own_extra, other_extra)
    full_router = full_extra[:, width : width + experts]
    gain_two = full_extra[:, width + 2 * experts].astype(F32)[None]
    tallies = full_extra[::own_rows, width + experts : width + 2 * experts].astype(F32)
    mine_only = (jnp.arange(experts, dtype=jnp.int32) == device).astype(F32)[None, :]
    counts = jnp.sum(tallies * mine_only, axis=1).astype(jnp.int32)
    offsets = jnp.cumsum(counts) - counts
    within = jnp.arange(most, dtype=jnp.int32)[None, :]
    slot_grid = offsets[:, None] + within
    usable = (within < counts[:, None]) & (slot_grid < capacity)
    slot_flat = jnp.where(usable, slot_grid, -1).reshape(-1)
    held_index = jnp.arange(capacity, dtype=jnp.int32)
    compact = (held_index[:, None] == slot_flat[None, :]).astype(BF)
    expand = (slot_flat[:, None] == held_index[None, :]).astype(BF)

    mixed_mine, mixed_sent = mixed_route(flags, [mixed_parts[0], *back])
    mixed_low, middle, second_slots = owner_forward(
        flags, mixed_mine, links.swap_core(mixed_sent), inputs, full_extra, gain_two, to_slots
    )
    arrived = all_to_all(second_slots.reshape(experts, most, width)).reshape(-1, width)

    held, grad_result, hidden, grad_inner, grad_back, taken_back, grad_logits = expert_layer(
        flags, arrived, cot_arrived, compact, expand, full_router, expert_in, expert_out
    )
    grad_returned = all_to_all(grad_back.reshape(experts, most, width)).reshape(-1, width)
    grad_router = dot_tn(held, grad_logits)
    grad_weight_out = dot_tn(hidden, grad_result)
    grad_weight_in = dot_tn(held, grad_inner)
    grad_returned = gate(grad_returned, grad_weight_in, grad_weight_out, grad_router)

    grad_middle, grad_branch, grad_mine, grad_sent, gain_rows = owner_backward(
        flags, grad_returned, to_tokens, cotangent, middle, gain_two, full_extra
    )
    routed = grad_route(flags, grad_mine, links.swap_core(grad_sent))
    got = tie(*[links.swap_level(routed[b], b) for b in (1, 2, 3)])

    keep, send = output_grads(flags, gate(mixed_low, routed[0]), grad_branch, grad_router, gain_rows, level_rows)
    summed = reduce_cores(links, keep, send)
    summed = reduce_groups(
        links, [summed[m * level_rows : (m + 1) * level_rows] for m in range(links.groups // 2)]
    )
    got = tie(*got, summed)[:-1]
    taken_back = gate(taken_back, *got).reshape(experts, most, width)
    taken_arrived = all_to_all(taken_back).reshape(-1, width)
    grad_queries, grad_near, grad_far = attention_backward(
        queries, pair, pair_far, probs, [routed[0], *got], mixed_parts
    )
    got_pair = links.swap_core(grad_far)
    grad_projected, keep, send = weight_grads(
        flags, normed_work, grad_queries, grad_near, got_pair, level_rows
    )
    grad_first_work = dot_nt(grad_projected, weights).astype(BF)
    core_sum = reduce_cores(links, keep, gate(send, taken_arrived))
    core_sum = gate(core_sum, grad_first_work)
    group_sum = reduce_groups(
        links, [core_sum[m * level_rows : (m + 1) * level_rows] for m in range(links.groups // 2)]
    )
    parts = gate(grad_first_work, core_sum).reshape(blocks, half_rows, width)
    back = tie(*[links.swap_level(parts[b], b) for b in (1, 2, 3)])
    near = (parts[0].astype(F32) + back[0].astype(F32)).astype(BF)
    far = (back[1].astype(F32) + back[2].astype(F32)).astype(BF)
    grad_first = workers_to_owner(links, near, far).astype(F32)
    source_own = inputs.astype(F32)
    inverse_one = lax.rsqrt(jnp.mean(source_own * source_own, axis=-1, keepdims=True) + EPSILON)
    normed_one = source_own * inverse_one
    grad_input = grad_middle + inverse_one * (
        grad_first - normed_one * jnp.mean(grad_first * normed_one, axis=-1, keepdims=True)
    )
    output = (middle + dot(to_tokens, taken_arrived)).astype(BF)

    columns = group_sum.shape[1]
    sums = jnp.concatenate([group_sum, summed], axis=1)
    sums = reduce_levels(links, gate(sums, *back))
    zero, one, two, three = [part[:, :columns] for part in sums]
    summed = sum(part[:, columns:] for part in sums)
    kept, cross = zero + two, one + three
    low, high = pick(level & 1, kept, cross), pick(level & 1, cross, kept)
    grad_weights = [
        jnp.concatenate(
            [part[:, i * half_width : (i + 1) * half_width] for part in (low, high)], axis=1
        )
        for i in range(3)
    ]
    grad_norm_one = sum(
        jnp.sum(w.astype(F32) * g, axis=1)
        for w, g in zip((w_query, w_key, w_value), grad_weights)
    )
    grad_weights = [g * scale for g in grad_weights]

    grad_w_output = summed[:, :width]
    grad_w_router = summed[:, width : width + experts]
    grad_norm_two = summed[:, width + experts]
    return (
        output,
        grad_input,
        grad_norm_one,
        grad_weights[0],
        grad_weights[1],
        grad_weights[2],
        grad_w_output,
        grad_norm_two,
        grad_w_router,
        grad_weight_in[None],
        grad_weight_out[None],
    )


def solution(mesh):
    return jax.shard_map(
        on_device,
        mesh=mesh,
        in_specs=(
            P(AXES, None),
            P(AXES),
            P(AXES, None),
            P(AXES, None),
            P(AXES, None),
            P(AXES, None),
            P(AXES),
            P(AXES, None),
            P(AXES, None, None),
            P(AXES, None, None),
            P(AXES, None),
            P(AXES, None),
        ),
        out_specs=(
            P(AXES, None),
            P(AXES, None),
            P(AXES),
            P(AXES, None),
            P(AXES, None),
            P(AXES, None),
            P(AXES, None),
            P(AXES),
            P(AXES, None),
            P(AXES, None, None),
            P(AXES, None, None),
        ),
        check_vma=False,
    )
```

```python
import functools

import jax
import jax.numpy as jnp
from jax import lax
from jax.experimental import pallas as pl
from jax.experimental.pallas import tpu as pltpu
from jax.sharding import PartitionSpec as P

HEAD_DIM = 64
AXES = ("group", "local")
BF = jnp.bfloat16
F32 = jnp.float32
EPSILON = 1e-06
VMEM_BYTES = 58 * 2**20
SMALL_BYTES = 24 * 2**20


def dot(left, right):
    return jnp.dot(left, right, preferred_element_type=F32)


def dot_tn(left, right):
    return lax.dot_general(left, right, (((0,), (0,)), ((), ())), preferred_element_type=F32)


def dot_nt(left, right):
    return lax.dot_general(left, right, (((1,), (1,)), ((), ())), preferred_element_type=F32)


class Links:
    def __init__(self):
        self.groups = lax.axis_size("group")
        self.levels = lax.axis_size("local")
        self.group = lax.axis_index("group")
        self.level = lax.axis_index("local")
        self.core = self.group % 2

    def permute(self, array, target):
        pairs = []
        for group in range(self.groups):
            for level in range(self.levels):
                other_group, other_level = target(group, level)
                pairs.append((group * self.levels + level, other_group * self.levels + other_level))
        return lax.ppermute(array, AXES, pairs)

    def swap_core(self, array):
        return self.permute(array, lambda g, l: (g ^ 1, l))

    def swap_level(self, array, mask):
        return self.permute(array, lambda g, l: (g, l ^ mask))

    def swap_group(self, array, mask):
        return self.permute(array, lambda g, l: (g ^ (2 * mask), l))


def gate(array, *after):
    return lax.optimization_barrier((array, *after))[0]


def tie(*arrays):
    return lax.optimization_barrier(arrays)


def pick(flag, first, second):
    return jnp.where(flag == 0, first, second)


def joined(flag, mine, other, axis=0):
    return jnp.concatenate([pick(flag, mine, other), pick(flag, other, mine)], axis=axis)


def ordered(index, parts):
    count = len(parts)
    if count == 1:
        return parts[0]
    top = count.bit_length() - 2
    half = count // 2
    low = index & (half - 1)
    return joined((index >> top) & 1, ordered(low, parts[:half]), ordered(low, parts[half:]))


def rows_of(array, index, rows):
    return lax.dynamic_slice_in_dim(array, index * rows, rows, axis=0)


def gather_levels(links, pieces):
    got = tie(*[links.swap_level(pieces[b], b) for b in range(1, links.levels)])
    return ordered(links.level, [pieces[0], *got])


def gather_groups(links, block):
    return [block] + [links.swap_group(block, m) for m in range(1, links.groups // 2)]


def in_order(links, own, other):
    pairs = [joined(links.core, mine, far) for mine, far in zip(own, other)]
    return ordered(links.group >> 1, pairs)


def reduce_cores(links, keep, send):
    return keep + links.swap_core(send).astype(F32)


def reduce_groups(links, parts):
    got = [links.swap_group(parts[m].astype(BF), m) for m in range(1, len(parts))]
    total = parts[0]
    for part in tie(*got):
        total = total + part.astype(F32)
    return total


def reduce_levels(links, block):
    rows = block.shape[0] // links.levels
    parts = [rows_of(block, links.level ^ b, rows) for b in range(links.levels)]
    got = tie(*[links.swap_level(parts[b].astype(BF), b) for b in range(1, links.levels)])
    return [parts[0], *got]


def owner_to_workers(links, array):
    half = array.shape[0] // 2
    mine = pick(links.core, array[:half], array[half:])
    other = links.swap_core(pick(links.core, array[half:], array[:half]))
    same = (links.level >> 1) ^ links.core
    return pick(same, mine, other), pick(same, other, mine)


def workers_to_owner(links, near, far):
    same = (links.level >> 1) ^ links.core
    mine = pick(same, near, far)
    other = links.swap_core(pick(same, far, near))
    return joined(links.core, mine, other)


PAIR = 2 * HEAD_DIM


def head_masks(dtype):
    lanes = lax.broadcasted_iota(jnp.int32, (1, PAIR), 1)
    return [(lanes // HEAD_DIM == head).astype(dtype) for head in range(2)]


CHUNK = 128


def forward_kernel(query_ref, key_ref, value_ref, key_far_ref, value_far_ref, *refs):
    mixed_refs, weights_ref, inverse_ref = refs[:-2], refs[-2], refs[-1]
    query = query_ref[...] * BF(HEAD_DIM**-0.5)
    key = jnp.concatenate([key_ref[...], key_far_ref[...]], axis=0)
    value = jnp.concatenate([value_ref[...], value_far_ref[...]], axis=0)
    value = jnp.concatenate([value, jnp.ones_like(value)], axis=1)
    first_head = lax.broadcasted_iota(jnp.int32, (1, PAIR), 1) < HEAD_DIM
    for part, mixed_ref in enumerate(mixed_refs):
        rows = slice(part * CHUNK, (part + 1) * CHUNK)
        sums = []
        for head, mask in enumerate(head_masks(BF)):
            scores = dot_nt(query[rows] * mask, key)
            weights = jnp.exp(scores - jnp.max(scores, axis=1, keepdims=True)).astype(BF)
            weights_ref[head, rows] = weights
            sums.append(dot(weights, value))
        mixed = jnp.where(first_head, sums[0][:, :PAIR], sums[1][:, :PAIR])
        inverse = 1.0 / jnp.where(first_head, sums[0][:, PAIR:], sums[1][:, PAIR:])
        inverse_ref[rows] = inverse
        mixed_ref[...] = (mixed * inverse).astype(BF)


def pair_column(rows, block=0):
    return pl.BlockSpec((rows, PAIR), lambda i: (0, block + i))


def weights_block(rows):
    return pl.BlockSpec((2, rows, 2 * rows), lambda i: (i, 0, 0))


def attention_forward(queries, pair, pair_far):
    rows, half_width = queries.shape
    pairs = half_width // PAIR
    return pl.pallas_call(
        forward_kernel,
        grid=(pairs,),
        in_specs=[pair_column(rows)] + [pair_column(rows), pair_column(rows, pairs)] * 2,
        out_specs=[pair_column(CHUNK)] * (rows // CHUNK) + [weights_block(rows), pair_column(rows)],
        out_shape=[low_shape(CHUNK, half_width)] * (rows // CHUNK)
        + [low_shape(2 * pairs, rows, 2 * rows), wide_shape(rows, half_width)],
        compiler_params=params(),
        cost_estimate=cost(2 * 10**9, 4096),
    )(queries, pair, pair, pair_far, pair_far)


def backward_kernel(
    query_ref, key_ref, value_ref, key_far_ref, value_far_ref, weights_ref, inverse_ref, *refs
):
    grad_refs, mixed_refs = refs[:4], refs[4:8]
    grad_query_ref, grad_near_ref, grad_far_ref = refs[8:]
    all_rows = query_ref.shape[0]
    factor = BF(HEAD_DIM**-0.5)
    query = query_ref[...] * factor
    key = jnp.concatenate([key_ref[...], key_far_ref[...]], axis=0)
    value = jnp.concatenate([value_ref[...], value_far_ref[...]], axis=0)
    grad = jnp.concatenate([ref[...] for ref in grad_refs], axis=0).astype(F32)
    grad = grad * inverse_ref[...]
    mixed = jnp.concatenate([ref[...] for ref in mixed_refs], axis=0)
    together = grad * mixed.astype(F32)
    grad = grad.astype(BF)
    grad_key = jnp.zeros((PAIR, 2 * all_rows), F32)
    grad_value = jnp.zeros((PAIR, 2 * all_rows), F32)
    for part in range(all_rows // (2 * CHUNK)):
        rows = slice(part * 2 * CHUNK, (part + 1) * 2 * CHUNK)
        grad_query = jnp.zeros((2 * CHUNK, PAIR), F32)
        for head, (mask, mask_wide) in enumerate(zip(head_masks(BF), head_masks(F32))):
            weights = weights_ref[head, rows]
            grad_one = grad[rows] * mask
            row_dots = jnp.sum(together[rows] * mask_wide, axis=1, keepdims=True)
            grad_weights = dot_nt(grad_one, value)
            grad_scores = (weights.astype(F32) * (grad_weights - row_dots)).astype(BF)
            grad_value = grad_value + dot_tn(grad_one, weights)
            grad_key = grad_key + dot_tn(query[rows] * mask, grad_scores)
            grad_query = grad_query + dot(grad_scores, key * (mask * factor))
        grad_query_ref[rows] = grad_query.astype(BF)
    for index, total in enumerate((grad_key, grad_value)):
        total = total.T
        grad_near_ref[index] = total[:all_rows].astype(BF)
        grad_far_ref[index] = total[all_rows:].astype(BF)


def attention_backward(queries, pair, pair_far, weights, inverse, grads, mixed):
    rows, half_width = queries.shape
    pairs = half_width // PAIR
    return pl.pallas_call(
        backward_kernel,
        grid=(pairs,),
        in_specs=[pair_column(rows)]
        + [pair_column(rows), pair_column(rows, pairs)] * 2
        + [weights_block(rows), pair_column(rows)]
        + [pair_column(rows // 4)] * 8,
        out_specs=[pair_column(rows)] + [pl.BlockSpec((2, rows, PAIR), lambda i: (0, 0, i))] * 2,
        out_shape=[low_shape(rows, half_width)] + [low_shape(2, rows, half_width)] * 2,
        compiler_params=params(),
        cost_estimate=cost(2 * 10**10, 4096),
    )(queries, pair, pair, pair_far, pair_far, weights, inverse, *grads, *mixed)


GELU_SCALE = 0.7978845608028654
GELU_CUBE = 0.044715


def gelu_and_slope(values):
    square = values * values
    bend = jnp.tanh(GELU_SCALE * values * (1.0 + GELU_CUBE * square))
    half = 0.5 + 0.5 * bend
    slope = half + 0.5 * values * (1.0 - bend * bend) * GELU_SCALE * (1.0 + 3 * GELU_CUBE * square)
    return values * half, slope


def whole(shape):
    return pl.BlockSpec(shape, lambda *_: (0,) * len(shape))


FLAGS = pl.BlockSpec(memory_space=pltpu.SMEM)
CORE, HALF, SAME, DEVICE, PLACE = range(5)


def params(size=VMEM_BYTES):
    return pltpu.CompilerParams(vmem_limit_bytes=size)


def cost(flops, size):
    return pl.CostEstimate(flops=flops, bytes_accessed=size, transcendentals=0)


def one_step(kernel, flags, operands, shapes, scratch=(), size=VMEM_BYTES):
    return pl.pallas_call(
        kernel,
        grid=(1,),
        in_specs=[FLAGS] + [whole(operand.shape) for operand in operands],
        out_specs=[whole(shape.shape) for shape in shapes],
        out_shape=shapes,
        scratch_shapes=list(scratch),
        compiler_params=params(size),
        cost_estimate=cost(0, 2**20),
    )(flags, *operands)


def low_shape(*shape):
    return jax.ShapeDtypeStruct(shape, BF)


def wide_shape(*shape):
    return jax.ShapeDtypeStruct(shape, F32)


def each_case(flags_ref, body):
    for half in range(2):
        for same in range(2):

            @pl.when((flags_ref[HALF] == half) & (flags_ref[SAME] == same))
            def _(half=half, same=same):
                body(half, same)


def turned_column(row):
    count = row.shape[1]
    rows = lax.broadcasted_iota(jnp.int32, (count, count), 0)
    lanes = lax.broadcasted_iota(jnp.int32, (count, count), 1)
    return jnp.sum(jnp.where(rows == lanes, row, 0.0), axis=1, keepdims=True)


def turned_row(column):
    count = column.shape[0]
    rows = lax.broadcasted_iota(jnp.int32, (count, count), 0)
    lanes = lax.broadcasted_iota(jnp.int32, (count, count), 1)
    return jnp.sum(jnp.where(rows == lanes, column, 0.0), axis=0, keepdims=True)


def pack_kernel(
    flags_ref,
    query_ref,
    key_ref,
    value_ref,
    output_ref,
    router_ref,
    routes_ref,
    norm_one_ref,
    norm_two_ref,
    kept_ref,
    cross_ref,
):
    own_rows, width = query_ref.shape
    experts = router_ref.shape[1]
    half_width = width // 2
    start = 3 * half_width
    tail = kept_ref.shape[1] - start - width
    scale = turned_column(norm_one_ref[...].astype(F32))
    first_half = flags_ref[HALF] == 0
    for index, ref in enumerate((query_ref, key_ref, value_ref)):
        scaled = (ref[...].astype(F32) * scale).astype(BF)
        low, high = scaled[:, :half_width], scaled[:, half_width:]
        columns = slice(index * half_width, (index + 1) * half_width)
        kept_ref[:, columns] = jnp.where(first_half, low, high)
        cross_ref[:, columns] = jnp.where(first_half, high, low)
    lanes = lax.broadcasted_iota(jnp.int32, (1, tail), 1)
    index = lax.broadcasted_iota(jnp.int32, (tail, 1), 0) - experts
    tally = jnp.sum((routes_ref[...] == index).astype(F32), axis=1, keepdims=True)
    tally = turned_row(tally)
    router = router_ref[...].astype(F32)
    router = jnp.concatenate([router, jnp.zeros((own_rows, tail - experts), F32)], axis=1)
    gain = turned_column(norm_two_ref[...].astype(F32))
    small = jnp.where(lanes < experts, router, jnp.where(lanes == 2 * experts, gain, tally))
    for ref in (kept_ref, cross_ref):
        ref[:, start : start + width] = output_ref[...]
        ref[:, start + width :] = small.astype(BF)


def pack(flags, operands):
    own_rows, width = operands[0].shape
    experts = operands[4].shape[1]
    tail = 2 * experts + 1
    columns = 3 * width // 2 + width + tail + -tail % 128
    return one_step(pack_kernel, flags, operands, [low_shape(own_rows, columns)] * 2)


def finish_kernel(
    flags_ref,
    zero_ref,
    one_ref,
    two_ref,
    three_ref,
    query_ref,
    key_ref,
    value_ref,
    norm_one_ref,
    grad_query_ref,
    grad_key_ref,
    grad_value_ref,
    grad_output_ref,
    grad_router_ref,
    grad_one_ref,
    grad_two_ref,
):
    width = query_ref.shape[1]
    experts = grad_router_ref.shape[1]
    half_width = width // 2
    start = 3 * half_width
    near = zero_ref[...] + two_ref[...].astype(F32)
    far = one_ref[...].astype(F32) + three_ref[...].astype(F32)
    scale = turned_column(norm_one_ref[...].astype(F32))
    first_half = flags_ref[HALF] == 0
    total = jnp.zeros_like(scale)
    pairs = ((query_ref, grad_query_ref), (key_ref, grad_key_ref), (value_ref, grad_value_ref))
    for index, (ref, grad_ref) in enumerate(pairs):
        columns = slice(index * half_width, (index + 1) * half_width)
        low = jnp.where(first_half, near[:, columns], far[:, columns])
        high = jnp.where(first_half, far[:, columns], near[:, columns])
        weight = ref[...].astype(F32)
        total = total + jnp.sum(weight[:, :half_width] * low, axis=1, keepdims=True)
        total = total + jnp.sum(weight[:, half_width:] * high, axis=1, keepdims=True)
        grad_ref[:, :half_width] = low * scale
        grad_ref[:, half_width:] = high * scale
    grad_one_ref[...] = turned_row(total)
    both = near[:, start:] + far[:, start:]
    grad_output_ref[...] = both[:, :width]
    small = both[:, width:]
    grad_router_ref[...] = small[:, :experts]
    lanes = lax.broadcasted_iota(jnp.int32, (1, small.shape[1]), 1)
    gain = jnp.sum(jnp.where(lanes == experts, small, 0.0), axis=1, keepdims=True)
    grad_two_ref[...] = turned_row(gain)


def finish(flags, operands, experts):
    own_rows, width = operands[4].shape
    shapes = [wide_shape(own_rows, width)] * 4
    shapes += [wide_shape(own_rows, experts)] + [wide_shape(1, own_rows)] * 2
    return one_step(finish_kernel, flags, operands, shapes, size=SMALL_BYTES)


def project_kernel(count, flags_ref, normed_ref, *refs):
    own_refs, other_refs = refs[:count], refs[count : 2 * count]
    query_ref, pair_ref, weight_ref, extra_ref = refs[2 * count :]
    columns = weight_ref.shape[1]
    rows = own_refs[0].shape[0]
    core = flags_ref[CORE]
    for m in range(count):
        place = 2 * (flags_ref[PLACE] ^ m)
        for index, ref in ((place + core, own_refs[m]), (place + 1 - core, other_refs[m])):
            place_rows = pl.ds(pl.multiple_of(index * rows, 16), rows)
            weight_ref[place_rows, :] = ref[:, :columns]
            extra_ref[place_rows, :] = ref[:, columns:]
    projected = dot(normed_ref[...], weight_ref[...]).astype(BF)
    query_ref[...] = projected[:, : query_ref.shape[1]]
    pair_ref[...] = projected[:, query_ref.shape[1] :]


def project(flags, normed, own, other):
    count = len(own)
    rows, width = normed.shape
    columns = 3 * width // 2
    shapes = [
        low_shape(rows, width // 2),
        low_shape(rows, width),
        low_shape(width, columns),
        low_shape(width, own[0].shape[1] - columns),
    ]
    kernel = functools.partial(project_kernel, count)
    return one_step(kernel, flags, [normed, *own, *other], shapes)


def mixed_route_kernel(flags_ref, zero_ref, one_ref, two_ref, three_ref, mine_ref, sent_ref):
    half_width = zero_ref.shape[1]

    def body(half, same):
        near_ref, far_ref = (mine_ref, sent_ref) if same == 0 else (sent_ref, mine_ref)
        for into_ref, refs in ((near_ref, (zero_ref, one_ref)), (far_ref, (two_ref, three_ref))):
            into_ref[:, :half_width] = refs[half][...]
            into_ref[:, half_width:] = refs[1 - half][...]

    each_case(flags_ref, body)


def mixed_route(flags, parts):
    rows, half_width = parts[0].shape
    shapes = [low_shape(rows, 2 * half_width)] * 2
    return one_step(mixed_route_kernel, flags, parts, shapes, size=SMALL_BYTES)


def grad_route_kernel(flags_ref, mine_ref, got_ref, zero_ref, one_ref, two_ref, three_ref):
    half_width = zero_ref.shape[1]

    def body(half, same):
        near_ref, far_ref = (mine_ref, got_ref) if same == 0 else (got_ref, mine_ref)
        for from_ref, refs in ((near_ref, (zero_ref, one_ref)), (far_ref, (two_ref, three_ref))):
            refs[half][...] = from_ref[:, :half_width]
            refs[1 - half][...] = from_ref[:, half_width:]

    each_case(flags_ref, body)


def grad_route(flags, mine, got):
    rows, width = mine.shape
    shapes = [low_shape(rows, width // 2)] * 4
    return one_step(grad_route_kernel, flags, [mine, got], shapes, size=SMALL_BYTES)


def owner_forward_kernel(
    flags_ref,
    mine_ref,
    got_ref,
    inputs_ref,
    weight_ref,
    gain_ref,
    to_slots_ref,
    mixed_ref,
    middle_ref,
    slots_ref,
):
    half_rows = mine_ref.shape[0]
    for core in range(2):

        @pl.when(flags_ref[CORE] == core)
        def _(core=core):
            refs = (mine_ref, got_ref)
            mixed_ref[:half_rows] = refs[core][...]
            mixed_ref[half_rows:] = refs[1 - core][...]

    weight = weight_ref[:, : mixed_ref.shape[1]]
    middle = inputs_ref[...].astype(F32) + dot(mixed_ref[...], weight)
    middle_ref[...] = middle
    inverse = lax.rsqrt(jnp.mean(middle * middle, axis=1, keepdims=True) + EPSILON)
    second_low = (middle * inverse * gain_ref[...]).astype(BF)
    slots_ref[...] = dot(to_slots_ref[...], second_low).astype(BF)


def owner_forward(flags, mine, got, inputs, full_extra, gain, to_slots):
    rows, width = inputs.shape
    shapes = [
        low_shape(rows, width),
        wide_shape(rows, width),
        low_shape(to_slots.shape[0], width),
    ]
    operands = [mine, got, inputs, full_extra, gain, to_slots]
    return one_step(owner_forward_kernel, flags, operands, shapes)


TILE = 1024


def cotangent_kernel(cot_ref, compact_ref, weight_out_ref, held_ref, back_ref):
    @pl.when(pl.program_id(0) == 0)
    def _():
        held_ref[...] = dot(compact_ref[...], cot_ref[...]).astype(BF)

    back_ref[...] = dot_nt(held_ref[...], weight_out_ref[0]).astype(BF)


def cotangent_layer(cot, compact, expert_out):
    slots, width = cot.shape
    capacity = compact.shape[0]
    hidden_width = expert_out.shape[1]
    return pl.pallas_call(
        cotangent_kernel,
        grid=(hidden_width // TILE,),
        in_specs=[
            whole((slots, width)),
            whole((capacity, slots)),
            pl.BlockSpec((1, TILE, width), lambda i: (0, i, 0)),
        ],
        out_specs=[whole((capacity, width)), pl.BlockSpec((capacity, TILE), lambda i: (0, i))],
        out_shape=[low_shape(capacity, width), low_shape(capacity, hidden_width)],
        compiler_params=params(),
        cost_estimate=cost(2 * capacity * width * hidden_width, 4 * width * hidden_width),
    )(cot, compact, expert_out)


def expert_kernel(
    flags_ref,
    arrived_ref,
    cot_ref,
    back_ref,
    compact_ref,
    expand_ref,
    router_ref,
    weight_in_ref,
    weight_out_ref,
    held_ref,
    grad_result_ref,
    hidden_ref,
    grad_inner_ref,
    grad_back_ref,
    taken_ref,
    grad_logits_ref,
    result_sum,
    grad_sum,
    probs,
    gates,
):
    step = pl.program_id(0)
    experts = router_ref.shape[1]
    lanes = lax.broadcasted_iota(jnp.int32, (1, experts), 1)
    mine = (lanes == flags_ref[DEVICE]).astype(F32)

    @pl.when(step == 0)
    def _():
        held = dot(compact_ref[...], arrived_ref[...]).astype(BF)
        held_ref[...] = held
        logits = dot(held, router_ref[...])
        weights = jnp.exp(logits - jnp.max(logits, axis=1, keepdims=True))
        router_probs = weights / jnp.sum(weights, axis=1, keepdims=True)
        probs[...] = router_probs
        gate = jnp.sum(router_probs * mine, axis=1, keepdims=True)
        gates[...] = gate
        grad_result_ref[...] = (gate * cot_ref[...].astype(F32)).astype(BF)
        result_sum[...] = jnp.zeros_like(result_sum)
        grad_sum[...] = jnp.zeros_like(grad_sum)

    weight_in = weight_in_ref[0]
    hidden, slope = gelu_and_slope(dot(held_ref[...], weight_in))
    hidden = hidden.astype(BF)
    hidden_ref[...] = hidden
    grad_inner = (back_ref[...].astype(F32) * (gates[...] * slope)).astype(BF)
    grad_inner_ref[...] = grad_inner
    result_sum[...] += dot(hidden, weight_out_ref[0])
    grad_sum[...] += dot_nt(grad_inner, weight_in)

    @pl.when(step == pl.num_programs(0) - 1)
    def _():
        result = result_sum[...].astype(BF).astype(F32)
        gate = gates[...]
        grad_gate = jnp.sum(cot_ref[...].astype(F32) * result, axis=1, keepdims=True)
        grad_logits = (grad_gate * probs[...] * (mine - gate)).astype(BF)
        grad_logits_ref[...] = grad_logits
        grad_held = grad_sum[...] + dot_nt(grad_logits, router_ref[...])
        grad_back_ref[...] = dot(expand_ref[...], grad_held.astype(BF)).astype(BF)
        taken_ref[...] = (gate * result).astype(BF)


def expert_layer(flags, arrived, cot, back, compact, expand, router, expert_in, expert_out):
    slots, width = arrived.shape
    capacity = compact.shape[0]
    hidden_width = expert_in.shape[2]
    experts = router.shape[1]
    wide = whole((capacity, width))
    tall = pl.BlockSpec((capacity, TILE), lambda i: (0, i))
    return pl.pallas_call(
        expert_kernel,
        grid=(hidden_width // TILE,),
        in_specs=[
            FLAGS,
            whole((slots, width)),
            wide,
            tall,
            whole((capacity, slots)),
            whole((slots, capacity)),
            whole((width, experts)),
            pl.BlockSpec((1, width, TILE), lambda i: (0, 0, i)),
            pl.BlockSpec((1, TILE, width), lambda i: (0, i, 0)),
        ],
        out_specs=[wide, wide, tall, tall, whole((slots, width)), wide]
        + [whole((capacity, experts))],
        out_shape=[
            low_shape(capacity, width),
            low_shape(capacity, width),
            low_shape(capacity, hidden_width),
            low_shape(capacity, hidden_width),
            low_shape(slots, width),
            low_shape(capacity, width),
            low_shape(capacity, experts),
        ],
        scratch_shapes=[
            pltpu.VMEM((capacity, width), F32),
            pltpu.VMEM((capacity, width), F32),
            pltpu.VMEM((capacity, experts), F32),
            pltpu.VMEM((capacity, 1), F32),
        ],
        compiler_params=params(),
        cost_estimate=cost(8 * capacity * width * hidden_width, 8 * width * hidden_width),
    )(flags, arrived, cot, back, compact, expand, router, expert_in, expert_out)


def owner_backward_kernel(
    flags_ref,
    returned_ref,
    to_tokens_ref,
    cotangent_ref,
    middle_ref,
    gain_ref,
    weight_ref,
    grad_middle_ref,
    grad_branch_ref,
    mine_ref,
    sent_ref,
    grad_gain_ref,
):
    half_rows = mine_ref.shape[0]
    middle = middle_ref[...]
    inverse = lax.rsqrt(jnp.mean(middle * middle, axis=1, keepdims=True) + EPSILON)
    normed = middle * inverse
    grad_second = dot(to_tokens_ref[...], returned_ref[...])
    grouped = (grad_second * normed).reshape(-1, GAIN_ROWS, grad_second.shape[1])
    grad_gain_ref[...] = jnp.sum(grouped, axis=0).astype(BF)
    scaled = grad_second * gain_ref[...]
    grad_middle = cotangent_ref[...].astype(F32) + inverse * (
        scaled - normed * jnp.mean(scaled * normed, axis=1, keepdims=True)
    )
    grad_middle_ref[...] = grad_middle
    grad_branch = grad_middle.astype(BF)
    grad_branch_ref[...] = grad_branch
    weight = weight_ref[:, : middle.shape[1]]
    grad_mixed = dot_nt(grad_branch, weight).astype(BF)
    for core in range(2):

        @pl.when(flags_ref[CORE] == core)
        def _(core=core):
            mine_ref[...] = grad_mixed[core * half_rows : (core + 1) * half_rows]
            sent_ref[...] = grad_mixed[(1 - core) * half_rows : (2 - core) * half_rows]


def owner_backward(flags, returned, to_tokens, cotangent, middle, gain, full_extra):
    rows, width = cotangent.shape
    shapes = [
        wide_shape(rows, width),
        low_shape(rows, width),
        low_shape(rows // 2, width),
        low_shape(rows // 2, width),
        low_shape(GAIN_ROWS, width),
    ]
    operands = [returned, to_tokens, cotangent, middle, gain, full_extra]
    return one_step(owner_backward_kernel, flags, operands, shapes)


GAIN_ROWS = 16


def deal_rows(flags_ref, total, keep_ref, send_ref, rows):
    core = flags_ref[CORE]
    for m in range(total.shape[0] // (2 * rows)):
        place = 2 * (flags_ref[PLACE] ^ m)
        keep_ref[m * rows : (m + 1) * rows, :] = total[
            pl.ds(pl.multiple_of((place + core) * rows, 8), rows), :
        ]
        send_ref[m * rows : (m + 1) * rows, :] = total[
            pl.ds(pl.multiple_of((place + 1 - core) * rows, 8), rows), :
        ].astype(BF)


def dealt(width, columns):
    return [wide_shape(width // 2, columns), low_shape(width // 2, columns)]


def weight_grads_kernel(
    rows,
    flags_ref,
    normed_ref,
    query_ref,
    near_ref,
    got_ref,
    mixed_ref,
    branch_ref,
    router_ref,
    gain_ref,
    projected_ref,
    keep_ref,
    send_ref,
    total,
):
    part = query_ref.shape[1]
    width, experts = router_ref.shape
    extra = total.shape[1] - 3 * part - width
    projected_ref[:, :part] = query_ref[...]
    for index in range(2):
        both = near_ref[index].astype(F32) + got_ref[index].astype(F32)
        projected_ref[:, (index + 1) * part : (index + 2) * part] = both.astype(BF)
    total[:, : 3 * part] = dot_tn(normed_ref[...], projected_ref[...])
    total[:, 3 * part : 3 * part + width] = dot_tn(mixed_ref[...], branch_ref[...])
    gain = dot_tn(gain_ref[...], jnp.ones((GAIN_ROWS, extra), BF))
    router = router_ref[...]
    router = jnp.concatenate([router, jnp.zeros((width, extra - experts), F32)], axis=1)
    lanes = lax.broadcasted_iota(jnp.int32, (1, extra), 1)
    total[:, 3 * part + width :] = jnp.where(lanes == experts, gain, router)
    deal_rows(flags_ref, total, keep_ref, send_ref, rows)


def weight_grads(flags, operands, rows):
    work_rows, width = operands[0].shape
    part = operands[1].shape[1]
    experts = operands[6].shape[1]
    columns = 3 * part + width + experts + 1
    columns += -columns % 128
    return one_step(
        functools.partial(weight_grads_kernel, rows),
        flags,
        operands,
        [low_shape(work_rows, 3 * part)] + dealt(width, columns),
        [pltpu.VMEM((width, columns), F32)],
        2 * SMALL_BYTES,
    )


def all_to_all(array):
    return lax.all_to_all(array, AXES, split_axis=0, concat_axis=0, tiled=True)


def on_device(
    inputs,
    norm_one,
    w_query,
    w_key,
    w_value,
    w_output,
    norm_two,
    w_router,
    expert_in,
    expert_out,
    routes,
    cotangent,
):
    links = Links()
    level, core = links.level, links.core
    device = links.group * links.levels + level
    devices = links.groups * links.levels
    rows, width = inputs.shape
    half_rows = rows // 2
    half_width = width // 2
    experts = w_router.shape[1]
    own_rows = norm_one.shape[0]
    most = 2 * rows // experts
    capacity = 5 * rows // 4
    blocks = links.levels

    same = (level >> 1) ^ core
    flags = jnp.stack([core, level & 1, same, device, links.group >> 1]).astype(jnp.int32)

    mine = pick(core, inputs[:half_rows], inputs[half_rows:])
    got = links.swap_core(pick(core, inputs[half_rows:], inputs[:half_rows]))
    kept, cross = pack(
        flags,
        [w_query, w_key, w_value, w_output, w_router, routes.reshape(1, rows)]
        + [norm_one.reshape(1, own_rows), norm_two.reshape(1, own_rows)],
    )
    level_block = gather_levels(links, [kept, cross, kept, cross])
    level_rows = level_block.shape[0]
    got = gate(got, kept, cross)
    near, far = pick(same, mine, got), pick(same, got, mine)
    near_first = links.swap_level(near, 1)
    far_first = links.swap_level(far, 2)
    far_second = links.swap_level(far_first, 1)
    own_blocks = gather_groups(links, level_block)
    chosen = gate(routes, level_block)[:, 0]
    picked = (chosen[:, None] == jnp.arange(experts, dtype=jnp.int32)[None, :]).astype(jnp.int32)
    rank = jnp.sum((jnp.cumsum(picked, axis=0) - picked) * picked, axis=1)
    place = chosen * most + rank
    slot_index = jnp.arange(experts * most, dtype=jnp.int32)
    to_slots = (slot_index[:, None] == place[None, :]).astype(BF)
    to_tokens = (place[:, None] == slot_index[None, :]).astype(BF)
    cot_slots = dot(to_slots, cotangent).astype(BF).reshape(experts, most, width)

    own_blocks = tie(*own_blocks, near_first, far_first, cot_slots)[:-3]
    other_blocks = [links.swap_core(part) for part in own_blocks]

    source = jnp.concatenate([near, near_first, far_first, far_second], axis=0).astype(F32)
    normed_work = (
        source * lax.rsqrt(jnp.mean(source * source, axis=-1, keepdims=True) + EPSILON)
    ).astype(BF)
    if level_rows % 16 == 0:
        queries, pair, weights, full_extra = project(flags, normed_work, own_blocks, other_blocks)
    else:
        full = in_order(links, own_blocks, other_blocks)
        weights, full_extra = full[:, : 3 * half_width], full[:, 3 * half_width :]
        projected = dot(normed_work, weights).astype(BF)
        queries, pair = projected[:, :half_width], projected[:, half_width:]
    pair_far = links.swap_core(pair)
    cot_arrived = all_to_all(gate(cot_slots, far_second)).reshape(-1, width)
    *mixed_parts, attention_weights, inverse = attention_forward(queries, pair, pair_far)
    mixed_parts = tie(*mixed_parts, cot_arrived)[:-1]

    back = tie(*[links.swap_level(mixed_parts[b], b) for b in (1, 2, 3)])
    full_router = full_extra[:, width : width + experts]
    gain_two = full_extra[:, width + 2 * experts].astype(F32)[None]
    tallies = full_extra[::own_rows, width + experts : width + 2 * experts].astype(F32)
    mine_only = (jnp.arange(experts, dtype=jnp.int32) == device).astype(F32)[None, :]
    counts = jnp.sum(tallies * mine_only, axis=1).astype(jnp.int32)
    offsets = jnp.cumsum(counts) - counts
    within = jnp.arange(most, dtype=jnp.int32)[None, :]
    slot_grid = offsets[:, None] + within
    usable = (within < counts[:, None]) & (slot_grid < capacity)
    slot_flat = jnp.where(usable, slot_grid, -1).reshape(-1)
    held_index = jnp.arange(capacity, dtype=jnp.int32)
    compact = (held_index[:, None] == slot_flat[None, :]).astype(BF)
    expand = (slot_flat[:, None] == held_index[None, :]).astype(BF)

    mixed_mine, mixed_sent = mixed_route(flags, [mixed_parts[0], *back])
    mixed_low, middle, second_slots = owner_forward(
        flags, mixed_mine, links.swap_core(mixed_sent), inputs, full_extra, gain_two, to_slots
    )
    arrived = all_to_all(second_slots.reshape(experts, most, width)).reshape(-1, width)

    cot_held, cot_back = cotangent_layer(gate(cot_arrived, second_slots), compact, expert_out)
    held, grad_result, hidden, grad_inner, grad_back, taken_held, grad_logits = expert_layer(
        flags,
        gate(arrived, cot_back),
        cot_held,
        cot_back,
        compact,
        expand,
        full_router,
        expert_in,
        expert_out,
    )
    grad_returned = all_to_all(grad_back.reshape(experts, most, width)).reshape(-1, width)
    grad_router = dot_tn(held, grad_logits)
    grad_weight_out = dot_tn(hidden, grad_result)
    grad_weight_in = dot_tn(held, grad_inner)
    taken_back = dot(expand, taken_held).astype(BF)
    grad_returned = gate(
        grad_returned, grad_weight_in, grad_weight_out, grad_router, taken_back, to_tokens
    )

    grad_middle, grad_branch, grad_mine, grad_sent, gain_rows = owner_backward(
        flags, grad_returned, to_tokens, cotangent, middle, gain_two, full_extra
    )
    routed = grad_route(flags, grad_mine, links.swap_core(grad_sent))
    got = [links.swap_level(routed[b], b) for b in (1, 2, 3)]

    got = tie(*got)
    taken_back = gate(taken_back, *got).reshape(experts, most, width)
    taken_arrived = all_to_all(taken_back).reshape(-1, width)
    grad_queries, grad_near, grad_far = attention_backward(
        queries,
        pair,
        pair_far,
        attention_weights,
        inverse,
        [routed[0], *got],
        mixed_parts,
    )
    got_pair = links.swap_core(grad_far)
    grad_projected, keep, send = weight_grads(
        flags,
        [normed_work, grad_queries, grad_near, got_pair]
        + [mixed_low, grad_branch, grad_router, gain_rows],
        level_rows,
    )
    grad_first_work = dot_nt(grad_projected, weights).astype(BF)
    core_sum = reduce_cores(links, keep, gate(send, taken_arrived))
    core_sum = gate(core_sum, grad_first_work)
    group_sum = reduce_groups(
        links, [core_sum[m * level_rows : (m + 1) * level_rows] for m in range(links.groups // 2)]
    )
    parts = gate(grad_first_work, core_sum).reshape(blocks, half_rows, width)
    back = tie(*[links.swap_level(parts[b], b) for b in (1, 2, 3)])
    near = (parts[0].astype(F32) + back[0].astype(F32)).astype(BF)
    far = (back[1].astype(F32) + back[2].astype(F32)).astype(BF)
    grad_first = workers_to_owner(links, near, far).astype(F32)
    source_own = inputs.astype(F32)
    inverse_one = lax.rsqrt(jnp.mean(source_own * source_own, axis=-1, keepdims=True) + EPSILON)
    normed_one = source_own * inverse_one
    grad_input = grad_middle + inverse_one * (
        grad_first - normed_one * jnp.mean(grad_first * normed_one, axis=-1, keepdims=True)
    )
    output = (middle + dot(to_tokens, taken_arrived)).astype(BF)

    sums = reduce_levels(links, gate(group_sum, *back))
    *grad_weights, grad_w_output, grad_w_router, grad_norm_one, grad_norm_two = finish(
        flags,
        [*sums, w_query, w_key, w_value, norm_one.reshape(1, own_rows)],
        experts,
    )
    return (
        output,
        grad_input,
        grad_norm_one.reshape(own_rows),
        grad_weights[0],
        grad_weights[1],
        grad_weights[2],
        grad_w_output,
        grad_norm_two.reshape(own_rows),
        grad_w_router,
        grad_weight_in[None],
        grad_weight_out[None],
    )


def solution(mesh):
    return jax.shard_map(
        on_device,
        mesh=mesh,
        in_specs=(
            P(AXES, None),
            P(AXES),
            P(AXES, None),
            P(AXES, None),
            P(AXES, None),
            P(AXES, None),
            P(AXES),
            P(AXES, None),
            P(AXES, None, None),
            P(AXES, None, None),
            P(AXES, None),
            P(AXES, None),
        ),
        out_specs=(
            P(AXES, None),
            P(AXES, None),
            P(AXES),
            P(AXES, None),
            P(AXES, None),
            P(AXES, None),
            P(AXES, None),
            P(AXES),
            P(AXES, None),
            P(AXES, None, None),
            P(AXES, None, None),
        ),
        check_vma=False,
    )
```

```python
import functools

import jax
import jax.numpy as jnp
from jax import lax
from jax.experimental import pallas as pl
from jax.experimental.pallas import tpu as pltpu
from jax.sharding import PartitionSpec as P

HEAD_DIM = 64
AXES = ("group", "local")
BF = jnp.bfloat16
F32 = jnp.float32
EPSILON = 1e-06
VMEM_BYTES = 58 * 2**20
SMALL_BYTES = 24 * 2**20


def dot(left, right):
    return jnp.dot(left, right, preferred_element_type=F32)


def dot_tn(left, right):
    return lax.dot_general(left, right, (((0,), (0,)), ((), ())), preferred_element_type=F32)


def dot_nt(left, right):
    return lax.dot_general(left, right, (((1,), (1,)), ((), ())), preferred_element_type=F32)


class Links:
    def __init__(self):
        self.groups = lax.axis_size("group")
        self.levels = lax.axis_size("local")
        self.group = lax.axis_index("group")
        self.level = lax.axis_index("local")
        self.core = self.group % 2

    def permute(self, array, target):
        pairs = []
        for group in range(self.groups):
            for level in range(self.levels):
                other_group, other_level = target(group, level)
                pairs.append((group * self.levels + level, other_group * self.levels + other_level))
        return lax.ppermute(array, AXES, pairs)

    def swap_core(self, array):
        return self.permute(array, lambda g, l: (g ^ 1, l))

    def swap_level(self, array, mask):
        return self.permute(array, lambda g, l: (g, l ^ mask))

    def swap_group(self, array, mask):
        return self.permute(array, lambda g, l: (g ^ (2 * mask), l))


def gate(array, *after):
    return lax.optimization_barrier((array, *after))[0]


def tie(*arrays):
    return lax.optimization_barrier(arrays)


def pick(flag, first, second):
    return jnp.where(flag == 0, first, second)


def joined(flag, mine, other, axis=0):
    return jnp.concatenate([pick(flag, mine, other), pick(flag, other, mine)], axis=axis)


def ordered(index, parts):
    count = len(parts)
    if count == 1:
        return parts[0]
    top = count.bit_length() - 2
    half = count // 2
    low = index & (half - 1)
    return joined((index >> top) & 1, ordered(low, parts[:half]), ordered(low, parts[half:]))


def rows_of(array, index, rows):
    return lax.dynamic_slice_in_dim(array, index * rows, rows, axis=0)


def gather_levels(links, pieces):
    got = tie(*[links.swap_level(pieces[b], b) for b in range(1, links.levels)])
    return ordered(links.level, [pieces[0], *got])


def gather_groups(links, block):
    return [block] + [links.swap_group(block, m) for m in range(1, links.groups // 2)]


def in_order(links, own, other):
    pairs = [joined(links.core, mine, far) for mine, far in zip(own, other)]
    return ordered(links.group >> 1, pairs)


def reduce_cores(links, keep, send):
    return keep + links.swap_core(send).astype(F32)


def reduce_groups(links, parts):
    got = [links.swap_group(parts[m].astype(BF), m) for m in range(1, len(parts))]
    total = parts[0]
    for part in tie(*got):
        total = total + part.astype(F32)
    return total


def reduce_levels(links, block):
    rows = block.shape[0] // links.levels
    parts = [rows_of(block, links.level ^ b, rows) for b in range(links.levels)]
    got = tie(*[links.swap_level(parts[b].astype(BF), b) for b in range(1, links.levels)])
    return [parts[0], *got]


def owner_to_workers(links, array):
    half = array.shape[0] // 2
    mine = pick(links.core, array[:half], array[half:])
    other = links.swap_core(pick(links.core, array[half:], array[:half]))
    same = (links.level >> 1) ^ links.core
    return pick(same, mine, other), pick(same, other, mine)


def workers_to_owner(links, near, far):
    same = (links.level >> 1) ^ links.core
    mine = pick(same, near, far)
    other = links.swap_core(pick(same, far, near))
    return joined(links.core, mine, other)


PAIR = 2 * HEAD_DIM


def head_masks(dtype):
    lanes = lax.broadcasted_iota(jnp.int32, (1, PAIR), 1)
    return [(lanes // HEAD_DIM == head).astype(dtype) for head in range(2)]


CHUNK = 128


def forward_kernel(query_ref, key_ref, value_ref, key_far_ref, value_far_ref, *refs):
    mixed_refs, weights_ref, inverse_ref = refs[:-2], refs[-2], refs[-1]
    query = query_ref[...] * BF(HEAD_DIM**-0.5)
    key = jnp.concatenate([key_ref[...], key_far_ref[...]], axis=0)
    value = jnp.concatenate([value_ref[...], value_far_ref[...]], axis=0)
    value = jnp.concatenate([value, jnp.ones_like(value)], axis=1)
    first_head = lax.broadcasted_iota(jnp.int32, (1, PAIR), 1) < HEAD_DIM
    for part, mixed_ref in enumerate(mixed_refs):
        rows = slice(part * CHUNK, (part + 1) * CHUNK)
        sums = []
        for head, mask in enumerate(head_masks(BF)):
            scores = dot_nt(query[rows] * mask, key)
            weights = jnp.exp(scores - jnp.max(scores, axis=1, keepdims=True)).astype(BF)
            weights_ref[head, rows] = weights
            sums.append(dot(weights, value))
        mixed = jnp.where(first_head, sums[0][:, :PAIR], sums[1][:, :PAIR])
        inverse = 1.0 / jnp.where(first_head, sums[0][:, PAIR:], sums[1][:, PAIR:])
        inverse_ref[rows] = inverse
        mixed_ref[...] = (mixed * inverse).astype(BF)


def pair_column(rows, block=0):
    return pl.BlockSpec((rows, PAIR), lambda i: (0, block + i))


def weights_block(rows):
    return pl.BlockSpec((2, rows, 2 * rows), lambda i: (i, 0, 0))


def attention_forward(queries, pair, pair_far):
    rows, half_width = queries.shape
    pairs = half_width // PAIR
    return pl.pallas_call(
        forward_kernel,
        grid=(pairs,),
        in_specs=[pair_column(rows)] + [pair_column(rows), pair_column(rows, pairs)] * 2,
        out_specs=[pair_column(CHUNK)] * (rows // CHUNK) + [weights_block(rows), pair_column(rows)],
        out_shape=[low_shape(CHUNK, half_width)] * (rows // CHUNK)
        + [low_shape(2 * pairs, rows, 2 * rows), wide_shape(rows, half_width)],
        compiler_params=params(),
        cost_estimate=cost(2 * 10**9, 4096),
    )(queries, pair, pair, pair_far, pair_far)


def backward_kernel(
    query_ref, key_ref, value_ref, key_far_ref, value_far_ref, weights_ref, inverse_ref, *refs
):
    grad_refs, mixed_refs = refs[:4], refs[4:8]
    grad_query_ref, grad_near_ref, grad_far_ref = refs[8:]
    all_rows = query_ref.shape[0]
    factor = BF(HEAD_DIM**-0.5)
    query = query_ref[...] * factor
    key = jnp.concatenate([key_ref[...], key_far_ref[...]], axis=0)
    value = jnp.concatenate([value_ref[...], value_far_ref[...]], axis=0)
    grad = jnp.concatenate([ref[...] for ref in grad_refs], axis=0).astype(F32)
    grad = grad * inverse_ref[...]
    mixed = jnp.concatenate([ref[...] for ref in mixed_refs], axis=0)
    together = grad * mixed.astype(F32)
    grad = grad.astype(BF)
    grad_key = jnp.zeros((PAIR, 2 * all_rows), F32)
    grad_value = jnp.zeros((PAIR, 2 * all_rows), F32)
    for part in range(all_rows // (2 * CHUNK)):
        rows = slice(part * 2 * CHUNK, (part + 1) * 2 * CHUNK)
        grad_query = jnp.zeros((2 * CHUNK, PAIR), F32)
        for head, (mask, mask_wide) in enumerate(zip(head_masks(BF), head_masks(F32))):
            weights = weights_ref[head, rows]
            grad_one = grad[rows] * mask
            row_dots = jnp.sum(together[rows] * mask_wide, axis=1, keepdims=True)
            grad_weights = dot_nt(grad_one, value)
            grad_scores = (weights.astype(F32) * (grad_weights - row_dots)).astype(BF)
            grad_value = grad_value + dot_tn(grad_one, weights)
            grad_key = grad_key + dot_tn(query[rows] * mask, grad_scores)
            grad_query = grad_query + dot(grad_scores, key * (mask * factor))
        grad_query_ref[rows] = grad_query.astype(BF)
    for index, total in enumerate((grad_key, grad_value)):
        total = total.T
        grad_near_ref[index] = total[:all_rows].astype(BF)
        grad_far_ref[index] = total[all_rows:].astype(BF)


def attention_backward(queries, pair, pair_far, weights, inverse, grads, mixed):
    rows, half_width = queries.shape
    pairs = half_width // PAIR
    return pl.pallas_call(
        backward_kernel,
        grid=(pairs,),
        in_specs=[pair_column(rows)]
        + [pair_column(rows), pair_column(rows, pairs)] * 2
        + [weights_block(rows), pair_column(rows)]
        + [pair_column(rows // 4)] * 8,
        out_specs=[pair_column(rows)] + [pl.BlockSpec((2, rows, PAIR), lambda i: (0, 0, i))] * 2,
        out_shape=[low_shape(rows, half_width)] + [low_shape(2, rows, half_width)] * 2,
        compiler_params=params(),
        cost_estimate=cost(2 * 10**10, 4096),
    )(queries, pair, pair, pair_far, pair_far, weights, inverse, *grads, *mixed)


GELU_SCALE = 0.7978845608028654
GELU_CUBE = 0.044715


def gelu_and_slope(values):
    square = values * values
    bend = jnp.tanh(GELU_SCALE * values * (1.0 + GELU_CUBE * square))
    half = 0.5 + 0.5 * bend
    slope = half + 0.5 * values * (1.0 - bend * bend) * GELU_SCALE * (1.0 + 3 * GELU_CUBE * square)
    return values * half, slope


def whole(shape):
    return pl.BlockSpec(shape, lambda *_: (0,) * len(shape))


FLAGS = pl.BlockSpec(memory_space=pltpu.SMEM)
CORE, HALF, SAME, DEVICE, PLACE = range(5)


def params(size=VMEM_BYTES):
    return pltpu.CompilerParams(vmem_limit_bytes=size)


def cost(flops, size):
    return pl.CostEstimate(flops=flops, bytes_accessed=size, transcendentals=0)


def one_step(kernel, flags, operands, shapes, scratch=(), size=VMEM_BYTES):
    return pl.pallas_call(
        kernel,
        grid=(1,),
        in_specs=[FLAGS] + [whole(operand.shape) for operand in operands],
        out_specs=[whole(shape.shape) for shape in shapes],
        out_shape=shapes,
        scratch_shapes=list(scratch),
        compiler_params=params(size),
        cost_estimate=cost(0, 2**20),
    )(flags, *operands)


def low_shape(*shape):
    return jax.ShapeDtypeStruct(shape, BF)


def wide_shape(*shape):
    return jax.ShapeDtypeStruct(shape, F32)


def each_case(flags_ref, body):
    for half in range(2):
        for same in range(2):

            @pl.when((flags_ref[HALF] == half) & (flags_ref[SAME] == same))
            def _(half=half, same=same):
                body(half, same)


def turned_column(row):
    count = row.shape[1]
    rows = lax.broadcasted_iota(jnp.int32, (count, count), 0)
    lanes = lax.broadcasted_iota(jnp.int32, (count, count), 1)
    return jnp.sum(jnp.where(rows == lanes, row, 0.0), axis=1, keepdims=True)


def turned_row(column):
    count = column.shape[0]
    rows = lax.broadcasted_iota(jnp.int32, (count, count), 0)
    lanes = lax.broadcasted_iota(jnp.int32, (count, count), 1)
    return jnp.sum(jnp.where(rows == lanes, column, 0.0), axis=0, keepdims=True)


def pack_kernel(
    flags_ref,
    query_ref,
    key_ref,
    value_ref,
    output_ref,
    router_ref,
    routes_ref,
    norm_one_ref,
    norm_two_ref,
    kept_ref,
    cross_ref,
):
    own_rows, width = query_ref.shape
    experts = router_ref.shape[1]
    half_width = width // 2
    start = 3 * half_width
    tail = kept_ref.shape[1] - start - width
    scale = turned_column(norm_one_ref[...].astype(F32))
    first_half = flags_ref[HALF] == 0
    for index, ref in enumerate((query_ref, key_ref, value_ref)):
        scaled = (ref[...].astype(F32) * scale).astype(BF)
        low, high = scaled[:, :half_width], scaled[:, half_width:]
        columns = slice(index * half_width, (index + 1) * half_width)
        kept_ref[:, columns] = jnp.where(first_half, low, high)
        cross_ref[:, columns] = jnp.where(first_half, high, low)
    lanes = lax.broadcasted_iota(jnp.int32, (1, tail), 1)
    index = lax.broadcasted_iota(jnp.int32, (tail, 1), 0) - experts
    tally = jnp.sum((routes_ref[...] == index).astype(F32), axis=1, keepdims=True)
    tally = turned_row(tally)
    router = router_ref[...].astype(F32)
    router = jnp.concatenate([router, jnp.zeros((own_rows, tail - experts), F32)], axis=1)
    gain = turned_column(norm_two_ref[...].astype(F32))
    small = jnp.where(lanes < experts, router, jnp.where(lanes == 2 * experts, gain, tally))
    for ref in (kept_ref, cross_ref):
        ref[:, start : start + width] = output_ref[...]
        ref[:, start + width :] = small.astype(BF)


def pack(flags, operands):
    own_rows, width = operands[0].shape
    experts = operands[4].shape[1]
    tail = 2 * experts + 1
    columns = 3 * width // 2 + width + tail + -tail % 128
    return one_step(pack_kernel, flags, operands, [low_shape(own_rows, columns)] * 2)


def finish_kernel(
    flags_ref,
    zero_ref,
    one_ref,
    two_ref,
    three_ref,
    query_ref,
    key_ref,
    value_ref,
    norm_one_ref,
    grad_query_ref,
    grad_key_ref,
    grad_value_ref,
    grad_output_ref,
    grad_router_ref,
    grad_one_ref,
    grad_two_ref,
):
    width = query_ref.shape[1]
    experts = grad_router_ref.shape[1]
    half_width = width // 2
    start = 3 * half_width
    near = zero_ref[...] + two_ref[...].astype(F32)
    far = one_ref[...].astype(F32) + three_ref[...].astype(F32)
    scale = turned_column(norm_one_ref[...].astype(F32))
    first_half = flags_ref[HALF] == 0
    total = jnp.zeros_like(scale)
    pairs = ((query_ref, grad_query_ref), (key_ref, grad_key_ref), (value_ref, grad_value_ref))
    for index, (ref, grad_ref) in enumerate(pairs):
        columns = slice(index * half_width, (index + 1) * half_width)
        low = jnp.where(first_half, near[:, columns], far[:, columns])
        high = jnp.where(first_half, far[:, columns], near[:, columns])
        weight = ref[...].astype(F32)
        total = total + jnp.sum(weight[:, :half_width] * low, axis=1, keepdims=True)
        total = total + jnp.sum(weight[:, half_width:] * high, axis=1, keepdims=True)
        grad_ref[:, :half_width] = low * scale
        grad_ref[:, half_width:] = high * scale
    grad_one_ref[...] = turned_row(total)
    both = near[:, start:] + far[:, start:]
    grad_output_ref[...] = both[:, :width]
    small = both[:, width:]
    grad_router_ref[...] = small[:, :experts]
    lanes = lax.broadcasted_iota(jnp.int32, (1, small.shape[1]), 1)
    gain = jnp.sum(jnp.where(lanes == experts, small, 0.0), axis=1, keepdims=True)
    grad_two_ref[...] = turned_row(gain)


def finish(flags, operands, experts):
    own_rows, width = operands[4].shape
    shapes = [wide_shape(own_rows, width)] * 4
    shapes += [wide_shape(own_rows, experts)] + [wide_shape(1, own_rows)] * 2
    return one_step(finish_kernel, flags, operands, shapes, size=SMALL_BYTES)


def project_kernel(count, flags_ref, normed_ref, *refs):
    own_refs, other_refs = refs[:count], refs[count : 2 * count]
    query_ref, pair_ref, weight_ref = refs[2 * count :]
    rows = own_refs[0].shape[0]
    core = flags_ref[CORE]
    for m in range(count):
        place = 2 * (flags_ref[PLACE] ^ m)
        for index, ref in ((place + core, own_refs[m]), (place + 1 - core, other_refs[m])):
            place_rows = pl.ds(pl.multiple_of(index * rows, 16), rows)
            weight_ref[place_rows, :] = ref[...]
    projected = dot(normed_ref[...], weight_ref[...]).astype(BF)
    query_ref[...] = projected[:, : query_ref.shape[1]]
    pair_ref[...] = projected[:, query_ref.shape[1] :]


def project(flags, normed, own, other):
    count = len(own)
    rows, width = normed.shape
    columns = 3 * width // 2
    shapes = [
        low_shape(rows, width // 2),
        low_shape(rows, width),
        low_shape(width, columns),
    ]
    kernel = functools.partial(project_kernel, count)
    return one_step(kernel, flags, [normed, *own, *other], shapes)


def assemble_kernel(lane, flags_ref, *refs):
    *own_refs, other_ref, full_ref, row_ref = refs
    rows = own_refs[0].shape[0]
    width = full_ref.shape[0]
    core = flags_ref[CORE]
    for m, own_ref in enumerate(own_refs):
        place = 2 * (flags_ref[PLACE] ^ m)
        full_ref[pl.ds(pl.multiple_of((place + core) * rows, 16), rows), :] = own_ref[...]
        full_ref[pl.ds(pl.multiple_of((place + 1 - core) * rows, 16), rows), :] = other_ref[
            m * rows : (m + 1) * rows, :
        ]
    start = width + lane // 128 * 128
    block = full_ref[:, start : start + 128].astype(F32).T
    row_ref[...] = block[lane % 128 : lane % 128 + 1]


def assemble(flags, operands, lane):
    columns = operands[0].shape[1]
    width = 2 * operands[-1].shape[0]
    shapes = [low_shape(width, columns), wide_shape(1, width)]
    return one_step(functools.partial(assemble_kernel, lane), flags, operands, shapes)


def mixed_route_kernel(flags_ref, zero_ref, one_ref, two_ref, three_ref, mine_ref, sent_ref):
    half_width = zero_ref.shape[1]

    def body(half, same):
        near_ref, far_ref = (mine_ref, sent_ref) if same == 0 else (sent_ref, mine_ref)
        for into_ref, refs in ((near_ref, (zero_ref, one_ref)), (far_ref, (two_ref, three_ref))):
            into_ref[:, :half_width] = refs[half][...]
            into_ref[:, half_width:] = refs[1 - half][...]

    each_case(flags_ref, body)


def mixed_route(flags, parts):
    rows, half_width = parts[0].shape
    shapes = [low_shape(rows, 2 * half_width)] * 2
    return one_step(mixed_route_kernel, flags, parts, shapes, size=SMALL_BYTES)


def grad_route_kernel(flags_ref, mine_ref, got_ref, zero_ref, one_ref, two_ref, three_ref):
    half_width = zero_ref.shape[1]

    def body(half, same):
        near_ref, far_ref = (mine_ref, got_ref) if same == 0 else (got_ref, mine_ref)
        for from_ref, refs in ((near_ref, (zero_ref, one_ref)), (far_ref, (two_ref, three_ref))):
            refs[half][...] = from_ref[:, :half_width]
            refs[1 - half][...] = from_ref[:, half_width:]

    each_case(flags_ref, body)


def grad_route(flags, mine, got):
    rows, width = mine.shape
    shapes = [low_shape(rows, width // 2)] * 4
    return one_step(grad_route_kernel, flags, [mine, got], shapes, size=SMALL_BYTES)


def owner_forward_kernel(
    flags_ref,
    mine_ref,
    got_ref,
    inputs_ref,
    weight_ref,
    gain_ref,
    to_slots_ref,
    mixed_ref,
    middle_ref,
    slots_ref,
):
    half_rows = mine_ref.shape[0]
    for core in range(2):

        @pl.when(flags_ref[CORE] == core)
        def _(core=core):
            refs = (mine_ref, got_ref)
            mixed_ref[:half_rows] = refs[core][...]
            mixed_ref[half_rows:] = refs[1 - core][...]

    weight = weight_ref[:, : mixed_ref.shape[1]]
    middle = inputs_ref[...].astype(F32) + dot(mixed_ref[...], weight)
    middle_ref[...] = middle
    inverse = lax.rsqrt(jnp.mean(middle * middle, axis=1, keepdims=True) + EPSILON)
    second_low = (middle * inverse * gain_ref[...]).astype(BF)
    slots_ref[...] = dot(to_slots_ref[...], second_low).astype(BF)


def owner_forward(flags, mine, got, inputs, full_extra, gain, to_slots):
    rows, width = inputs.shape
    shapes = [
        low_shape(rows, width),
        wide_shape(rows, width),
        low_shape(to_slots.shape[0], width),
    ]
    operands = [mine, got, inputs, full_extra, gain, to_slots]
    return one_step(owner_forward_kernel, flags, operands, shapes)


TILE = 1024


def cotangent_kernel(cot_ref, compact_ref, weight_out_ref, held_ref, back_ref):
    @pl.when(pl.program_id(0) == 0)
    def _():
        held_ref[...] = dot(compact_ref[...], cot_ref[...]).astype(BF)

    back_ref[...] = dot_nt(held_ref[...], weight_out_ref[0]).astype(BF)


def cotangent_layer(cot, compact, expert_out):
    slots, width = cot.shape
    capacity = compact.shape[0]
    hidden_width = expert_out.shape[1]
    return pl.pallas_call(
        cotangent_kernel,
        grid=(hidden_width // TILE,),
        in_specs=[
            whole((slots, width)),
            whole((capacity, slots)),
            pl.BlockSpec((1, TILE, width), lambda i: (0, i, 0)),
        ],
        out_specs=[whole((capacity, width)), pl.BlockSpec((capacity, TILE), lambda i: (0, i))],
        out_shape=[low_shape(capacity, width), low_shape(capacity, hidden_width)],
        compiler_params=params(),
        cost_estimate=cost(2 * capacity * width * hidden_width, 4 * width * hidden_width),
    )(cot, compact, expert_out)


def expert_kernel(
    flags_ref,
    arrived_ref,
    cot_ref,
    back_ref,
    compact_ref,
    expand_ref,
    router_ref,
    weight_in_ref,
    weight_out_ref,
    held_ref,
    grad_result_ref,
    hidden_ref,
    grad_inner_ref,
    grad_back_ref,
    taken_ref,
    grad_logits_ref,
    result_sum,
    grad_sum,
    probs,
    gates,
):
    step = pl.program_id(0)
    experts = router_ref.shape[1]
    lanes = lax.broadcasted_iota(jnp.int32, (1, experts), 1)
    mine = (lanes == flags_ref[DEVICE]).astype(F32)

    @pl.when(step == 0)
    def _():
        held = dot(compact_ref[...], arrived_ref[...]).astype(BF)
        held_ref[...] = held
        logits = dot(held, router_ref[...])
        weights = jnp.exp(logits - jnp.max(logits, axis=1, keepdims=True))
        router_probs = weights / jnp.sum(weights, axis=1, keepdims=True)
        probs[...] = router_probs
        gate = jnp.sum(router_probs * mine, axis=1, keepdims=True)
        gates[...] = gate
        grad_result_ref[...] = (gate * cot_ref[...].astype(F32)).astype(BF)
        result_sum[...] = jnp.zeros_like(result_sum)
        grad_sum[...] = jnp.zeros_like(grad_sum)

    weight_in = weight_in_ref[0]
    hidden, slope = gelu_and_slope(dot(held_ref[...], weight_in))
    hidden = hidden.astype(BF)
    hidden_ref[...] = hidden
    grad_inner = (back_ref[...].astype(F32) * (gates[...] * slope)).astype(BF)
    grad_inner_ref[...] = grad_inner
    result_sum[...] += dot(hidden, weight_out_ref[0])
    grad_sum[...] += dot_nt(grad_inner, weight_in)

    @pl.when(step == pl.num_programs(0) - 1)
    def _():
        result = result_sum[...].astype(BF).astype(F32)
        gate = gates[...]
        grad_gate = jnp.sum(cot_ref[...].astype(F32) * result, axis=1, keepdims=True)
        grad_logits = (grad_gate * probs[...] * (mine - gate)).astype(BF)
        grad_logits_ref[...] = grad_logits
        grad_held = grad_sum[...] + dot_nt(grad_logits, router_ref[...])
        grad_back_ref[...] = dot(expand_ref[...], grad_held.astype(BF)).astype(BF)
        taken_ref[...] = (gate * result).astype(BF)


def expert_layer(flags, arrived, cot, back, compact, expand, router, expert_in, expert_out):
    slots, width = arrived.shape
    capacity = compact.shape[0]
    hidden_width = expert_in.shape[2]
    experts = router.shape[1]
    wide = whole((capacity, width))
    tall = pl.BlockSpec((capacity, TILE), lambda i: (0, i))
    return pl.pallas_call(
        expert_kernel,
        grid=(hidden_width // TILE,),
        in_specs=[
            FLAGS,
            whole((slots, width)),
            wide,
            tall,
            whole((capacity, slots)),
            whole((slots, capacity)),
            whole((width, experts)),
            pl.BlockSpec((1, width, TILE), lambda i: (0, 0, i)),
            pl.BlockSpec((1, TILE, width), lambda i: (0, i, 0)),
        ],
        out_specs=[wide, wide, tall, tall, whole((slots, width)), wide]
        + [whole((capacity, experts))],
        out_shape=[
            low_shape(capacity, width),
            low_shape(capacity, width),
            low_shape(capacity, hidden_width),
            low_shape(capacity, hidden_width),
            low_shape(slots, width),
            low_shape(capacity, width),
            low_shape(capacity, experts),
        ],
        scratch_shapes=[
            pltpu.VMEM((capacity, width), F32),
            pltpu.VMEM((capacity, width), F32),
            pltpu.VMEM((capacity, experts), F32),
            pltpu.VMEM((capacity, 1), F32),
        ],
        compiler_params=params(),
        cost_estimate=cost(8 * capacity * width * hidden_width, 8 * width * hidden_width),
    )(flags, arrived, cot, back, compact, expand, router, expert_in, expert_out)


def owner_backward_kernel(
    flags_ref,
    returned_ref,
    to_tokens_ref,
    cotangent_ref,
    middle_ref,
    gain_ref,
    weight_ref,
    grad_middle_ref,
    grad_branch_ref,
    mine_ref,
    sent_ref,
    grad_gain_ref,
):
    half_rows = mine_ref.shape[0]
    middle = middle_ref[...]
    inverse = lax.rsqrt(jnp.mean(middle * middle, axis=1, keepdims=True) + EPSILON)
    normed = middle * inverse
    grad_second = dot(to_tokens_ref[...], returned_ref[...])
    grouped = (grad_second * normed).reshape(-1, GAIN_ROWS, grad_second.shape[1])
    grad_gain_ref[...] = jnp.sum(grouped, axis=0).astype(BF)
    scaled = grad_second * gain_ref[...]
    grad_middle = cotangent_ref[...].astype(F32) + inverse * (
        scaled - normed * jnp.mean(scaled * normed, axis=1, keepdims=True)
    )
    grad_middle_ref[...] = grad_middle
    grad_branch = grad_middle.astype(BF)
    grad_branch_ref[...] = grad_branch
    weight = weight_ref[:, : middle.shape[1]]
    grad_mixed = dot_nt(grad_branch, weight).astype(BF)
    for core in range(2):

        @pl.when(flags_ref[CORE] == core)
        def _(core=core):
            mine_ref[...] = grad_mixed[core * half_rows : (core + 1) * half_rows]
            sent_ref[...] = grad_mixed[(1 - core) * half_rows : (2 - core) * half_rows]


def owner_backward(flags, returned, to_tokens, cotangent, middle, gain, full_extra):
    rows, width = cotangent.shape
    shapes = [
        wide_shape(rows, width),
        low_shape(rows, width),
        low_shape(rows // 2, width),
        low_shape(rows // 2, width),
        low_shape(GAIN_ROWS, width),
    ]
    operands = [returned, to_tokens, cotangent, middle, gain, full_extra]
    return one_step(owner_backward_kernel, flags, operands, shapes)


GAIN_ROWS = 16


def deal_rows(flags_ref, total, keep_ref, send_ref, rows):
    core = flags_ref[CORE]
    for m in range(total.shape[0] // (2 * rows)):
        place = 2 * (flags_ref[PLACE] ^ m)
        keep_ref[m * rows : (m + 1) * rows, :] = total[
            pl.ds(pl.multiple_of((place + core) * rows, 8), rows), :
        ]
        send_ref[m * rows : (m + 1) * rows, :] = total[
            pl.ds(pl.multiple_of((place + 1 - core) * rows, 8), rows), :
        ].astype(BF)


def dealt(width, columns):
    return [wide_shape(width // 2, columns), low_shape(width // 2, columns)]


def weight_grads_kernel(
    rows,
    flags_ref,
    normed_ref,
    query_ref,
    near_ref,
    got_ref,
    mixed_ref,
    branch_ref,
    router_ref,
    gain_ref,
    projected_ref,
    keep_ref,
    send_ref,
    total,
):
    part = query_ref.shape[1]
    width, experts = router_ref.shape
    extra = total.shape[1] - 3 * part - width
    projected_ref[:, :part] = query_ref[...]
    for index in range(2):
        both = near_ref[index].astype(F32) + got_ref[index].astype(F32)
        projected_ref[:, (index + 1) * part : (index + 2) * part] = both.astype(BF)
    total[:, : 3 * part] = dot_tn(normed_ref[...], projected_ref[...])
    total[:, 3 * part : 3 * part + width] = dot_tn(mixed_ref[...], branch_ref[...])
    gain = dot_tn(gain_ref[...], jnp.ones((GAIN_ROWS, extra), BF))
    router = router_ref[...]
    router = jnp.concatenate([router, jnp.zeros((width, extra - experts), F32)], axis=1)
    lanes = lax.broadcasted_iota(jnp.int32, (1, extra), 1)
    total[:, 3 * part + width :] = jnp.where(lanes == experts, gain, router)
    deal_rows(flags_ref, total, keep_ref, send_ref, rows)


def weight_grads(flags, operands, rows):
    work_rows, width = operands[0].shape
    part = operands[1].shape[1]
    experts = operands[6].shape[1]
    columns = 3 * part + width + experts + 1
    columns += -columns % 128
    return one_step(
        functools.partial(weight_grads_kernel, rows),
        flags,
        operands,
        [low_shape(work_rows, 3 * part)] + dealt(width, columns),
        [pltpu.VMEM((width, columns), F32)],
        2 * SMALL_BYTES,
    )


def all_to_all(array):
    return lax.all_to_all(array, AXES, split_axis=0, concat_axis=0, tiled=True)


def on_device(
    inputs,
    norm_one,
    w_query,
    w_key,
    w_value,
    w_output,
    norm_two,
    w_router,
    expert_in,
    expert_out,
    routes,
    cotangent,
):
    links = Links()
    level, core = links.level, links.core
    device = links.group * links.levels + level
    devices = links.groups * links.levels
    rows, width = inputs.shape
    half_rows = rows // 2
    half_width = width // 2
    experts = w_router.shape[1]
    own_rows = norm_one.shape[0]
    most = 2 * rows // experts
    capacity = 5 * rows // 4
    blocks = links.levels

    same = (level >> 1) ^ core
    flags = jnp.stack([core, level & 1, same, device, links.group >> 1]).astype(jnp.int32)

    mine = pick(core, inputs[:half_rows], inputs[half_rows:])
    got = links.swap_core(pick(core, inputs[half_rows:], inputs[:half_rows]))
    kept, cross = pack(
        flags,
        [w_query, w_key, w_value, w_output, w_router, routes.reshape(1, rows)]
        + [norm_one.reshape(1, own_rows), norm_two.reshape(1, own_rows)],
    )
    level_block = gather_levels(links, [kept, cross, kept, cross])
    level_rows = level_block.shape[0]
    got = gate(got, kept, cross)
    near, far = pick(same, mine, got), pick(same, got, mine)
    near_first = links.swap_level(near, 1)
    far_first = links.swap_level(far, 2)
    far_second = links.swap_level(far_first, 1)
    level_weights = level_block[:, : 3 * half_width]
    own_blocks = gather_groups(links, level_weights)
    chosen = gate(routes, level_block)[:, 0]
    picked = (chosen[:, None] == jnp.arange(experts, dtype=jnp.int32)[None, :]).astype(jnp.int32)
    rank = jnp.sum((jnp.cumsum(picked, axis=0) - picked) * picked, axis=1)
    place = chosen * most + rank
    slot_index = jnp.arange(experts * most, dtype=jnp.int32)
    to_slots = (slot_index[:, None] == place[None, :]).astype(BF)
    to_tokens = (place[:, None] == slot_index[None, :]).astype(BF)
    cot_slots = dot(to_slots, cotangent).astype(BF).reshape(experts, most, width)

    own_blocks = tie(*own_blocks, near_first, far_first, cot_slots)[:-3]
    other_blocks = [links.swap_core(part) for part in own_blocks]

    source = jnp.concatenate([near, near_first, far_first, far_second], axis=0).astype(F32)
    normed_work = (
        source * lax.rsqrt(jnp.mean(source * source, axis=-1, keepdims=True) + EPSILON)
    ).astype(BF)
    own_extra = gather_groups(links, gate(level_block[:, 3 * half_width :], *own_blocks))
    if level_rows % 16 == 0:
        queries, pair, weights = project(flags, normed_work, own_blocks, other_blocks)
    else:
        weights = in_order(links, own_blocks, other_blocks)
        projected = dot(normed_work, weights).astype(BF)
        queries, pair = projected[:, :half_width], projected[:, half_width:]
    pair_far = links.swap_core(pair)
    cot_arrived = all_to_all(gate(cot_slots, *own_blocks)).reshape(-1, width)
    *mixed_parts, attention_weights, inverse = attention_forward(queries, pair, pair_far)
    mixed_parts = tie(*mixed_parts, cot_arrived, *own_extra)[:4]

    own_extra = tie(*own_extra, *mixed_parts)[: len(own_extra)]
    other_extra = links.swap_core(jnp.concatenate(own_extra, axis=0))
    if level_rows % 16 == 0:
        full_extra, gain_two = assemble(flags, [*own_extra, other_extra], 2 * experts)
    else:
        other_parts = [
            other_extra[m * level_rows : (m + 1) * level_rows] for m in range(len(own_extra))
        ]
        full_extra = in_order(links, own_extra, other_parts)
        gain_two = full_extra[:, width + 2 * experts].astype(F32)[None]
    full_router = full_extra[:, width : width + experts]
    last_part = gate(mixed_parts[3], gain_two)
    back = [links.swap_level(mixed_parts[1], 1), links.swap_level(mixed_parts[2], 2)]
    back = tie(*back, links.swap_level(last_part, 3))
    tallies = full_extra[::own_rows, width + experts : width + 2 * experts].astype(F32)
    mine_only = (jnp.arange(experts, dtype=jnp.int32) == device).astype(F32)[None, :]
    counts = jnp.sum(tallies * mine_only, axis=1).astype(jnp.int32)
    offsets = jnp.cumsum(counts) - counts
    within = jnp.arange(most, dtype=jnp.int32)[None, :]
    slot_grid = offsets[:, None] + within
    usable = (within < counts[:, None]) & (slot_grid < capacity)
    slot_flat = jnp.where(usable, slot_grid, -1).reshape(-1)
    held_index = jnp.arange(capacity, dtype=jnp.int32)
    compact = (held_index[:, None] == slot_flat[None, :]).astype(BF)
    expand = (slot_flat[:, None] == held_index[None, :]).astype(BF)

    mixed_mine, mixed_sent = mixed_route(flags, [mixed_parts[0], *back])
    mixed_low, middle, second_slots = owner_forward(
        flags, mixed_mine, links.swap_core(mixed_sent), inputs, full_extra, gain_two, to_slots
    )
    arrived = all_to_all(second_slots.reshape(experts, most, width)).reshape(-1, width)

    cot_held, cot_back = cotangent_layer(gate(cot_arrived, second_slots), compact, expert_out)
    held, grad_result, hidden, grad_inner, grad_back, taken_held, grad_logits = expert_layer(
        flags,
        gate(arrived, cot_back),
        cot_held,
        cot_back,
        compact,
        expand,
        full_router,
        expert_in,
        expert_out,
    )
    grad_returned = all_to_all(grad_back.reshape(experts, most, width)).reshape(-1, width)
    grad_router = dot_tn(held, grad_logits)
    grad_weight_out = dot_tn(hidden, grad_result)
    grad_weight_in = dot_tn(held, grad_inner)
    taken_back = dot(expand, taken_held).astype(BF)
    grad_returned = gate(
        grad_returned, grad_weight_in, grad_weight_out, grad_router, taken_back, to_tokens
    )

    grad_middle, grad_branch, grad_mine, grad_sent, gain_rows = owner_backward(
        flags, grad_returned, to_tokens, cotangent, middle, gain_two, full_extra
    )
    routed = grad_route(flags, grad_mine, links.swap_core(grad_sent))
    got = [links.swap_level(routed[b], b) for b in (1, 2, 3)]

    got = tie(*got)
    taken_back = gate(taken_back, *got).reshape(experts, most, width)
    taken_arrived = all_to_all(taken_back).reshape(-1, width)
    grad_queries, grad_near, grad_far = attention_backward(
        queries,
        pair,
        pair_far,
        attention_weights,
        inverse,
        [routed[0], *got],
        mixed_parts,
    )
    got_pair = links.swap_core(grad_far)
    grad_projected, keep, send = weight_grads(
        flags,
        [normed_work, grad_queries, grad_near, got_pair]
        + [mixed_low, grad_branch, grad_router, gain_rows],
        level_rows,
    )
    grad_first_work = dot_nt(grad_projected, weights).astype(BF)
    core_sum = reduce_cores(links, keep, gate(send, taken_arrived))
    core_sum = gate(core_sum, grad_first_work)
    group_sum = reduce_groups(
        links, [core_sum[m * level_rows : (m + 1) * level_rows] for m in range(links.groups // 2)]
    )
    parts = gate(grad_first_work, core_sum).reshape(blocks, half_rows, width)
    back = tie(*[links.swap_level(parts[b], b) for b in (1, 2, 3)])
    near = (parts[0].astype(F32) + back[0].astype(F32)).astype(BF)
    far = (back[1].astype(F32) + back[2].astype(F32)).astype(BF)
    grad_first = workers_to_owner(links, near, far).astype(F32)
    source_own = inputs.astype(F32)
    inverse_one = lax.rsqrt(jnp.mean(source_own * source_own, axis=-1, keepdims=True) + EPSILON)
    normed_one = source_own * inverse_one
    grad_input = grad_middle + inverse_one * (
        grad_first - normed_one * jnp.mean(grad_first * normed_one, axis=-1, keepdims=True)
    )
    output = (middle + dot(to_tokens, taken_arrived)).astype(BF)

    sums = reduce_levels(links, gate(group_sum, *back))
    *grad_weights, grad_w_output, grad_w_router, grad_norm_one, grad_norm_two = finish(
        flags,
        [*sums, w_query, w_key, w_value, norm_one.reshape(1, own_rows)],
        experts,
    )
    return (
        output,
        grad_input,
        grad_norm_one.reshape(own_rows),
        grad_weights[0],
        grad_weights[1],
        grad_weights[2],
        grad_w_output,
        grad_norm_two.reshape(own_rows),
        grad_w_router,
        grad_weight_in[None],
        grad_weight_out[None],
    )


def solution(mesh):
    return jax.shard_map(
        on_device,
        mesh=mesh,
        in_specs=(
            P(AXES, None),
            P(AXES),
            P(AXES, None),
            P(AXES, None),
            P(AXES, None),
            P(AXES, None),
            P(AXES),
            P(AXES, None),
            P(AXES, None, None),
            P(AXES, None, None),
            P(AXES, None),
            P(AXES, None),
        ),
        out_specs=(
            P(AXES, None),
            P(AXES, None),
            P(AXES),
            P(AXES, None),
            P(AXES, None),
            P(AXES, None),
            P(AXES, None),
            P(AXES),
            P(AXES, None),
            P(AXES, None, None),
            P(AXES, None, None),
        ),
        check_vma=False,
    )
```

```python
import functools

import jax
import jax.numpy as jnp
from jax import lax
from jax.experimental import pallas as pl
from jax.experimental.pallas import tpu as pltpu
from jax.sharding import PartitionSpec as P

HEAD_DIM = 64
AXES = ("group", "local")
BF = jnp.bfloat16
F32 = jnp.float32
EPSILON = 1e-06
VMEM_BYTES = 58 * 2**20
SMALL_BYTES = 24 * 2**20


def dot(left, right):
    return jnp.dot(left, right, preferred_element_type=F32)


def dot_tn(left, right):
    return lax.dot_general(left, right, (((0,), (0,)), ((), ())), preferred_element_type=F32)


def dot_nt(left, right):
    return lax.dot_general(left, right, (((1,), (1,)), ((), ())), preferred_element_type=F32)


class Links:
    def __init__(self):
        self.groups = lax.axis_size("group")
        self.levels = lax.axis_size("local")
        self.group = lax.axis_index("group")
        self.level = lax.axis_index("local")
        self.core = self.group % 2

    def permute(self, array, target):
        pairs = []
        for group in range(self.groups):
            for level in range(self.levels):
                other_group, other_level = target(group, level)
                pairs.append((group * self.levels + level, other_group * self.levels + other_level))
        return lax.ppermute(array, AXES, pairs)

    def swap_core(self, array):
        return self.permute(array, lambda g, l: (g ^ 1, l))

    def swap_level(self, array, mask):
        return self.permute(array, lambda g, l: (g, l ^ mask))

    def swap_group(self, array, mask):
        return self.permute(array, lambda g, l: (g ^ (2 * mask), l))


def gate(array, *after):
    return lax.optimization_barrier((array, *after))[0]


def tie(*arrays):
    return lax.optimization_barrier(arrays)


def pick(flag, first, second):
    return jnp.where(flag == 0, first, second)


def joined(flag, mine, other, axis=0):
    return jnp.concatenate([pick(flag, mine, other), pick(flag, other, mine)], axis=axis)


def ordered(index, parts):
    count = len(parts)
    if count == 1:
        return parts[0]
    top = count.bit_length() - 2
    half = count // 2
    low = index & (half - 1)
    return joined((index >> top) & 1, ordered(low, parts[:half]), ordered(low, parts[half:]))


def rows_of(array, index, rows):
    return lax.dynamic_slice_in_dim(array, index * rows, rows, axis=0)


def gather_levels(links, pieces):
    got = tie(*[links.swap_level(pieces[b], b) for b in range(1, links.levels)])
    return ordered(links.level, [pieces[0], *got])


def gather_groups(links, block):
    return [block] + [links.swap_group(block, m) for m in range(1, links.groups // 2)]


def in_order(links, own, other):
    pairs = [joined(links.core, mine, far) for mine, far in zip(own, other)]
    return ordered(links.group >> 1, pairs)


def reduce_cores(links, keep, send):
    return keep + links.swap_core(send).astype(F32)


def reduce_groups(links, parts):
    got = [links.swap_group(parts[m].astype(BF), m) for m in range(1, len(parts))]
    total = parts[0]
    for part in tie(*got):
        total = total + part.astype(F32)
    return total


def reduce_levels(links, block, before_last):
    rows = block.shape[0] // links.levels
    parts = [rows_of(block, links.level ^ b, rows) for b in range(links.levels)]
    sent = [part.astype(BF) for part in parts[1:]]
    sent[-1] = gate(sent[-1], before_last)
    got = tie(*[links.swap_level(part, b + 1) for b, part in enumerate(sent)])
    return [parts[0], *got]


def owner_to_workers(links, array):
    half = array.shape[0] // 2
    mine = pick(links.core, array[:half], array[half:])
    other = links.swap_core(pick(links.core, array[half:], array[:half]))
    same = (links.level >> 1) ^ links.core
    return pick(same, mine, other), pick(same, other, mine)


def workers_to_owner(links, near, far):
    same = (links.level >> 1) ^ links.core
    mine = pick(same, near, far)
    other = links.swap_core(pick(same, far, near))
    return joined(links.core, mine, other)


PAIR = 2 * HEAD_DIM


def head_masks(dtype):
    lanes = lax.broadcasted_iota(jnp.int32, (1, PAIR), 1)
    return [(lanes // HEAD_DIM == head).astype(dtype) for head in range(2)]


CHUNK = 128


def forward_kernel(query_ref, key_ref, value_ref, key_far_ref, value_far_ref, *refs):
    mixed_refs, weights_ref, inverse_ref = refs[:-2], refs[-2], refs[-1]
    query = query_ref[...] * BF(HEAD_DIM**-0.5)
    key = jnp.concatenate([key_ref[...], key_far_ref[...]], axis=0)
    value = jnp.concatenate([value_ref[...], value_far_ref[...]], axis=0)
    value = jnp.concatenate([value, jnp.ones_like(value)], axis=1)
    first_head = lax.broadcasted_iota(jnp.int32, (1, PAIR), 1) < HEAD_DIM
    for part, mixed_ref in enumerate(mixed_refs):
        rows = slice(part * CHUNK, (part + 1) * CHUNK)
        sums = []
        for head, mask in enumerate(head_masks(BF)):
            scores = dot_nt(query[rows] * mask, key)
            weights = jnp.exp(scores - jnp.max(scores, axis=1, keepdims=True)).astype(BF)
            weights_ref[head, rows] = weights
            sums.append(dot(weights, value))
        mixed = jnp.where(first_head, sums[0][:, :PAIR], sums[1][:, :PAIR])
        inverse = 1.0 / jnp.where(first_head, sums[0][:, PAIR:], sums[1][:, PAIR:])
        inverse_ref[rows] = inverse
        mixed_ref[...] = (mixed * inverse).astype(BF)


def pair_column(rows, block=0):
    return pl.BlockSpec((rows, PAIR), lambda i: (0, block + i))


def weights_block(rows):
    return pl.BlockSpec((2, rows, 2 * rows), lambda i: (i, 0, 0))


def attention_forward(queries, pair, pair_far):
    rows, half_width = queries.shape
    pairs = half_width // PAIR
    return pl.pallas_call(
        forward_kernel,
        grid=(pairs,),
        in_specs=[pair_column(rows)] + [pair_column(rows), pair_column(rows, pairs)] * 2,
        out_specs=[pair_column(CHUNK)] * (rows // CHUNK) + [weights_block(rows), pair_column(rows)],
        out_shape=[low_shape(CHUNK, half_width)] * (rows // CHUNK)
        + [low_shape(2 * pairs, rows, 2 * rows), wide_shape(rows, half_width)],
        compiler_params=params(),
        cost_estimate=cost(2 * 10**9, 4096),
    )(queries, pair, pair, pair_far, pair_far)


def backward_kernel(
    query_ref, key_ref, value_ref, key_far_ref, value_far_ref, weights_ref, inverse_ref, *refs
):
    grad_refs, mixed_refs = refs[:4], refs[4:8]
    grad_query_ref, grad_near_ref, grad_far_ref = refs[8:]
    all_rows = query_ref.shape[0]
    factor = BF(HEAD_DIM**-0.5)
    query = query_ref[...] * factor
    key = jnp.concatenate([key_ref[...], key_far_ref[...]], axis=0)
    value = jnp.concatenate([value_ref[...], value_far_ref[...]], axis=0)
    grad = jnp.concatenate([ref[...] for ref in grad_refs], axis=0).astype(F32)
    grad = grad * inverse_ref[...]
    mixed = jnp.concatenate([ref[...] for ref in mixed_refs], axis=0)
    together = grad * mixed.astype(F32)
    grad = grad.astype(BF)
    grad_key = jnp.zeros((PAIR, 2 * all_rows), F32)
    grad_value = jnp.zeros((PAIR, 2 * all_rows), F32)
    for part in range(all_rows // (2 * CHUNK)):
        rows = slice(part * 2 * CHUNK, (part + 1) * 2 * CHUNK)
        grad_query = jnp.zeros((2 * CHUNK, PAIR), F32)
        for head, (mask, mask_wide) in enumerate(zip(head_masks(BF), head_masks(F32))):
            weights = weights_ref[head, rows]
            grad_one = grad[rows] * mask
            row_dots = jnp.sum(together[rows] * mask_wide, axis=1, keepdims=True)
            grad_weights = dot_nt(grad_one, value)
            grad_scores = (weights.astype(F32) * (grad_weights - row_dots)).astype(BF)
            grad_value = grad_value + dot_tn(grad_one, weights)
            grad_key = grad_key + dot_tn(query[rows] * mask, grad_scores)
            grad_query = grad_query + dot(grad_scores, key * (mask * factor))
        grad_query_ref[rows] = grad_query.astype(BF)
    for index, total in enumerate((grad_key, grad_value)):
        total = total.T
        grad_near_ref[index] = total[:all_rows].astype(BF)
        grad_far_ref[index] = total[all_rows:].astype(BF)


def attention_backward(queries, pair, pair_far, weights, inverse, grads, mixed):
    rows, half_width = queries.shape
    pairs = half_width // PAIR
    return pl.pallas_call(
        backward_kernel,
        grid=(pairs,),
        in_specs=[pair_column(rows)]
        + [pair_column(rows), pair_column(rows, pairs)] * 2
        + [weights_block(rows), pair_column(rows)]
        + [pair_column(rows // 4)] * 8,
        out_specs=[pair_column(rows)] + [pl.BlockSpec((2, rows, PAIR), lambda i: (0, 0, i))] * 2,
        out_shape=[low_shape(rows, half_width)] + [low_shape(2, rows, half_width)] * 2,
        compiler_params=params(),
        cost_estimate=cost(2 * 10**10, 4096),
    )(queries, pair, pair, pair_far, pair_far, weights, inverse, *grads, *mixed)


GELU_SCALE = 0.7978845608028654
GELU_CUBE = 0.044715


def gelu_and_slope(values):
    square = values * values
    bend = jnp.tanh(GELU_SCALE * values * (1.0 + GELU_CUBE * square))
    half = 0.5 + 0.5 * bend
    slope = half + 0.5 * values * (1.0 - bend * bend) * GELU_SCALE * (1.0 + 3 * GELU_CUBE * square)
    return values * half, slope


def whole(shape):
    return pl.BlockSpec(shape, lambda *_: (0,) * len(shape))


FLAGS = pl.BlockSpec(memory_space=pltpu.SMEM)
CORE, HALF, SAME, DEVICE, PLACE = range(5)


def params(size=VMEM_BYTES):
    return pltpu.CompilerParams(vmem_limit_bytes=size)


def cost(flops, size):
    return pl.CostEstimate(flops=flops, bytes_accessed=size, transcendentals=0)


def one_step(kernel, flags, operands, shapes, scratch=(), size=VMEM_BYTES):
    return pl.pallas_call(
        kernel,
        grid=(1,),
        in_specs=[FLAGS] + [whole(operand.shape) for operand in operands],
        out_specs=[whole(shape.shape) for shape in shapes],
        out_shape=shapes,
        scratch_shapes=list(scratch),
        compiler_params=params(size),
        cost_estimate=cost(0, 2**20),
    )(flags, *operands)


def low_shape(*shape):
    return jax.ShapeDtypeStruct(shape, BF)


def wide_shape(*shape):
    return jax.ShapeDtypeStruct(shape, F32)


def each_case(flags_ref, body):
    for half in range(2):
        for same in range(2):

            @pl.when((flags_ref[HALF] == half) & (flags_ref[SAME] == same))
            def _(half=half, same=same):
                body(half, same)


def turned_column(row):
    count = row.shape[1]
    rows = lax.broadcasted_iota(jnp.int32, (count, count), 0)
    lanes = lax.broadcasted_iota(jnp.int32, (count, count), 1)
    return jnp.sum(jnp.where(rows == lanes, row, 0.0), axis=1, keepdims=True)


def turned_row(column):
    count = column.shape[0]
    rows = lax.broadcasted_iota(jnp.int32, (count, count), 0)
    lanes = lax.broadcasted_iota(jnp.int32, (count, count), 1)
    return jnp.sum(jnp.where(rows == lanes, column, 0.0), axis=0, keepdims=True)


def pack_kernel(
    flags_ref,
    query_ref,
    key_ref,
    value_ref,
    output_ref,
    router_ref,
    routes_ref,
    norm_one_ref,
    norm_two_ref,
    kept_ref,
    cross_ref,
):
    own_rows, width = query_ref.shape
    experts = router_ref.shape[1]
    half_width = width // 2
    start = 3 * half_width
    tail = kept_ref.shape[1] - start - width
    scale = turned_column(norm_one_ref[...].astype(F32))
    first_half = flags_ref[HALF] == 0
    for index, ref in enumerate((query_ref, key_ref, value_ref)):
        scaled = (ref[...].astype(F32) * scale).astype(BF)
        low, high = scaled[:, :half_width], scaled[:, half_width:]
        columns = slice(index * half_width, (index + 1) * half_width)
        kept_ref[:, columns] = jnp.where(first_half, low, high)
        cross_ref[:, columns] = jnp.where(first_half, high, low)
    lanes = lax.broadcasted_iota(jnp.int32, (1, tail), 1)
    index = lax.broadcasted_iota(jnp.int32, (tail, 1), 0) - experts
    tally = jnp.sum((routes_ref[...] == index).astype(F32), axis=1, keepdims=True)
    tally = turned_row(tally)
    router = router_ref[...].astype(F32)
    router = jnp.concatenate([router, jnp.zeros((own_rows, tail - experts), F32)], axis=1)
    gain = turned_column(norm_two_ref[...].astype(F32))
    small = jnp.where(lanes < experts, router, jnp.where(lanes == 2 * experts, gain, tally))
    for ref in (kept_ref, cross_ref):
        ref[:, start : start + width] = output_ref[...]
        ref[:, start + width :] = small.astype(BF)


def pack(flags, operands):
    own_rows, width = operands[0].shape
    experts = operands[4].shape[1]
    tail = 2 * experts + 1
    columns = 3 * width // 2 + width + tail + -tail % 128
    return one_step(pack_kernel, flags, operands, [low_shape(own_rows, columns)] * 2)


def finish_kernel(
    flags_ref,
    zero_ref,
    one_ref,
    two_ref,
    three_ref,
    query_ref,
    key_ref,
    value_ref,
    norm_one_ref,
    grad_query_ref,
    grad_key_ref,
    grad_value_ref,
    grad_output_ref,
    grad_router_ref,
    grad_one_ref,
    grad_two_ref,
):
    width = query_ref.shape[1]
    experts = grad_router_ref.shape[1]
    half_width = width // 2
    start = 3 * half_width
    near = zero_ref[...] + two_ref[...].astype(F32)
    far = one_ref[...].astype(F32) + three_ref[...].astype(F32)
    scale = turned_column(norm_one_ref[...].astype(F32))
    first_half = flags_ref[HALF] == 0
    total = jnp.zeros_like(scale)
    pairs = ((query_ref, grad_query_ref), (key_ref, grad_key_ref), (value_ref, grad_value_ref))
    for index, (ref, grad_ref) in enumerate(pairs):
        columns = slice(index * half_width, (index + 1) * half_width)
        low = jnp.where(first_half, near[:, columns], far[:, columns])
        high = jnp.where(first_half, far[:, columns], near[:, columns])
        weight = ref[...].astype(F32)
        total = total + jnp.sum(weight[:, :half_width] * low, axis=1, keepdims=True)
        total = total + jnp.sum(weight[:, half_width:] * high, axis=1, keepdims=True)
        grad_ref[:, :half_width] = low * scale
        grad_ref[:, half_width:] = high * scale
    grad_one_ref[...] = turned_row(total)
    both = near[:, start:] + far[:, start:]
    grad_output_ref[...] = both[:, :width]
    small = both[:, width:]
    grad_router_ref[...] = small[:, :experts]
    lanes = lax.broadcasted_iota(jnp.int32, (1, small.shape[1]), 1)
    gain = jnp.sum(jnp.where(lanes == experts, small, 0.0), axis=1, keepdims=True)
    grad_two_ref[...] = turned_row(gain)


def finish(flags, operands, experts):
    own_rows, width = operands[4].shape
    shapes = [wide_shape(own_rows, width)] * 4
    shapes += [wide_shape(own_rows, experts)] + [wide_shape(1, own_rows)] * 2
    return one_step(finish_kernel, flags, operands, shapes, size=SMALL_BYTES)


def project_kernel(count, flags_ref, normed_ref, *refs):
    own_refs, other_refs = refs[:count], refs[count : 2 * count]
    query_ref, pair_ref, weight_ref = refs[2 * count :]
    rows = own_refs[0].shape[0]
    core = flags_ref[CORE]
    for m in range(count):
        place = 2 * (flags_ref[PLACE] ^ m)
        for index, ref in ((place + core, own_refs[m]), (place + 1 - core, other_refs[m])):
            place_rows = pl.ds(pl.multiple_of(index * rows, 16), rows)
            weight_ref[place_rows, :] = ref[...]
    projected = dot(normed_ref[...], weight_ref[...]).astype(BF)
    query_ref[...] = projected[:, : query_ref.shape[1]]
    pair_ref[...] = projected[:, query_ref.shape[1] :]


def project(flags, normed, own, other):
    count = len(own)
    rows, width = normed.shape
    columns = 3 * width // 2
    shapes = [
        low_shape(rows, width // 2),
        low_shape(rows, width),
        low_shape(width, columns),
    ]
    kernel = functools.partial(project_kernel, count)
    return one_step(kernel, flags, [normed, *own, *other], shapes)


def assemble_kernel(lane, flags_ref, *refs):
    *own_refs, other_ref, full_ref, row_ref = refs
    rows = own_refs[0].shape[0]
    width = full_ref.shape[0]
    core = flags_ref[CORE]
    for m, own_ref in enumerate(own_refs):
        place = 2 * (flags_ref[PLACE] ^ m)
        full_ref[pl.ds(pl.multiple_of((place + core) * rows, 16), rows), :] = own_ref[...]
        full_ref[pl.ds(pl.multiple_of((place + 1 - core) * rows, 16), rows), :] = other_ref[
            m * rows : (m + 1) * rows, :
        ]
    start = width + lane // 128 * 128
    block = full_ref[:, start : start + 128].astype(F32).T
    row_ref[...] = block[lane % 128 : lane % 128 + 1]


def assemble(flags, operands, lane):
    columns = operands[0].shape[1]
    width = 2 * operands[-1].shape[0]
    shapes = [low_shape(width, columns), wide_shape(1, width)]
    return one_step(functools.partial(assemble_kernel, lane), flags, operands, shapes)


def mixed_route_kernel(flags_ref, zero_ref, one_ref, two_ref, three_ref, mine_ref, sent_ref):
    half_width = zero_ref.shape[1]

    def body(half, same):
        near_ref, far_ref = (mine_ref, sent_ref) if same == 0 else (sent_ref, mine_ref)
        for into_ref, refs in ((near_ref, (zero_ref, one_ref)), (far_ref, (two_ref, three_ref))):
            into_ref[:, :half_width] = refs[half][...]
            into_ref[:, half_width:] = refs[1 - half][...]

    each_case(flags_ref, body)


def mixed_route(flags, parts):
    rows, half_width = parts[0].shape
    shapes = [low_shape(rows, 2 * half_width)] * 2
    return one_step(mixed_route_kernel, flags, parts, shapes, size=SMALL_BYTES)


def grad_route_kernel(flags_ref, mine_ref, got_ref, zero_ref, one_ref, two_ref, three_ref):
    half_width = zero_ref.shape[1]

    def body(half, same):
        near_ref, far_ref = (mine_ref, got_ref) if same == 0 else (got_ref, mine_ref)
        for from_ref, refs in ((near_ref, (zero_ref, one_ref)), (far_ref, (two_ref, three_ref))):
            refs[half][...] = from_ref[:, :half_width]
            refs[1 - half][...] = from_ref[:, half_width:]

    each_case(flags_ref, body)


def grad_route(flags, mine, got):
    rows, width = mine.shape
    shapes = [low_shape(rows, width // 2)] * 4
    return one_step(grad_route_kernel, flags, [mine, got], shapes, size=SMALL_BYTES)


def owner_forward_kernel(
    flags_ref,
    mine_ref,
    got_ref,
    inputs_ref,
    weight_ref,
    gain_ref,
    to_slots_ref,
    mixed_ref,
    middle_ref,
    slots_ref,
):
    half_rows = mine_ref.shape[0]
    for core in range(2):

        @pl.when(flags_ref[CORE] == core)
        def _(core=core):
            refs = (mine_ref, got_ref)
            mixed_ref[:half_rows] = refs[core][...]
            mixed_ref[half_rows:] = refs[1 - core][...]

    weight = weight_ref[:, : mixed_ref.shape[1]]
    middle = inputs_ref[...].astype(F32) + dot(mixed_ref[...], weight)
    middle_ref[...] = middle
    inverse = lax.rsqrt(jnp.mean(middle * middle, axis=1, keepdims=True) + EPSILON)
    second_low = (middle * inverse * gain_ref[...]).astype(BF)
    slots_ref[...] = dot(to_slots_ref[...], second_low).astype(BF)


def owner_forward(flags, mine, got, inputs, full_extra, gain, to_slots):
    rows, width = inputs.shape
    shapes = [
        low_shape(rows, width),
        wide_shape(rows, width),
        low_shape(to_slots.shape[0], width),
    ]
    operands = [mine, got, inputs, full_extra, gain, to_slots]
    return one_step(owner_forward_kernel, flags, operands, shapes)


TILE = 1024


def cotangent_kernel(cot_ref, compact_ref, weight_out_ref, held_ref, back_ref):
    @pl.when(pl.program_id(0) == 0)
    def _():
        held_ref[...] = dot(compact_ref[...], cot_ref[...]).astype(BF)

    back_ref[...] = dot_nt(held_ref[...], weight_out_ref[0]).astype(BF)


def cotangent_layer(cot, compact, expert_out):
    slots, width = cot.shape
    capacity = compact.shape[0]
    hidden_width = expert_out.shape[1]
    return pl.pallas_call(
        cotangent_kernel,
        grid=(hidden_width // TILE,),
        in_specs=[
            whole((slots, width)),
            whole((capacity, slots)),
            pl.BlockSpec((1, TILE, width), lambda i: (0, i, 0)),
        ],
        out_specs=[whole((capacity, width)), pl.BlockSpec((capacity, TILE), lambda i: (0, i))],
        out_shape=[low_shape(capacity, width), low_shape(capacity, hidden_width)],
        compiler_params=params(),
        cost_estimate=cost(2 * capacity * width * hidden_width, 4 * width * hidden_width),
    )(cot, compact, expert_out)


def expert_kernel(
    flags_ref,
    arrived_ref,
    cot_ref,
    back_ref,
    compact_ref,
    expand_ref,
    router_ref,
    weight_in_ref,
    held_ref,
    grad_result_ref,
    hidden_ref,
    grad_inner_ref,
    grad_back_ref,
    grad_logits_ref,
    gate_ref,
    grad_sum,
    probs,
    grad_gate,
):
    step = pl.program_id(0)
    experts = router_ref.shape[1]
    lanes = lax.broadcasted_iota(jnp.int32, (1, experts), 1)
    mine = (lanes == flags_ref[DEVICE]).astype(F32)

    @pl.when(step == 0)
    def _():
        held = dot(compact_ref[...], arrived_ref[...]).astype(BF)
        held_ref[...] = held
        logits = dot(held, router_ref[...])
        weights = jnp.exp(logits - jnp.max(logits, axis=1, keepdims=True))
        router_probs = weights / jnp.sum(weights, axis=1, keepdims=True)
        probs[...] = router_probs
        gate_rows = jnp.sum(router_probs * mine, axis=1, keepdims=True)
        gate_ref[...] = gate_rows
        grad_result_ref[...] = (gate_rows * cot_ref[...].astype(F32)).astype(BF)
        grad_sum[...] = jnp.zeros_like(grad_sum)
        grad_gate[...] = jnp.zeros_like(grad_gate)

    weight_in = weight_in_ref[0]
    hidden, slope = gelu_and_slope(dot(held_ref[...], weight_in))
    hidden = hidden.astype(BF)
    hidden_ref[...] = hidden
    back = back_ref[...].astype(F32)
    grad_inner = (back * (gate_ref[...] * slope)).astype(BF)
    grad_inner_ref[...] = grad_inner
    grad_gate[...] += jnp.sum(hidden.astype(F32) * back, axis=1, keepdims=True)
    grad_sum[...] += dot_nt(grad_inner, weight_in)

    @pl.when(step == pl.num_programs(0) - 1)
    def _():
        grad_logits = (grad_gate[...] * probs[...] * (mine - gate_ref[...])).astype(BF)
        grad_logits_ref[...] = grad_logits
        grad_held = grad_sum[...] + dot_nt(grad_logits, router_ref[...])
        grad_back_ref[...] = dot(expand_ref[...], grad_held.astype(BF)).astype(BF)


def expert_layer(flags, arrived, cot, back, compact, expand, router, expert_in):
    slots, width = arrived.shape
    capacity = compact.shape[0]
    hidden_width = expert_in.shape[2]
    experts = router.shape[1]
    wide = whole((capacity, width))
    tall = pl.BlockSpec((capacity, TILE), lambda i: (0, i))
    return pl.pallas_call(
        expert_kernel,
        grid=(hidden_width // TILE,),
        in_specs=[
            FLAGS,
            whole((slots, width)),
            wide,
            tall,
            whole((capacity, slots)),
            whole((slots, capacity)),
            whole((width, experts)),
            pl.BlockSpec((1, width, TILE), lambda i: (0, 0, i)),
        ],
        out_specs=[wide, wide, tall, tall, whole((slots, width))]
        + [whole((capacity, experts)), whole((capacity, 1))],
        out_shape=[
            low_shape(capacity, width),
            low_shape(capacity, width),
            low_shape(capacity, hidden_width),
            low_shape(capacity, hidden_width),
            low_shape(slots, width),
            low_shape(capacity, experts),
            wide_shape(capacity, 1),
        ],
        scratch_shapes=[
            pltpu.VMEM((capacity, width), F32),
            pltpu.VMEM((capacity, experts), F32),
            pltpu.VMEM((capacity, 1), F32),
        ],
        compiler_params=params(),
        cost_estimate=cost(8 * capacity * width * hidden_width, 8 * width * hidden_width),
    )(flags, arrived, cot, back, compact, expand, router, expert_in)


def owner_backward_kernel(
    flags_ref,
    returned_ref,
    to_tokens_ref,
    cotangent_ref,
    middle_ref,
    gain_ref,
    weight_ref,
    grad_middle_ref,
    grad_branch_ref,
    mine_ref,
    sent_ref,
    grad_gain_ref,
):
    half_rows = mine_ref.shape[0]
    middle = middle_ref[...]
    inverse = lax.rsqrt(jnp.mean(middle * middle, axis=1, keepdims=True) + EPSILON)
    normed = middle * inverse
    grad_second = dot(to_tokens_ref[...], returned_ref[...])
    grouped = (grad_second * normed).reshape(-1, GAIN_ROWS, grad_second.shape[1])
    grad_gain_ref[...] = jnp.sum(grouped, axis=0).astype(BF)
    scaled = grad_second * gain_ref[...]
    grad_middle = cotangent_ref[...].astype(F32) + inverse * (
        scaled - normed * jnp.mean(scaled * normed, axis=1, keepdims=True)
    )
    grad_middle_ref[...] = grad_middle
    grad_branch = grad_middle.astype(BF)
    grad_branch_ref[...] = grad_branch
    weight = weight_ref[:, : middle.shape[1]]
    grad_mixed = dot_nt(grad_branch, weight).astype(BF)
    for core in range(2):

        @pl.when(flags_ref[CORE] == core)
        def _(core=core):
            mine_ref[...] = grad_mixed[core * half_rows : (core + 1) * half_rows]
            sent_ref[...] = grad_mixed[(1 - core) * half_rows : (2 - core) * half_rows]


def owner_backward(flags, returned, to_tokens, cotangent, middle, gain, full_extra):
    rows, width = cotangent.shape
    shapes = [
        wide_shape(rows, width),
        low_shape(rows, width),
        low_shape(rows // 2, width),
        low_shape(rows // 2, width),
        low_shape(GAIN_ROWS, width),
    ]
    operands = [returned, to_tokens, cotangent, middle, gain, full_extra]
    return one_step(owner_backward_kernel, flags, operands, shapes)


GAIN_ROWS = 16


def deal_rows(flags_ref, total, keep_ref, send_ref, rows):
    core = flags_ref[CORE]
    for m in range(total.shape[0] // (2 * rows)):
        place = 2 * (flags_ref[PLACE] ^ m)
        keep_ref[m * rows : (m + 1) * rows, :] = total[
            pl.ds(pl.multiple_of((place + core) * rows, 8), rows), :
        ]
        send_ref[m * rows : (m + 1) * rows, :] = total[
            pl.ds(pl.multiple_of((place + 1 - core) * rows, 8), rows), :
        ].astype(BF)


def dealt(width, columns):
    return [wide_shape(width // 2, columns), low_shape(width // 2, columns)]


def weight_grads_kernel(
    rows,
    flags_ref,
    normed_ref,
    query_ref,
    near_ref,
    got_ref,
    mixed_ref,
    branch_ref,
    router_ref,
    gain_ref,
    projected_ref,
    keep_ref,
    send_ref,
    total,
):
    part = query_ref.shape[1]
    width, experts = router_ref.shape
    extra = total.shape[1] - 3 * part - width
    projected_ref[:, :part] = query_ref[...]
    for index in range(2):
        both = near_ref[index].astype(F32) + got_ref[index].astype(F32)
        projected_ref[:, (index + 1) * part : (index + 2) * part] = both.astype(BF)
    total[:, : 3 * part] = dot_tn(normed_ref[...], projected_ref[...])
    total[:, 3 * part : 3 * part + width] = dot_tn(mixed_ref[...], branch_ref[...])
    gain = dot_tn(gain_ref[...], jnp.ones((GAIN_ROWS, extra), BF))
    router = router_ref[...]
    router = jnp.concatenate([router, jnp.zeros((width, extra - experts), F32)], axis=1)
    lanes = lax.broadcasted_iota(jnp.int32, (1, extra), 1)
    total[:, 3 * part + width :] = jnp.where(lanes == experts, gain, router)
    deal_rows(flags_ref, total, keep_ref, send_ref, rows)


def weight_grads(flags, operands, rows):
    work_rows, width = operands[0].shape
    part = operands[1].shape[1]
    experts = operands[6].shape[1]
    columns = 3 * part + width + experts + 1
    columns += -columns % 128
    return one_step(
        functools.partial(weight_grads_kernel, rows),
        flags,
        operands,
        [low_shape(work_rows, 3 * part)] + dealt(width, columns),
        [pltpu.VMEM((width, columns), F32)],
        2 * SMALL_BYTES,
    )


def all_to_all(array):
    return lax.all_to_all(array, AXES, split_axis=0, concat_axis=0, tiled=True)


def on_device(
    inputs,
    norm_one,
    w_query,
    w_key,
    w_value,
    w_output,
    norm_two,
    w_router,
    expert_in,
    expert_out,
    routes,
    cotangent,
):
    links = Links()
    level, core = links.level, links.core
    device = links.group * links.levels + level
    devices = links.groups * links.levels
    rows, width = inputs.shape
    half_rows = rows // 2
    half_width = width // 2
    experts = w_router.shape[1]
    own_rows = norm_one.shape[0]
    most = 2 * rows // experts
    capacity = 5 * rows // 4
    blocks = links.levels

    same = (level >> 1) ^ core
    flags = jnp.stack([core, level & 1, same, device, links.group >> 1]).astype(jnp.int32)

    mine = pick(core, inputs[:half_rows], inputs[half_rows:])
    got = links.swap_core(pick(core, inputs[half_rows:], inputs[:half_rows]))
    kept, cross = pack(
        flags,
        [w_query, w_key, w_value, w_output, w_router, routes.reshape(1, rows)]
        + [norm_one.reshape(1, own_rows), norm_two.reshape(1, own_rows)],
    )
    level_block = gather_levels(links, [kept, cross, kept, cross])
    level_rows = level_block.shape[0]
    got = gate(got, kept, cross)
    near, far = pick(same, mine, got), pick(same, got, mine)
    near_first = links.swap_level(near, 1)
    far_first = links.swap_level(far, 2)
    far_second = links.swap_level(far_first, 1)
    level_weights = level_block[:, : 3 * half_width]
    own_blocks = gather_groups(links, level_weights)
    chosen = gate(routes, level_block)[:, 0]
    picked = (chosen[:, None] == jnp.arange(experts, dtype=jnp.int32)[None, :]).astype(jnp.int32)
    rank = jnp.sum((jnp.cumsum(picked, axis=0) - picked) * picked, axis=1)
    place = chosen * most + rank
    slot_index = jnp.arange(experts * most, dtype=jnp.int32)
    to_slots = (slot_index[:, None] == place[None, :]).astype(BF)
    to_tokens = (place[:, None] == slot_index[None, :]).astype(BF)
    cot_slots = dot(to_slots, cotangent).astype(BF).reshape(experts, most, width)

    own_blocks = tie(*own_blocks, near_first, far_first, cot_slots)[:-3]
    other_blocks = [links.swap_core(part) for part in own_blocks]

    source = jnp.concatenate([near, near_first, far_first, far_second], axis=0).astype(F32)
    normed_work = (
        source * lax.rsqrt(jnp.mean(source * source, axis=-1, keepdims=True) + EPSILON)
    ).astype(BF)
    own_extra = gather_groups(links, gate(level_block[:, 3 * half_width :], *own_blocks))
    if level_rows % 16 == 0:
        queries, pair, weights = project(flags, normed_work, own_blocks, other_blocks)
    else:
        weights = in_order(links, own_blocks, other_blocks)
        projected = dot(normed_work, weights).astype(BF)
        queries, pair = projected[:, :half_width], projected[:, half_width:]
    pair_far = links.swap_core(pair)
    cot_arrived = all_to_all(gate(cot_slots, *own_blocks)).reshape(-1, width)
    *mixed_parts, attention_weights, inverse = attention_forward(queries, pair, pair_far)
    mixed_parts = tie(*mixed_parts, cot_arrived, *own_extra)[:4]

    own_extra = tie(*own_extra, *mixed_parts)[: len(own_extra)]
    other_extra = links.swap_core(jnp.concatenate(own_extra, axis=0))
    if level_rows % 16 == 0:
        full_extra, gain_two = assemble(flags, [*own_extra, other_extra], 2 * experts)
    else:
        other_parts = [
            other_extra[m * level_rows : (m + 1) * level_rows] for m in range(len(own_extra))
        ]
        full_extra = in_order(links, own_extra, other_parts)
        gain_two = full_extra[:, width + 2 * experts].astype(F32)[None]
    full_router = full_extra[:, width : width + experts]
    last_part = gate(mixed_parts[3], gain_two)
    back = [links.swap_level(mixed_parts[1], 1), links.swap_level(mixed_parts[2], 2)]
    back = tie(*back, links.swap_level(last_part, 3))
    tallies = full_extra[::own_rows, width + experts : width + 2 * experts].astype(F32)
    mine_only = (jnp.arange(experts, dtype=jnp.int32) == device).astype(F32)[None, :]
    counts = jnp.sum(tallies * mine_only, axis=1).astype(jnp.int32)
    offsets = jnp.cumsum(counts) - counts
    within = jnp.arange(most, dtype=jnp.int32)[None, :]
    slot_grid = offsets[:, None] + within
    usable = (within < counts[:, None]) & (slot_grid < capacity)
    slot_flat = jnp.where(usable, slot_grid, -1).reshape(-1)
    held_index = jnp.arange(capacity, dtype=jnp.int32)
    compact = (held_index[:, None] == slot_flat[None, :]).astype(BF)
    expand = (slot_flat[:, None] == held_index[None, :]).astype(BF)

    mixed_mine, mixed_sent = mixed_route(flags, [mixed_parts[0], *back])
    mixed_low, middle, second_slots = owner_forward(
        flags, mixed_mine, links.swap_core(mixed_sent), inputs, full_extra, gain_two, to_slots
    )
    arrived = all_to_all(second_slots.reshape(experts, most, width)).reshape(-1, width)

    cot_held, cot_back = cotangent_layer(gate(cot_arrived, second_slots), compact, expert_out)
    held, grad_result, hidden, grad_inner, grad_back, grad_logits, gate_rows = expert_layer(
        flags,
        gate(arrived, cot_back),
        cot_held,
        cot_back,
        compact,
        expand,
        full_router,
        expert_in,
    )
    grad_returned = all_to_all(grad_back.reshape(experts, most, width)).reshape(-1, width)
    grad_router = dot_tn(held, grad_logits)
    grad_weight_out = dot_tn(hidden, grad_result)
    grad_weight_in = dot_tn(held, grad_inner)
    result = dot(hidden, expert_out[0]).astype(BF).astype(F32)
    taken_back = dot(expand, (gate_rows * result).astype(BF)).astype(BF)
    grad_returned = gate(
        grad_returned, grad_weight_in, grad_weight_out, grad_router, taken_back, to_tokens
    )

    grad_middle, grad_branch, grad_mine, grad_sent, gain_rows = owner_backward(
        flags, grad_returned, to_tokens, cotangent, middle, gain_two, full_extra
    )
    routed = grad_route(flags, grad_mine, links.swap_core(grad_sent))
    got = [links.swap_level(routed[b], b) for b in (1, 2, 3)]

    got = tie(*got)
    taken_back = gate(taken_back, *got).reshape(experts, most, width)
    taken_arrived = all_to_all(taken_back).reshape(-1, width)
    grad_queries, grad_near, grad_far = attention_backward(
        queries,
        pair,
        pair_far,
        attention_weights,
        inverse,
        [routed[0], *got],
        mixed_parts,
    )
    got_pair = links.swap_core(grad_far)
    grad_projected, keep, send = weight_grads(
        flags,
        [normed_work, grad_queries, grad_near, got_pair]
        + [mixed_low, grad_branch, grad_router, gain_rows],
        level_rows,
    )
    grad_first_work = dot_nt(grad_projected, weights).astype(BF)
    core_sum = reduce_cores(links, keep, gate(send, taken_arrived))
    core_sum = gate(core_sum, grad_first_work)
    group_sum = reduce_groups(
        links, [core_sum[m * level_rows : (m + 1) * level_rows] for m in range(links.groups // 2)]
    )
    parts = gate(grad_first_work, core_sum).reshape(blocks, half_rows, width)
    back = tie(*[links.swap_level(parts[b], b) for b in (1, 2, 3)])
    back = tie(*back, group_sum)[:-1]
    near = (parts[0].astype(F32) + back[0].astype(F32)).astype(BF)
    far = (back[1].astype(F32) + back[2].astype(F32)).astype(BF)
    grad_first = workers_to_owner(links, near, far).astype(F32)
    source_own = inputs.astype(F32)
    inverse_one = lax.rsqrt(jnp.mean(source_own * source_own, axis=-1, keepdims=True) + EPSILON)
    normed_one = source_own * inverse_one
    grad_input = grad_middle + inverse_one * (
        grad_first - normed_one * jnp.mean(grad_first * normed_one, axis=-1, keepdims=True)
    )
    output = (middle + dot(to_tokens, taken_arrived)).astype(BF)

    sums = reduce_levels(links, gate(group_sum, *back), grad_input)
    *grad_weights, grad_w_output, grad_w_router, grad_norm_one, grad_norm_two = finish(
        flags,
        [*sums, w_query, w_key, w_value, norm_one.reshape(1, own_rows)],
        experts,
    )
    return (
        output,
        grad_input,
        grad_norm_one.reshape(own_rows),
        grad_weights[0],
        grad_weights[1],
        grad_weights[2],
        grad_w_output,
        grad_norm_two.reshape(own_rows),
        grad_w_router,
        grad_weight_in[None],
        grad_weight_out[None],
    )


def solution(mesh):
    return jax.shard_map(
        on_device,
        mesh=mesh,
        in_specs=(
            P(AXES, None),
            P(AXES),
            P(AXES, None),
            P(AXES, None),
            P(AXES, None),
            P(AXES, None),
            P(AXES),
            P(AXES, None),
            P(AXES, None, None),
            P(AXES, None, None),
            P(AXES, None),
            P(AXES, None),
        ),
        out_specs=(
            P(AXES, None),
            P(AXES, None),
            P(AXES),
            P(AXES, None),
            P(AXES, None),
            P(AXES, None),
            P(AXES, None),
            P(AXES),
            P(AXES, None),
            P(AXES, None, None),
            P(AXES, None, None),
        ),
        check_vma=False,
    )
```

```python
import functools

import jax
import jax.numpy as jnp
from jax import lax
from jax.experimental import pallas as pl
from jax.experimental.pallas import tpu as pltpu
from jax.sharding import PartitionSpec as P

HEAD_DIM = 64
AXES = ("group", "local")
BF = jnp.bfloat16
F32 = jnp.float32
EPSILON = 1e-06
VMEM_BYTES = 58 * 2**20
SMALL_BYTES = 24 * 2**20


def dot(left, right):
    return jnp.dot(left, right, preferred_element_type=F32)


def dot_tn(left, right):
    return lax.dot_general(left, right, (((0,), (0,)), ((), ())), preferred_element_type=F32)


def dot_nt(left, right):
    return lax.dot_general(left, right, (((1,), (1,)), ((), ())), preferred_element_type=F32)


class Links:
    def __init__(self):
        self.groups = lax.axis_size("group")
        self.levels = lax.axis_size("local")
        self.group = lax.axis_index("group")
        self.level = lax.axis_index("local")
        self.core = self.group % 2

    def permute(self, array, target):
        pairs = []
        for group in range(self.groups):
            for level in range(self.levels):
                other_group, other_level = target(group, level)
                pairs.append((group * self.levels + level, other_group * self.levels + other_level))
        return lax.ppermute(array, AXES, pairs)

    def swap_core(self, array):
        return self.permute(array, lambda g, l: (g ^ 1, l))

    def swap_level(self, array, mask):
        return self.permute(array, lambda g, l: (g, l ^ mask))

    def swap_group(self, array, mask):
        return self.permute(array, lambda g, l: (g ^ (2 * mask), l))


def gate(array, *after):
    return lax.optimization_barrier((array, *after))[0]


def tie(*arrays):
    return lax.optimization_barrier(arrays)


def pick(flag, first, second):
    return jnp.where(flag == 0, first, second)


def joined(flag, mine, other, axis=0):
    return jnp.concatenate([pick(flag, mine, other), pick(flag, other, mine)], axis=axis)


def ordered(index, parts):
    count = len(parts)
    if count == 1:
        return parts[0]
    top = count.bit_length() - 2
    half = count // 2
    low = index & (half - 1)
    return joined((index >> top) & 1, ordered(low, parts[:half]), ordered(low, parts[half:]))


def rows_of(array, index, rows):
    return lax.dynamic_slice_in_dim(array, index * rows, rows, axis=0)


def gather_levels(links, pieces):
    got = tie(*[links.swap_level(pieces[b], b) for b in range(1, links.levels)])
    return ordered(links.level, [pieces[0], *got])


def gather_groups(links, block):
    return [block] + [links.swap_group(block, m) for m in range(1, links.groups // 2)]


def in_order(links, own, other):
    pairs = [joined(links.core, mine, far) for mine, far in zip(own, other)]
    return ordered(links.group >> 1, pairs)


def reduce_cores(links, keep, send):
    return keep + links.swap_core(send).astype(F32)


def reduce_groups(links, parts):
    got = [links.swap_group(parts[m].astype(BF), m) for m in range(1, len(parts))]
    total = parts[0]
    for part in tie(*got):
        total = total + part.astype(F32)
    return total


def reduce_levels(links, block, before_last):
    rows = block.shape[0] // links.levels
    parts = [rows_of(block, links.level ^ b, rows) for b in range(links.levels)]
    sent = [part.astype(BF) for part in parts[1:]]
    sent[0] = gate(sent[0], before_last)
    got = tie(*[links.swap_level(part, b + 1) for b, part in enumerate(sent)])
    return [parts[0], *got]


def owner_to_workers(links, array):
    half = array.shape[0] // 2
    mine = pick(links.core, array[:half], array[half:])
    other = links.swap_core(pick(links.core, array[half:], array[:half]))
    same = (links.level >> 1) ^ links.core
    return pick(same, mine, other), pick(same, other, mine)


def workers_to_owner(links, near, far):
    same = (links.level >> 1) ^ links.core
    mine = pick(same, near, far)
    other = links.swap_core(pick(same, far, near))
    return joined(links.core, mine, other)


PAIR = 2 * HEAD_DIM


def head_masks(dtype):
    lanes = lax.broadcasted_iota(jnp.int32, (1, PAIR), 1)
    return [(lanes // HEAD_DIM == head).astype(dtype) for head in range(2)]


CHUNK = 128


def forward_kernel(query_ref, key_ref, value_ref, key_far_ref, value_far_ref, *refs):
    mixed_refs, weights_ref, inverse_ref = refs[:-2], refs[-2], refs[-1]
    query = query_ref[...] * BF(HEAD_DIM**-0.5)
    key = jnp.concatenate([key_ref[...], key_far_ref[...]], axis=0)
    value = jnp.concatenate([value_ref[...], value_far_ref[...]], axis=0)
    value = jnp.concatenate([value, jnp.ones_like(value)], axis=1)
    first_head = lax.broadcasted_iota(jnp.int32, (1, PAIR), 1) < HEAD_DIM
    for part, mixed_ref in enumerate(mixed_refs):
        rows = slice(part * CHUNK, (part + 1) * CHUNK)
        sums = []
        for head, mask in enumerate(head_masks(BF)):
            scores = dot_nt(query[rows] * mask, key)
            weights = jnp.exp(scores - jnp.max(scores, axis=1, keepdims=True)).astype(BF)
            weights_ref[head, rows] = weights
            sums.append(dot(weights, value))
        mixed = jnp.where(first_head, sums[0][:, :PAIR], sums[1][:, :PAIR])
        inverse = 1.0 / jnp.where(first_head, sums[0][:, PAIR:], sums[1][:, PAIR:])
        inverse_ref[rows] = inverse
        mixed_ref[...] = (mixed * inverse).astype(BF)


def pair_column(rows, block=0):
    return pl.BlockSpec((rows, PAIR), lambda i: (0, block + i))


def weights_block(rows):
    return pl.BlockSpec((2, rows, 2 * rows), lambda i: (i, 0, 0))


def attention_forward(queries, pair, pair_far):
    rows, half_width = queries.shape
    pairs = half_width // PAIR
    return pl.pallas_call(
        forward_kernel,
        grid=(pairs,),
        in_specs=[pair_column(rows)] + [pair_column(rows), pair_column(rows, pairs)] * 2,
        out_specs=[pair_column(CHUNK)] * (rows // CHUNK) + [weights_block(rows), pair_column(rows)],
        out_shape=[low_shape(CHUNK, half_width)] * (rows // CHUNK)
        + [low_shape(2 * pairs, rows, 2 * rows), wide_shape(rows, half_width)],
        compiler_params=params(),
        cost_estimate=cost(2 * 10**9, 4096),
    )(queries, pair, pair, pair_far, pair_far)


def backward_kernel(
    query_ref, key_ref, value_ref, key_far_ref, value_far_ref, weights_ref, inverse_ref, *refs
):
    grad_refs, mixed_refs = refs[:4], refs[4:8]
    grad_query_ref, grad_near_ref, grad_far_ref = refs[8:]
    all_rows = query_ref.shape[0]
    factor = BF(HEAD_DIM**-0.5)
    query = query_ref[...] * factor
    key = jnp.concatenate([key_ref[...], key_far_ref[...]], axis=0)
    value = jnp.concatenate([value_ref[...], value_far_ref[...]], axis=0)
    grad = jnp.concatenate([ref[...] for ref in grad_refs], axis=0).astype(F32)
    grad = grad * inverse_ref[...]
    mixed = jnp.concatenate([ref[...] for ref in mixed_refs], axis=0)
    together = grad * mixed.astype(F32)
    grad = grad.astype(BF)
    grad_key = jnp.zeros((PAIR, 2 * all_rows), F32)
    grad_value = jnp.zeros((PAIR, 2 * all_rows), F32)
    for part in range(all_rows // (2 * CHUNK)):
        rows = slice(part * 2 * CHUNK, (part + 1) * 2 * CHUNK)
        grad_query = jnp.zeros((2 * CHUNK, PAIR), F32)
        for head, (mask, mask_wide) in enumerate(zip(head_masks(BF), head_masks(F32))):
            weights = weights_ref[head, rows]
            grad_one = grad[rows] * mask
            row_dots = jnp.sum(together[rows] * mask_wide, axis=1, keepdims=True)
            grad_weights = dot_nt(grad_one, value)
            grad_scores = (weights.astype(F32) * (grad_weights - row_dots)).astype(BF)
            grad_value = grad_value + dot_tn(grad_one, weights)
            grad_key = grad_key + dot_tn(query[rows] * mask, grad_scores)
            grad_query = grad_query + dot(grad_scores, key * (mask * factor))
        grad_query_ref[rows] = grad_query.astype(BF)
    for index, total in enumerate((grad_key, grad_value)):
        total = total.T
        grad_near_ref[index] = total[:all_rows].astype(BF)
        grad_far_ref[index] = total[all_rows:].astype(BF)


def attention_backward(queries, pair, pair_far, weights, inverse, grads, mixed):
    rows, half_width = queries.shape
    pairs = half_width // PAIR
    return pl.pallas_call(
        backward_kernel,
        grid=(pairs,),
        in_specs=[pair_column(rows)]
        + [pair_column(rows), pair_column(rows, pairs)] * 2
        + [weights_block(rows), pair_column(rows)]
        + [pair_column(rows // 4)] * 8,
        out_specs=[pair_column(rows)] + [pl.BlockSpec((2, rows, PAIR), lambda i: (0, 0, i))] * 2,
        out_shape=[low_shape(rows, half_width)] + [low_shape(2, rows, half_width)] * 2,
        compiler_params=params(),
        cost_estimate=cost(2 * 10**10, 4096),
    )(queries, pair, pair, pair_far, pair_far, weights, inverse, *grads, *mixed)


GELU_SCALE = 0.7978845608028654
GELU_CUBE = 0.044715


def gelu_and_slope(values):
    square = values * values
    bend = jnp.tanh(GELU_SCALE * values * (1.0 + GELU_CUBE * square))
    half = 0.5 + 0.5 * bend
    slope = half + 0.5 * values * (1.0 - bend * bend) * GELU_SCALE * (1.0 + 3 * GELU_CUBE * square)
    return values * half, slope


def whole(shape):
    return pl.BlockSpec(shape, lambda *_: (0,) * len(shape))


FLAGS = pl.BlockSpec(memory_space=pltpu.SMEM)
CORE, HALF, SAME, DEVICE, PLACE = range(5)


def params(size=VMEM_BYTES):
    return pltpu.CompilerParams(vmem_limit_bytes=size)


def cost(flops, size):
    return pl.CostEstimate(flops=flops, bytes_accessed=size, transcendentals=0)


def one_step(kernel, flags, operands, shapes, scratch=(), size=VMEM_BYTES):
    return pl.pallas_call(
        kernel,
        grid=(1,),
        in_specs=[FLAGS] + [whole(operand.shape) for operand in operands],
        out_specs=[whole(shape.shape) for shape in shapes],
        out_shape=shapes,
        scratch_shapes=list(scratch),
        compiler_params=params(size),
        cost_estimate=cost(0, 2**20),
    )(flags, *operands)


def low_shape(*shape):
    return jax.ShapeDtypeStruct(shape, BF)


def wide_shape(*shape):
    return jax.ShapeDtypeStruct(shape, F32)


def each_case(flags_ref, body):
    for half in range(2):
        for same in range(2):

            @pl.when((flags_ref[HALF] == half) & (flags_ref[SAME] == same))
            def _(half=half, same=same):
                body(half, same)


def turned_column(row):
    count = row.shape[1]
    rows = lax.broadcasted_iota(jnp.int32, (count, count), 0)
    lanes = lax.broadcasted_iota(jnp.int32, (count, count), 1)
    return jnp.sum(jnp.where(rows == lanes, row, 0.0), axis=1, keepdims=True)


def turned_row(column):
    count = column.shape[0]
    rows = lax.broadcasted_iota(jnp.int32, (count, count), 0)
    lanes = lax.broadcasted_iota(jnp.int32, (count, count), 1)
    return jnp.sum(jnp.where(rows == lanes, column, 0.0), axis=0, keepdims=True)


def pack_kernel(
    flags_ref,
    query_ref,
    key_ref,
    value_ref,
    output_ref,
    router_ref,
    routes_ref,
    norm_one_ref,
    norm_two_ref,
    kept_ref,
    cross_ref,
):
    own_rows, width = query_ref.shape
    experts = router_ref.shape[1]
    half_width = width // 2
    start = 3 * half_width
    tail = kept_ref.shape[1] - start - width
    scale = turned_column(norm_one_ref[...].astype(F32))
    first_half = flags_ref[HALF] == 0
    for index, ref in enumerate((query_ref, key_ref, value_ref)):
        scaled = (ref[...].astype(F32) * scale).astype(BF)
        low, high = scaled[:, :half_width], scaled[:, half_width:]
        columns = slice(index * half_width, (index + 1) * half_width)
        kept_ref[:, columns] = jnp.where(first_half, low, high)
        cross_ref[:, columns] = jnp.where(first_half, high, low)
    lanes = lax.broadcasted_iota(jnp.int32, (1, tail), 1)
    index = lax.broadcasted_iota(jnp.int32, (tail, 1), 0) - experts
    tally = jnp.sum((routes_ref[...] == index).astype(F32), axis=1, keepdims=True)
    tally = turned_row(tally)
    router = router_ref[...].astype(F32)
    router = jnp.concatenate([router, jnp.zeros((own_rows, tail - experts), F32)], axis=1)
    gain = turned_column(norm_two_ref[...].astype(F32))
    small = jnp.where(lanes < experts, router, jnp.where(lanes == 2 * experts, gain, tally))
    for ref in (kept_ref, cross_ref):
        ref[:, start : start + width] = output_ref[...]
        ref[:, start + width :] = small.astype(BF)


def pack(flags, operands):
    own_rows, width = operands[0].shape
    experts = operands[4].shape[1]
    tail = 2 * experts + 1
    columns = 3 * width // 2 + width + tail + -tail % 128
    return one_step(pack_kernel, flags, operands, [low_shape(own_rows, columns)] * 2)


def finish_kernel(
    flags_ref,
    zero_ref,
    one_ref,
    two_ref,
    three_ref,
    query_ref,
    key_ref,
    value_ref,
    norm_one_ref,
    grad_query_ref,
    grad_key_ref,
    grad_value_ref,
    grad_output_ref,
    grad_router_ref,
    grad_one_ref,
    grad_two_ref,
):
    width = query_ref.shape[1]
    experts = grad_router_ref.shape[1]
    half_width = width // 2
    start = 3 * half_width
    near = zero_ref[...] + two_ref[...].astype(F32)
    far = one_ref[...].astype(F32) + three_ref[...].astype(F32)
    scale = turned_column(norm_one_ref[...].astype(F32))
    first_half = flags_ref[HALF] == 0
    total = jnp.zeros_like(scale)
    pairs = ((query_ref, grad_query_ref), (key_ref, grad_key_ref), (value_ref, grad_value_ref))
    for index, (ref, grad_ref) in enumerate(pairs):
        columns = slice(index * half_width, (index + 1) * half_width)
        low = jnp.where(first_half, near[:, columns], far[:, columns])
        high = jnp.where(first_half, far[:, columns], near[:, columns])
        weight = ref[...].astype(F32)
        total = total + jnp.sum(weight[:, :half_width] * low, axis=1, keepdims=True)
        total = total + jnp.sum(weight[:, half_width:] * high, axis=1, keepdims=True)
        grad_ref[:, :half_width] = low * scale
        grad_ref[:, half_width:] = high * scale
    grad_one_ref[...] = turned_row(total)
    both = near[:, start:] + far[:, start:]
    grad_output_ref[...] = both[:, :width]
    small = both[:, width:]
    grad_router_ref[...] = small[:, :experts]
    lanes = lax.broadcasted_iota(jnp.int32, (1, small.shape[1]), 1)
    gain = jnp.sum(jnp.where(lanes == experts, small, 0.0), axis=1, keepdims=True)
    grad_two_ref[...] = turned_row(gain)


def finish(flags, operands, experts):
    own_rows, width = operands[4].shape
    shapes = [wide_shape(own_rows, width)] * 4
    shapes += [wide_shape(own_rows, experts)] + [wide_shape(1, own_rows)] * 2
    return one_step(finish_kernel, flags, operands, shapes, size=SMALL_BYTES)


def project_kernel(count, flags_ref, normed_ref, *refs):
    own_refs, other_refs = refs[:count], refs[count : 2 * count]
    query_ref, pair_ref, weight_ref = refs[2 * count :]
    rows = own_refs[0].shape[0]
    core = flags_ref[CORE]
    for m in range(count):
        place = 2 * (flags_ref[PLACE] ^ m)
        for index, ref in ((place + core, own_refs[m]), (place + 1 - core, other_refs[m])):
            place_rows = pl.ds(pl.multiple_of(index * rows, 16), rows)
            weight_ref[place_rows, :] = ref[...]
    projected = dot(normed_ref[...], weight_ref[...]).astype(BF)
    query_ref[...] = projected[:, : query_ref.shape[1]]
    pair_ref[...] = projected[:, query_ref.shape[1] :]


def project(flags, normed, own, other):
    count = len(own)
    rows, width = normed.shape
    columns = 3 * width // 2
    shapes = [
        low_shape(rows, width // 2),
        low_shape(rows, width),
        low_shape(width, columns),
    ]
    kernel = functools.partial(project_kernel, count)
    return one_step(kernel, flags, [normed, *own, *other], shapes)


def assemble_kernel(lane, flags_ref, *refs):
    *own_refs, other_ref, full_ref, row_ref = refs
    rows = own_refs[0].shape[0]
    width = full_ref.shape[0]
    core = flags_ref[CORE]
    for m, own_ref in enumerate(own_refs):
        place = 2 * (flags_ref[PLACE] ^ m)
        full_ref[pl.ds(pl.multiple_of((place + core) * rows, 16), rows), :] = own_ref[...]
        full_ref[pl.ds(pl.multiple_of((place + 1 - core) * rows, 16), rows), :] = other_ref[
            m * rows : (m + 1) * rows, :
        ]
    start = width + lane // 128 * 128
    block = full_ref[:, start : start + 128].astype(F32).T
    row_ref[...] = block[lane % 128 : lane % 128 + 1]


def assemble(flags, operands, lane):
    columns = operands[0].shape[1]
    width = 2 * operands[-1].shape[0]
    shapes = [low_shape(width, columns), wide_shape(1, width)]
    return one_step(functools.partial(assemble_kernel, lane), flags, operands, shapes)


def mixed_route_kernel(flags_ref, zero_ref, one_ref, two_ref, three_ref, mine_ref, sent_ref):
    half_width = zero_ref.shape[1]

    def body(half, same):
        near_ref, far_ref = (mine_ref, sent_ref) if same == 0 else (sent_ref, mine_ref)
        for into_ref, refs in ((near_ref, (zero_ref, one_ref)), (far_ref, (two_ref, three_ref))):
            into_ref[:, :half_width] = refs[half][...]
            into_ref[:, half_width:] = refs[1 - half][...]

    each_case(flags_ref, body)


def mixed_route(flags, parts):
    rows, half_width = parts[0].shape
    shapes = [low_shape(rows, 2 * half_width)] * 2
    return one_step(mixed_route_kernel, flags, parts, shapes, size=SMALL_BYTES)


def grad_route_kernel(flags_ref, mine_ref, got_ref, zero_ref, one_ref, two_ref, three_ref):
    half_width = zero_ref.shape[1]

    def body(half, same):
        near_ref, far_ref = (mine_ref, got_ref) if same == 0 else (got_ref, mine_ref)
        for from_ref, refs in ((near_ref, (zero_ref, one_ref)), (far_ref, (two_ref, three_ref))):
            refs[half][...] = from_ref[:, :half_width]
            refs[1 - half][...] = from_ref[:, half_width:]

    each_case(flags_ref, body)


def grad_route(flags, mine, got):
    rows, width = mine.shape
    shapes = [low_shape(rows, width // 2)] * 4
    return one_step(grad_route_kernel, flags, [mine, got], shapes, size=SMALL_BYTES)


def owner_forward_kernel(
    flags_ref,
    mine_ref,
    got_ref,
    inputs_ref,
    weight_ref,
    gain_ref,
    to_slots_ref,
    mixed_ref,
    middle_ref,
    slots_ref,
):
    half_rows = mine_ref.shape[0]
    for core in range(2):

        @pl.when(flags_ref[CORE] == core)
        def _(core=core):
            refs = (mine_ref, got_ref)
            mixed_ref[:half_rows] = refs[core][...]
            mixed_ref[half_rows:] = refs[1 - core][...]

    weight = weight_ref[:, : mixed_ref.shape[1]]
    middle = inputs_ref[...].astype(F32) + dot(mixed_ref[...], weight)
    middle_ref[...] = middle
    inverse = lax.rsqrt(jnp.mean(middle * middle, axis=1, keepdims=True) + EPSILON)
    second_low = (middle * inverse * gain_ref[...]).astype(BF)
    slots_ref[...] = dot(to_slots_ref[...], second_low).astype(BF)


def owner_forward(flags, mine, got, inputs, full_extra, gain, to_slots):
    rows, width = inputs.shape
    shapes = [
        low_shape(rows, width),
        wide_shape(rows, width),
        low_shape(to_slots.shape[0], width),
    ]
    operands = [mine, got, inputs, full_extra, gain, to_slots]
    return one_step(owner_forward_kernel, flags, operands, shapes)


TILE = 1024


def cotangent_kernel(cot_ref, compact_ref, weight_out_ref, held_ref, back_ref):
    @pl.when(pl.program_id(0) == 0)
    def _():
        held_ref[...] = dot(compact_ref[...], cot_ref[...]).astype(BF)

    back_ref[...] = dot_nt(held_ref[...], weight_out_ref[0]).astype(BF)


def cotangent_layer(cot, compact, expert_out):
    slots, width = cot.shape
    capacity = compact.shape[0]
    hidden_width = expert_out.shape[1]
    return pl.pallas_call(
        cotangent_kernel,
        grid=(hidden_width // TILE,),
        in_specs=[
            whole((slots, width)),
            whole((capacity, slots)),
            pl.BlockSpec((1, TILE, width), lambda i: (0, i, 0)),
        ],
        out_specs=[whole((capacity, width)), pl.BlockSpec((capacity, TILE), lambda i: (0, i))],
        out_shape=[low_shape(capacity, width), low_shape(capacity, hidden_width)],
        compiler_params=params(),
        cost_estimate=cost(2 * capacity * width * hidden_width, 4 * width * hidden_width),
    )(cot, compact, expert_out)


def expert_kernel(
    flags_ref,
    arrived_ref,
    cot_ref,
    back_ref,
    compact_ref,
    expand_ref,
    router_ref,
    weight_in_ref,
    held_ref,
    grad_result_ref,
    hidden_ref,
    grad_inner_ref,
    grad_back_ref,
    grad_logits_ref,
    gate_ref,
    grad_sum,
    probs,
    grad_gate,
):
    step = pl.program_id(0)
    experts = router_ref.shape[1]
    lanes = lax.broadcasted_iota(jnp.int32, (1, experts), 1)
    mine = (lanes == flags_ref[DEVICE]).astype(F32)

    @pl.when(step == 0)
    def _():
        held = dot(compact_ref[...], arrived_ref[...]).astype(BF)
        held_ref[...] = held
        logits = dot(held, router_ref[...])
        weights = jnp.exp(logits - jnp.max(logits, axis=1, keepdims=True))
        router_probs = weights / jnp.sum(weights, axis=1, keepdims=True)
        probs[...] = router_probs
        gate_rows = jnp.sum(router_probs * mine, axis=1, keepdims=True)
        gate_ref[...] = gate_rows
        grad_result_ref[...] = (gate_rows * cot_ref[...].astype(F32)).astype(BF)
        grad_sum[...] = jnp.zeros_like(grad_sum)
        grad_gate[...] = jnp.zeros_like(grad_gate)

    weight_in = weight_in_ref[0]
    hidden, slope = gelu_and_slope(dot(held_ref[...], weight_in))
    hidden = hidden.astype(BF)
    hidden_ref[...] = hidden
    back = back_ref[...].astype(F32)
    grad_inner = (back * (gate_ref[...] * slope)).astype(BF)
    grad_inner_ref[...] = grad_inner
    grad_gate[...] += jnp.sum(hidden.astype(F32) * back, axis=1, keepdims=True)
    grad_sum[...] += dot_nt(grad_inner, weight_in)

    @pl.when(step == pl.num_programs(0) - 1)
    def _():
        grad_logits = (grad_gate[...] * probs[...] * (mine - gate_ref[...])).astype(BF)
        grad_logits_ref[...] = grad_logits
        grad_held = grad_sum[...] + dot_nt(grad_logits, router_ref[...])
        grad_back_ref[...] = dot(expand_ref[...], grad_held.astype(BF)).astype(BF)


def expert_layer(flags, arrived, cot, back, compact, expand, router, expert_in):
    slots, width = arrived.shape
    capacity = compact.shape[0]
    hidden_width = expert_in.shape[2]
    experts = router.shape[1]
    wide = whole((capacity, width))
    tall = pl.BlockSpec((capacity, TILE), lambda i: (0, i))
    return pl.pallas_call(
        expert_kernel,
        grid=(hidden_width // TILE,),
        in_specs=[
            FLAGS,
            whole((slots, width)),
            wide,
            tall,
            whole((capacity, slots)),
            whole((slots, capacity)),
            whole((width, experts)),
            pl.BlockSpec((1, width, TILE), lambda i: (0, 0, i)),
        ],
        out_specs=[wide, wide, tall, tall, whole((slots, width))]
        + [whole((capacity, experts)), whole((capacity, 1))],
        out_shape=[
            low_shape(capacity, width),
            low_shape(capacity, width),
            low_shape(capacity, hidden_width),
            low_shape(capacity, hidden_width),
            low_shape(slots, width),
            low_shape(capacity, experts),
            wide_shape(capacity, 1),
        ],
        scratch_shapes=[
            pltpu.VMEM((capacity, width), F32),
            pltpu.VMEM((capacity, experts), F32),
            pltpu.VMEM((capacity, 1), F32),
        ],
        compiler_params=params(),
        cost_estimate=cost(8 * capacity * width * hidden_width, 8 * width * hidden_width),
    )(flags, arrived, cot, back, compact, expand, router, expert_in)


def owner_backward_kernel(
    flags_ref,
    returned_ref,
    to_tokens_ref,
    cotangent_ref,
    middle_ref,
    gain_ref,
    weight_ref,
    grad_middle_ref,
    grad_branch_ref,
    mine_ref,
    sent_ref,
    grad_gain_ref,
):
    half_rows = mine_ref.shape[0]
    middle = middle_ref[...]
    inverse = lax.rsqrt(jnp.mean(middle * middle, axis=1, keepdims=True) + EPSILON)
    normed = middle * inverse
    grad_second = dot(to_tokens_ref[...], returned_ref[...])
    grouped = (grad_second * normed).reshape(-1, GAIN_ROWS, grad_second.shape[1])
    grad_gain_ref[...] = jnp.sum(grouped, axis=0).astype(BF)
    scaled = grad_second * gain_ref[...]
    grad_middle = cotangent_ref[...].astype(F32) + inverse * (
        scaled - normed * jnp.mean(scaled * normed, axis=1, keepdims=True)
    )
    grad_middle_ref[...] = grad_middle
    grad_branch = grad_middle.astype(BF)
    grad_branch_ref[...] = grad_branch
    weight = weight_ref[:, : middle.shape[1]]
    grad_mixed = dot_nt(grad_branch, weight).astype(BF)
    for core in range(2):

        @pl.when(flags_ref[CORE] == core)
        def _(core=core):
            mine_ref[...] = grad_mixed[core * half_rows : (core + 1) * half_rows]
            sent_ref[...] = grad_mixed[(1 - core) * half_rows : (2 - core) * half_rows]


def owner_backward(flags, returned, to_tokens, cotangent, middle, gain, full_extra):
    rows, width = cotangent.shape
    shapes = [
        wide_shape(rows, width),
        low_shape(rows, width),
        low_shape(rows // 2, width),
        low_shape(rows // 2, width),
        low_shape(GAIN_ROWS, width),
    ]
    operands = [returned, to_tokens, cotangent, middle, gain, full_extra]
    return one_step(owner_backward_kernel, flags, operands, shapes)


GAIN_ROWS = 16


def deal_rows(flags_ref, total, keep_ref, send_ref, rows):
    core = flags_ref[CORE]
    for m in range(total.shape[0] // (2 * rows)):
        place = 2 * (flags_ref[PLACE] ^ m)
        keep_ref[m * rows : (m + 1) * rows, :] = total[
            pl.ds(pl.multiple_of((place + core) * rows, 8), rows), :
        ]
        send_ref[m * rows : (m + 1) * rows, :] = total[
            pl.ds(pl.multiple_of((place + 1 - core) * rows, 8), rows), :
        ].astype(BF)


def dealt(width, columns):
    return [wide_shape(width // 2, columns), low_shape(width // 2, columns)]


def weight_grads_kernel(
    rows,
    flags_ref,
    normed_ref,
    query_ref,
    near_ref,
    got_ref,
    mixed_ref,
    branch_ref,
    router_ref,
    gain_ref,
    projected_ref,
    keep_ref,
    send_ref,
    total,
):
    part = query_ref.shape[1]
    width, experts = router_ref.shape
    extra = total.shape[1] - 3 * part - width
    projected_ref[:, :part] = query_ref[...]
    for index in range(2):
        both = near_ref[index].astype(F32) + got_ref[index].astype(F32)
        projected_ref[:, (index + 1) * part : (index + 2) * part] = both.astype(BF)
    total[:, : 3 * part] = dot_tn(normed_ref[...], projected_ref[...])
    total[:, 3 * part : 3 * part + width] = dot_tn(mixed_ref[...], branch_ref[...])
    gain = dot_tn(gain_ref[...], jnp.ones((GAIN_ROWS, extra), BF))
    router = router_ref[...]
    router = jnp.concatenate([router, jnp.zeros((width, extra - experts), F32)], axis=1)
    lanes = lax.broadcasted_iota(jnp.int32, (1, extra), 1)
    total[:, 3 * part + width :] = jnp.where(lanes == experts, gain, router)
    deal_rows(flags_ref, total, keep_ref, send_ref, rows)


def weight_grads(flags, operands, rows):
    work_rows, width = operands[0].shape
    part = operands[1].shape[1]
    experts = operands[6].shape[1]
    columns = 3 * part + width + experts + 1
    columns += -columns % 128
    return one_step(
        functools.partial(weight_grads_kernel, rows),
        flags,
        operands,
        [low_shape(work_rows, 3 * part)] + dealt(width, columns),
        [pltpu.VMEM((width, columns), F32)],
        2 * SMALL_BYTES,
    )


def all_to_all(array):
    return lax.all_to_all(array, AXES, split_axis=0, concat_axis=0, tiled=True)


def on_device(
    inputs,
    norm_one,
    w_query,
    w_key,
    w_value,
    w_output,
    norm_two,
    w_router,
    expert_in,
    expert_out,
    routes,
    cotangent,
):
    links = Links()
    level, core = links.level, links.core
    device = links.group * links.levels + level
    devices = links.groups * links.levels
    rows, width = inputs.shape
    half_rows = rows // 2
    half_width = width // 2
    experts = w_router.shape[1]
    own_rows = norm_one.shape[0]
    most = 2 * rows // experts
    capacity = 5 * rows // 4
    blocks = links.levels

    same = (level >> 1) ^ core
    flags = jnp.stack([core, level & 1, same, device, links.group >> 1]).astype(jnp.int32)

    mine = pick(core, inputs[:half_rows], inputs[half_rows:])
    got = links.swap_core(pick(core, inputs[half_rows:], inputs[:half_rows]))
    kept, cross = pack(
        flags,
        [w_query, w_key, w_value, w_output, w_router, routes.reshape(1, rows)]
        + [norm_one.reshape(1, own_rows), norm_two.reshape(1, own_rows)],
    )
    level_block = gather_levels(links, [kept, cross, kept, cross])
    level_rows = level_block.shape[0]
    got = gate(got, kept, cross)
    near, far = pick(same, mine, got), pick(same, got, mine)
    near_first = links.swap_level(near, 1)
    far_first = links.swap_level(far, 2)
    far_second = links.swap_level(far_first, 1)
    level_weights = level_block[:, : 3 * half_width]
    own_blocks = gather_groups(links, level_weights)
    chosen = gate(routes, level_block)[:, 0]
    picked = (chosen[:, None] == jnp.arange(experts, dtype=jnp.int32)[None, :]).astype(jnp.int32)
    rank = jnp.sum((jnp.cumsum(picked, axis=0) - picked) * picked, axis=1)
    place = chosen * most + rank
    slot_index = jnp.arange(experts * most, dtype=jnp.int32)
    to_slots = (slot_index[:, None] == place[None, :]).astype(BF)
    to_tokens = (place[:, None] == slot_index[None, :]).astype(BF)
    cot_slots = dot(to_slots, cotangent).astype(BF).reshape(experts, most, width)

    own_blocks = tie(*own_blocks, near_first, far_first, cot_slots)[:-3]
    other_blocks = [links.swap_core(part) for part in own_blocks]

    source = jnp.concatenate([near, near_first, far_first, far_second], axis=0).astype(F32)
    normed_work = (
        source * lax.rsqrt(jnp.mean(source * source, axis=-1, keepdims=True) + EPSILON)
    ).astype(BF)
    own_extra = gather_groups(links, gate(level_block[:, 3 * half_width :], *own_blocks))
    if level_rows % 16 == 0:
        queries, pair, weights = project(flags, normed_work, own_blocks, other_blocks)
    else:
        weights = in_order(links, own_blocks, other_blocks)
        projected = dot(normed_work, weights).astype(BF)
        queries, pair = projected[:, :half_width], projected[:, half_width:]
    pair_far = links.swap_core(pair)
    cot_arrived = all_to_all(gate(cot_slots, *own_blocks)).reshape(-1, width)
    *mixed_parts, attention_weights, inverse = attention_forward(queries, pair, pair_far)
    mixed_parts = tie(*mixed_parts, cot_arrived, *own_extra)[:4]

    own_extra = tie(*own_extra, *mixed_parts)[: len(own_extra)]
    other_extra = links.swap_core(jnp.concatenate(own_extra, axis=0))
    if level_rows % 16 == 0:
        full_extra, gain_two = assemble(flags, [*own_extra, other_extra], 2 * experts)
    else:
        other_parts = [
            other_extra[m * level_rows : (m + 1) * level_rows] for m in range(len(own_extra))
        ]
        full_extra = in_order(links, own_extra, other_parts)
        gain_two = full_extra[:, width + 2 * experts].astype(F32)[None]
    full_router = full_extra[:, width : width + experts]
    last_part = gate(mixed_parts[1], gain_two)
    back = [links.swap_level(mixed_parts[2], 2), links.swap_level(mixed_parts[3], 3)]
    back = tie(links.swap_level(last_part, 1), *back)
    tallies = full_extra[::own_rows, width + experts : width + 2 * experts].astype(F32)
    mine_only = (jnp.arange(experts, dtype=jnp.int32) == device).astype(F32)[None, :]
    counts = jnp.sum(tallies * mine_only, axis=1).astype(jnp.int32)
    offsets = jnp.cumsum(counts) - counts
    within = jnp.arange(most, dtype=jnp.int32)[None, :]
    slot_grid = offsets[:, None] + within
    usable = (within < counts[:, None]) & (slot_grid < capacity)
    slot_flat = jnp.where(usable, slot_grid, -1).reshape(-1)
    held_index = jnp.arange(capacity, dtype=jnp.int32)
    compact = (held_index[:, None] == slot_flat[None, :]).astype(BF)
    expand = (slot_flat[:, None] == held_index[None, :]).astype(BF)

    mixed_mine, mixed_sent = mixed_route(flags, [mixed_parts[0], *back])
    mixed_low, middle, second_slots = owner_forward(
        flags, mixed_mine, links.swap_core(mixed_sent), inputs, full_extra, gain_two, to_slots
    )
    arrived = all_to_all(second_slots.reshape(experts, most, width)).reshape(-1, width)

    cot_held, cot_back = cotangent_layer(gate(cot_arrived, second_slots), compact, expert_out)
    held, grad_result, hidden, grad_inner, grad_back, grad_logits, gate_rows = expert_layer(
        flags,
        gate(arrived, cot_back),
        cot_held,
        cot_back,
        compact,
        expand,
        full_router,
        expert_in,
    )
    grad_returned = all_to_all(grad_back.reshape(experts, most, width)).reshape(-1, width)
    grad_router = dot_tn(held, grad_logits)
    grad_weight_out = dot_tn(hidden, grad_result)
    grad_weight_in = dot_tn(held, grad_inner)
    result = dot(hidden, expert_out[0]).astype(BF).astype(F32)
    taken_back = dot(expand, (gate_rows * result).astype(BF)).astype(BF)
    grad_returned = gate(
        grad_returned, grad_weight_in, grad_weight_out, grad_router, taken_back, to_tokens
    )

    grad_middle, grad_branch, grad_mine, grad_sent, gain_rows = owner_backward(
        flags, grad_returned, to_tokens, cotangent, middle, gain_two, full_extra
    )
    routed = grad_route(flags, grad_mine, links.swap_core(grad_sent))
    got = [links.swap_level(routed[b], b) for b in (1, 2, 3)]

    got = tie(*got)
    taken_back = gate(taken_back, *got).reshape(experts, most, width)
    taken_arrived = all_to_all(taken_back).reshape(-1, width)
    grad_queries, grad_near, grad_far = attention_backward(
        queries,
        pair,
        pair_far,
        attention_weights,
        inverse,
        [routed[0], *got],
        mixed_parts,
    )
    got_pair = links.swap_core(grad_far)
    grad_projected, keep, send = weight_grads(
        flags,
        [normed_work, grad_queries, grad_near, got_pair]
        + [mixed_low, grad_branch, grad_router, gain_rows],
        level_rows,
    )
    grad_first_work = dot_nt(grad_projected, weights).astype(BF)
    core_sum = reduce_cores(links, keep, gate(send, taken_arrived))
    core_sum = gate(core_sum, grad_first_work)
    group_sum = reduce_groups(
        links, [core_sum[m * level_rows : (m + 1) * level_rows] for m in range(links.groups // 2)]
    )
    parts = gate(grad_first_work, core_sum).reshape(blocks, half_rows, width)
    back = tie(*[links.swap_level(parts[b], b) for b in (1, 2, 3)])
    back = tie(*back, group_sum)[:-1]
    near = (parts[0].astype(F32) + back[0].astype(F32)).astype(BF)
    far = (back[1].astype(F32) + back[2].astype(F32)).astype(BF)
    grad_first = workers_to_owner(links, near, far).astype(F32)
    source_own = inputs.astype(F32)
    inverse_one = lax.rsqrt(jnp.mean(source_own * source_own, axis=-1, keepdims=True) + EPSILON)
    normed_one = source_own * inverse_one
    grad_input = grad_middle + inverse_one * (
        grad_first - normed_one * jnp.mean(grad_first * normed_one, axis=-1, keepdims=True)
    )
    output = (middle + dot(to_tokens, taken_arrived)).astype(BF)

    sums = reduce_levels(links, gate(group_sum, *back), grad_input)
    *grad_weights, grad_w_output, grad_w_router, grad_norm_one, grad_norm_two = finish(
        flags,
        [*sums, w_query, w_key, w_value, norm_one.reshape(1, own_rows)],
        experts,
    )
    return (
        output,
        grad_input,
        grad_norm_one.reshape(own_rows),
        grad_weights[0],
        grad_weights[1],
        grad_weights[2],
        grad_w_output,
        grad_norm_two.reshape(own_rows),
        grad_w_router,
        grad_weight_in[None],
        grad_weight_out[None],
    )


def solution(mesh):
    return jax.shard_map(
        on_device,
        mesh=mesh,
        in_specs=(
            P(AXES, None),
            P(AXES),
            P(AXES, None),
            P(AXES, None),
            P(AXES, None),
            P(AXES, None),
            P(AXES),
            P(AXES, None),
            P(AXES, None, None),
            P(AXES, None, None),
            P(AXES, None),
            P(AXES, None),
        ),
        out_specs=(
            P(AXES, None),
            P(AXES, None),
            P(AXES),
            P(AXES, None),
            P(AXES, None),
            P(AXES, None),
            P(AXES, None),
            P(AXES),
            P(AXES, None),
            P(AXES, None, None),
            P(AXES, None, None),
        ),
        check_vma=False,
    )
```

```python
import functools

import jax
import jax.numpy as jnp
from jax import lax
from jax.experimental import pallas as pl
from jax.experimental.pallas import tpu as pltpu
from jax.sharding import PartitionSpec as P

HEAD_DIM = 64
AXES = ("group", "local")
BF = jnp.bfloat16
F32 = jnp.float32
EPSILON = 1e-06
VMEM_BYTES = 58 * 2**20
SMALL_BYTES = 24 * 2**20


def dot(left, right):
    return jnp.dot(left, right, preferred_element_type=F32)


def dot_tn(left, right):
    return lax.dot_general(left, right, (((0,), (0,)), ((), ())), preferred_element_type=F32)


def dot_nt(left, right):
    return lax.dot_general(left, right, (((1,), (1,)), ((), ())), preferred_element_type=F32)


class Links:
    def __init__(self):
        self.groups = lax.axis_size("group")
        self.levels = lax.axis_size("local")
        self.group = lax.axis_index("group")
        self.level = lax.axis_index("local")
        self.core = self.group % 2

    def permute(self, array, target):
        pairs = []
        for group in range(self.groups):
            for level in range(self.levels):
                other_group, other_level = target(group, level)
                pairs.append((group * self.levels + level, other_group * self.levels + other_level))
        return lax.ppermute(array, AXES, pairs)

    def swap_core(self, array):
        return self.permute(array, lambda g, l: (g ^ 1, l))

    def swap_level(self, array, mask):
        return self.permute(array, lambda g, l: (g, l ^ mask))

    def swap_group(self, array, mask):
        return self.permute(array, lambda g, l: (g ^ (2 * mask), l))


def gate(array, *after):
    return lax.optimization_barrier((array, *after))[0]


def tie(*arrays):
    return lax.optimization_barrier(arrays)


def pick(flag, first, second):
    return jnp.where(flag == 0, first, second)


def joined(flag, mine, other, axis=0):
    return jnp.concatenate([pick(flag, mine, other), pick(flag, other, mine)], axis=axis)


def ordered(index, parts):
    count = len(parts)
    if count == 1:
        return parts[0]
    top = count.bit_length() - 2
    half = count // 2
    low = index & (half - 1)
    return joined((index >> top) & 1, ordered(low, parts[:half]), ordered(low, parts[half:]))


def rows_of(array, index, rows):
    return lax.dynamic_slice_in_dim(array, index * rows, rows, axis=0)


def gather_levels(links, pieces):
    got = tie(*[links.swap_level(pieces[b], b) for b in range(1, links.levels)])
    return ordered(links.level, [pieces[0], *got])


def gather_groups(links, block):
    return [block] + [links.swap_group(block, m) for m in range(1, links.groups // 2)]


def in_order(links, own, other):
    pairs = [joined(links.core, mine, far) for mine, far in zip(own, other)]
    return ordered(links.group >> 1, pairs)


def reduce_cores(links, keep, send):
    return keep + links.swap_core(send).astype(F32)


def reduce_groups(links, parts):
    got = [links.swap_group(parts[m].astype(BF), m) for m in range(1, len(parts))]
    total = parts[0]
    for part in tie(*got):
        total = total + part.astype(F32)
    return total


def reduce_levels(links, block, before_last):
    rows = block.shape[0] // links.levels
    parts = [rows_of(block, links.level ^ b, rows) for b in range(links.levels)]
    sent = [part.astype(BF) for part in parts[1:]]
    sent[0] = gate(sent[0], before_last)
    got = tie(*[links.swap_level(part, b + 1) for b, part in enumerate(sent)])
    return [parts[0], *got]


def owner_to_workers(links, array):
    half = array.shape[0] // 2
    mine = pick(links.core, array[:half], array[half:])
    other = links.swap_core(pick(links.core, array[half:], array[:half]))
    same = (links.level >> 1) ^ links.core
    return pick(same, mine, other), pick(same, other, mine)


def workers_to_owner(links, near, far):
    same = (links.level >> 1) ^ links.core
    mine = pick(same, near, far)
    other = links.swap_core(pick(same, far, near))
    return joined(links.core, mine, other)


PAIR = 2 * HEAD_DIM


def head_masks(dtype):
    lanes = lax.broadcasted_iota(jnp.int32, (1, PAIR), 1)
    return [(lanes // HEAD_DIM == head).astype(dtype) for head in range(2)]


CHUNK = 128


def forward_kernel(query_ref, key_ref, value_ref, key_far_ref, value_far_ref, *refs):
    mixed_refs, weights_ref, inverse_ref = refs[:-2], refs[-2], refs[-1]
    query = query_ref[...] * BF(HEAD_DIM**-0.5)
    key = jnp.concatenate([key_ref[...], key_far_ref[...]], axis=0)
    value = jnp.concatenate([value_ref[...], value_far_ref[...]], axis=0)
    value = jnp.concatenate([value, jnp.ones_like(value)], axis=1)
    first_head = lax.broadcasted_iota(jnp.int32, (1, PAIR), 1) < HEAD_DIM
    for part, mixed_ref in enumerate(mixed_refs):
        rows = slice(part * CHUNK, (part + 1) * CHUNK)
        sums = []
        for head, mask in enumerate(head_masks(BF)):
            scores = dot_nt(query[rows] * mask, key)
            weights = jnp.exp(scores - jnp.max(scores, axis=1, keepdims=True)).astype(BF)
            weights_ref[head, rows] = weights
            sums.append(dot(weights, value))
        mixed = jnp.where(first_head, sums[0][:, :PAIR], sums[1][:, :PAIR])
        inverse = 1.0 / jnp.where(first_head, sums[0][:, PAIR:], sums[1][:, PAIR:])
        inverse_ref[rows] = inverse
        mixed_ref[...] = (mixed * inverse).astype(BF)


def pair_column(rows, block=0):
    return pl.BlockSpec((rows, PAIR), lambda i: (0, block + i))


def weights_block(rows):
    return pl.BlockSpec((2, rows, 2 * rows), lambda i: (i, 0, 0))


def attention_forward(queries, pair, pair_far):
    rows, half_width = queries.shape
    pairs = half_width // PAIR
    return pl.pallas_call(
        forward_kernel,
        grid=(pairs,),
        in_specs=[pair_column(rows)] + [pair_column(rows), pair_column(rows, pairs)] * 2,
        out_specs=[pair_column(CHUNK)] * (rows // CHUNK) + [weights_block(rows), pair_column(rows)],
        out_shape=[low_shape(CHUNK, half_width)] * (rows // CHUNK)
        + [low_shape(2 * pairs, rows, 2 * rows), wide_shape(rows, half_width)],
        compiler_params=params(),
        cost_estimate=cost(2 * 10**9, 4096),
    )(queries, pair, pair, pair_far, pair_far)


def backward_kernel(
    query_ref, key_ref, value_ref, key_far_ref, value_far_ref, weights_ref, inverse_ref, *refs
):
    grad_refs, mixed_refs = refs[:4], refs[4:8]
    grad_query_ref, grad_near_ref, grad_far_ref = refs[8:]
    all_rows = query_ref.shape[0]
    factor = BF(HEAD_DIM**-0.5)
    query = query_ref[...] * factor
    key = jnp.concatenate([key_ref[...], key_far_ref[...]], axis=0)
    value = jnp.concatenate([value_ref[...], value_far_ref[...]], axis=0)
    grad = jnp.concatenate([ref[...] for ref in grad_refs], axis=0).astype(F32)
    grad = grad * inverse_ref[...]
    mixed = jnp.concatenate([ref[...] for ref in mixed_refs], axis=0)
    together = grad * mixed.astype(F32)
    grad = grad.astype(BF)
    grad_key = jnp.zeros((PAIR, 2 * all_rows), F32)
    grad_value = jnp.zeros((PAIR, 2 * all_rows), F32)
    for part in range(all_rows // (2 * CHUNK)):
        rows = slice(part * 2 * CHUNK, (part + 1) * 2 * CHUNK)
        grad_query = jnp.zeros((2 * CHUNK, PAIR), F32)
        for head, (mask, mask_wide) in enumerate(zip(head_masks(BF), head_masks(F32))):
            weights = weights_ref[head, rows]
            grad_one = grad[rows] * mask
            row_dots = jnp.sum(together[rows] * mask_wide, axis=1, keepdims=True)
            grad_weights = dot_nt(grad_one, value)
            grad_scores = (weights.astype(F32) * (grad_weights - row_dots)).astype(BF)
            grad_value = grad_value + dot_tn(grad_one, weights)
            grad_key = grad_key + dot_tn(query[rows] * mask, grad_scores)
            grad_query = grad_query + dot(grad_scores, key * (mask * factor))
        grad_query_ref[rows] = grad_query.astype(BF)
    for index, total in enumerate((grad_key, grad_value)):
        total = total.T
        grad_near_ref[index] = total[:all_rows].astype(BF)
        grad_far_ref[index] = total[all_rows:].astype(BF)


def attention_backward(queries, pair, pair_far, weights, inverse, grads, mixed):
    rows, half_width = queries.shape
    pairs = half_width // PAIR
    return pl.pallas_call(
        backward_kernel,
        grid=(pairs,),
        in_specs=[pair_column(rows)]
        + [pair_column(rows), pair_column(rows, pairs)] * 2
        + [weights_block(rows), pair_column(rows)]
        + [pair_column(rows // 4)] * 8,
        out_specs=[pair_column(rows)] + [pl.BlockSpec((2, rows, PAIR), lambda i: (0, 0, i))] * 2,
        out_shape=[low_shape(rows, half_width)] + [low_shape(2, rows, half_width)] * 2,
        compiler_params=params(),
        cost_estimate=cost(2 * 10**10, 4096),
    )(queries, pair, pair, pair_far, pair_far, weights, inverse, *grads, *mixed)


GELU_SCALE = 0.7978845608028654
GELU_CUBE = 0.044715


def gelu_and_slope(values):
    square = values * values
    bend = jnp.tanh(GELU_SCALE * values * (1.0 + GELU_CUBE * square))
    half = 0.5 + 0.5 * bend
    slope = half + 0.5 * values * (1.0 - bend * bend) * GELU_SCALE * (1.0 + 3 * GELU_CUBE * square)
    return values * half, slope


def whole(shape):
    return pl.BlockSpec(shape, lambda *_: (0,) * len(shape))


FLAGS = pl.BlockSpec(memory_space=pltpu.SMEM)
CORE, HALF, SAME, DEVICE, PLACE = range(5)


def params(size=VMEM_BYTES):
    return pltpu.CompilerParams(vmem_limit_bytes=size)


def cost(flops, size):
    return pl.CostEstimate(flops=flops, bytes_accessed=size, transcendentals=0)


def one_step(kernel, flags, operands, shapes, scratch=(), size=VMEM_BYTES):
    return pl.pallas_call(
        kernel,
        grid=(1,),
        in_specs=[FLAGS] + [whole(operand.shape) for operand in operands],
        out_specs=[whole(shape.shape) for shape in shapes],
        out_shape=shapes,
        scratch_shapes=list(scratch),
        compiler_params=params(size),
        cost_estimate=cost(0, 2**20),
    )(flags, *operands)


def low_shape(*shape):
    return jax.ShapeDtypeStruct(shape, BF)


def wide_shape(*shape):
    return jax.ShapeDtypeStruct(shape, F32)


def each_case(flags_ref, body):
    for half in range(2):
        for same in range(2):

            @pl.when((flags_ref[HALF] == half) & (flags_ref[SAME] == same))
            def _(half=half, same=same):
                body(half, same)


def turned_column(row):
    count = row.shape[1]
    rows = lax.broadcasted_iota(jnp.int32, (count, count), 0)
    lanes = lax.broadcasted_iota(jnp.int32, (count, count), 1)
    return jnp.sum(jnp.where(rows == lanes, row, 0.0), axis=1, keepdims=True)


def turned_row(column):
    count = column.shape[0]
    rows = lax.broadcasted_iota(jnp.int32, (count, count), 0)
    lanes = lax.broadcasted_iota(jnp.int32, (count, count), 1)
    return jnp.sum(jnp.where(rows == lanes, column, 0.0), axis=0, keepdims=True)


def pack_kernel(
    flags_ref,
    query_ref,
    key_ref,
    value_ref,
    output_ref,
    router_ref,
    routes_ref,
    norm_one_ref,
    norm_two_ref,
    kept_ref,
    cross_ref,
):
    own_rows, width = query_ref.shape
    experts = router_ref.shape[1]
    half_width = width // 2
    start = 3 * half_width
    tail = kept_ref.shape[1] - start - width
    scale = turned_column(norm_one_ref[...].astype(F32))
    first_half = flags_ref[HALF] == 0
    for index, ref in enumerate((query_ref, key_ref, value_ref)):
        scaled = (ref[...].astype(F32) * scale).astype(BF)
        low, high = scaled[:, :half_width], scaled[:, half_width:]
        columns = slice(index * half_width, (index + 1) * half_width)
        kept_ref[:, columns] = jnp.where(first_half, low, high)
        cross_ref[:, columns] = jnp.where(first_half, high, low)
    lanes = lax.broadcasted_iota(jnp.int32, (1, tail), 1)
    index = lax.broadcasted_iota(jnp.int32, (tail, 1), 0) - experts
    tally = jnp.sum((routes_ref[...] == index).astype(F32), axis=1, keepdims=True)
    tally = turned_row(tally)
    router = router_ref[...].astype(F32)
    router = jnp.concatenate([router, jnp.zeros((own_rows, tail - experts), F32)], axis=1)
    gain = turned_column(norm_two_ref[...].astype(F32))
    small = jnp.where(lanes < experts, router, jnp.where(lanes == 2 * experts, gain, tally))
    for ref in (kept_ref, cross_ref):
        ref[:, start : start + width] = output_ref[...]
        ref[:, start + width :] = small.astype(BF)


def pack(flags, operands):
    own_rows, width = operands[0].shape
    experts = operands[4].shape[1]
    tail = 2 * experts + 1
    columns = 3 * width // 2 + width + tail + -tail % 128
    return one_step(pack_kernel, flags, operands, [low_shape(own_rows, columns)] * 2)


def finish_kernel(
    flags_ref,
    zero_ref,
    one_ref,
    two_ref,
    three_ref,
    query_ref,
    key_ref,
    value_ref,
    norm_one_ref,
    grad_query_ref,
    grad_key_ref,
    grad_value_ref,
    grad_output_ref,
    grad_router_ref,
    grad_one_ref,
    grad_two_ref,
):
    width = query_ref.shape[1]
    experts = grad_router_ref.shape[1]
    half_width = width // 2
    start = 3 * half_width
    near = zero_ref[...] + two_ref[...].astype(F32)
    far = one_ref[...].astype(F32) + three_ref[...].astype(F32)
    scale = turned_column(norm_one_ref[...].astype(F32))
    first_half = flags_ref[HALF] == 0
    total = jnp.zeros_like(scale)
    pairs = ((query_ref, grad_query_ref), (key_ref, grad_key_ref), (value_ref, grad_value_ref))
    for index, (ref, grad_ref) in enumerate(pairs):
        columns = slice(index * half_width, (index + 1) * half_width)
        low = jnp.where(first_half, near[:, columns], far[:, columns])
        high = jnp.where(first_half, far[:, columns], near[:, columns])
        weight = ref[...].astype(F32)
        total = total + jnp.sum(weight[:, :half_width] * low, axis=1, keepdims=True)
        total = total + jnp.sum(weight[:, half_width:] * high, axis=1, keepdims=True)
        grad_ref[:, :half_width] = low * scale
        grad_ref[:, half_width:] = high * scale
    grad_one_ref[...] = turned_row(total)
    both = near[:, start:] + far[:, start:]
    grad_output_ref[...] = both[:, :width]
    small = both[:, width:]
    grad_router_ref[...] = small[:, :experts]
    lanes = lax.broadcasted_iota(jnp.int32, (1, small.shape[1]), 1)
    gain = jnp.sum(jnp.where(lanes == experts, small, 0.0), axis=1, keepdims=True)
    grad_two_ref[...] = turned_row(gain)


def finish(flags, operands, experts):
    own_rows, width = operands[4].shape
    shapes = [wide_shape(own_rows, width)] * 4
    shapes += [wide_shape(own_rows, experts)] + [wide_shape(1, own_rows)] * 2
    return one_step(finish_kernel, flags, operands, shapes, size=SMALL_BYTES)


def project_kernel(count, flags_ref, normed_ref, *refs):
    own_refs, other_refs = refs[:count], refs[count : 2 * count]
    query_ref, pair_ref, weight_ref = refs[2 * count :]
    rows = own_refs[0].shape[0]
    core = flags_ref[CORE]
    for m in range(count):
        place = 2 * (flags_ref[PLACE] ^ m)
        for index, ref in ((place + core, own_refs[m]), (place + 1 - core, other_refs[m])):
            place_rows = pl.ds(pl.multiple_of(index * rows, 16), rows)
            weight_ref[place_rows, :] = ref[...]
    projected = dot(normed_ref[...], weight_ref[...]).astype(BF)
    query_ref[...] = projected[:, : query_ref.shape[1]]
    pair_ref[...] = projected[:, query_ref.shape[1] :]


def project(flags, normed, own, other):
    count = len(own)
    rows, width = normed.shape
    columns = 3 * width // 2
    shapes = [
        low_shape(rows, width // 2),
        low_shape(rows, width),
        low_shape(width, columns),
    ]
    kernel = functools.partial(project_kernel, count)
    return one_step(kernel, flags, [normed, *own, *other], shapes)


def assemble_kernel(lane, flags_ref, *refs):
    *own_refs, other_ref, full_ref, row_ref = refs
    rows = own_refs[0].shape[0]
    width = full_ref.shape[0]
    core = flags_ref[CORE]
    for m, own_ref in enumerate(own_refs):
        place = 2 * (flags_ref[PLACE] ^ m)
        full_ref[pl.ds(pl.multiple_of((place + core) * rows, 16), rows), :] = own_ref[...]
        full_ref[pl.ds(pl.multiple_of((place + 1 - core) * rows, 16), rows), :] = other_ref[
            m * rows : (m + 1) * rows, :
        ]
    start = width + lane // 128 * 128
    block = full_ref[:, start : start + 128].astype(F32).T
    row_ref[...] = block[lane % 128 : lane % 128 + 1]


def assemble(flags, operands, lane):
    columns = operands[0].shape[1]
    width = 2 * operands[-1].shape[0]
    shapes = [low_shape(width, columns), wide_shape(1, width)]
    return one_step(functools.partial(assemble_kernel, lane), flags, operands, shapes)


def mixed_route_kernel(flags_ref, zero_ref, one_ref, two_ref, three_ref, mine_ref, sent_ref):
    half_width = zero_ref.shape[1]

    def body(half, same):
        near_ref, far_ref = (mine_ref, sent_ref) if same == 0 else (sent_ref, mine_ref)
        for into_ref, refs in ((near_ref, (zero_ref, one_ref)), (far_ref, (two_ref, three_ref))):
            into_ref[:, :half_width] = refs[half][...]
            into_ref[:, half_width:] = refs[1 - half][...]

    each_case(flags_ref, body)


def mixed_route(flags, parts):
    rows, half_width = parts[0].shape
    shapes = [low_shape(rows, 2 * half_width)] * 2
    return one_step(mixed_route_kernel, flags, parts, shapes, size=SMALL_BYTES)


def grad_route_kernel(flags_ref, mine_ref, got_ref, zero_ref, one_ref, two_ref, three_ref):
    half_width = zero_ref.shape[1]

    def body(half, same):
        near_ref, far_ref = (mine_ref, got_ref) if same == 0 else (got_ref, mine_ref)
        for from_ref, refs in ((near_ref, (zero_ref, one_ref)), (far_ref, (two_ref, three_ref))):
            refs[half][...] = from_ref[:, :half_width]
            refs[1 - half][...] = from_ref[:, half_width:]

    each_case(flags_ref, body)


def grad_route(flags, mine, got):
    rows, width = mine.shape
    shapes = [low_shape(rows, width // 2)] * 4
    return one_step(grad_route_kernel, flags, [mine, got], shapes, size=SMALL_BYTES)


def owner_forward_kernel(
    flags_ref,
    mine_ref,
    got_ref,
    inputs_ref,
    weight_ref,
    gain_ref,
    to_slots_ref,
    mixed_ref,
    middle_ref,
    slots_ref,
):
    half_rows = mine_ref.shape[0]
    for core in range(2):

        @pl.when(flags_ref[CORE] == core)
        def _(core=core):
            refs = (mine_ref, got_ref)
            mixed_ref[:half_rows] = refs[core][...]
            mixed_ref[half_rows:] = refs[1 - core][...]

    weight = weight_ref[:, : mixed_ref.shape[1]]
    middle = inputs_ref[...].astype(F32) + dot(mixed_ref[...], weight)
    middle_ref[...] = middle
    inverse = lax.rsqrt(jnp.mean(middle * middle, axis=1, keepdims=True) + EPSILON)
    second_low = (middle * inverse * gain_ref[...]).astype(BF)
    slots_ref[...] = dot(to_slots_ref[...], second_low).astype(BF)


def owner_forward(flags, mine, got, inputs, full_extra, gain, to_slots):
    rows, width = inputs.shape
    shapes = [
        low_shape(rows, width),
        wide_shape(rows, width),
        low_shape(to_slots.shape[0], width),
    ]
    operands = [mine, got, inputs, full_extra, gain, to_slots]
    return one_step(owner_forward_kernel, flags, operands, shapes)


TILE = 1024


def cotangent_kernel(cot_ref, compact_ref, weight_out_ref, held_ref, back_ref):
    @pl.when(pl.program_id(0) == 0)
    def _():
        held_ref[...] = dot(compact_ref[...], cot_ref[...]).astype(BF)

    back_ref[...] = dot_nt(held_ref[...], weight_out_ref[0]).astype(BF)


def cotangent_layer(cot, compact, expert_out):
    slots, width = cot.shape
    capacity = compact.shape[0]
    hidden_width = expert_out.shape[1]
    return pl.pallas_call(
        cotangent_kernel,
        grid=(hidden_width // TILE,),
        in_specs=[
            whole((slots, width)),
            whole((capacity, slots)),
            pl.BlockSpec((1, TILE, width), lambda i: (0, i, 0)),
        ],
        out_specs=[whole((capacity, width)), pl.BlockSpec((capacity, TILE), lambda i: (0, i))],
        out_shape=[low_shape(capacity, width), low_shape(capacity, hidden_width)],
        compiler_params=params(),
        cost_estimate=cost(2 * capacity * width * hidden_width, 4 * width * hidden_width),
    )(cot, compact, expert_out)


def expert_kernel(
    flags_ref,
    arrived_ref,
    cot_ref,
    back_ref,
    compact_ref,
    expand_ref,
    router_ref,
    weight_in_ref,
    held_ref,
    grad_result_ref,
    hidden_ref,
    grad_inner_ref,
    grad_back_ref,
    grad_logits_ref,
    gate_ref,
    grad_sum,
    probs,
    grad_gate,
):
    step = pl.program_id(0)
    experts = router_ref.shape[1]
    lanes = lax.broadcasted_iota(jnp.int32, (1, experts), 1)
    mine = (lanes == flags_ref[DEVICE]).astype(F32)

    @pl.when(step == 0)
    def _():
        held = dot(compact_ref[...], arrived_ref[...]).astype(BF)
        held_ref[...] = held
        logits = dot(held, router_ref[...])
        weights = jnp.exp(logits - jnp.max(logits, axis=1, keepdims=True))
        router_probs = weights / jnp.sum(weights, axis=1, keepdims=True)
        probs[...] = router_probs
        gate_rows = jnp.sum(router_probs * mine, axis=1, keepdims=True)
        gate_ref[...] = gate_rows
        grad_result_ref[...] = (gate_rows * cot_ref[...].astype(F32)).astype(BF)
        grad_sum[...] = jnp.zeros_like(grad_sum)
        grad_gate[...] = jnp.zeros_like(grad_gate)

    weight_in = weight_in_ref[0]
    hidden, slope = gelu_and_slope(dot(held_ref[...], weight_in))
    hidden = hidden.astype(BF)
    hidden_ref[...] = hidden
    back = back_ref[...].astype(F32)
    grad_inner = (back * (gate_ref[...] * slope)).astype(BF)
    grad_inner_ref[...] = grad_inner
    grad_gate[...] += jnp.sum(hidden.astype(F32) * back, axis=1, keepdims=True)
    grad_sum[...] += dot_nt(grad_inner, weight_in)

    @pl.when(step == pl.num_programs(0) - 1)
    def _():
        grad_logits = (grad_gate[...] * probs[...] * (mine - gate_ref[...])).astype(BF)
        grad_logits_ref[...] = grad_logits
        grad_held = grad_sum[...] + dot_nt(grad_logits, router_ref[...])
        grad_back_ref[...] = dot(expand_ref[...], grad_held.astype(BF)).astype(BF)


def expert_layer(flags, arrived, cot, back, compact, expand, router, expert_in):
    slots, width = arrived.shape
    capacity = compact.shape[0]
    hidden_width = expert_in.shape[2]
    experts = router.shape[1]
    wide = whole((capacity, width))
    tall = pl.BlockSpec((capacity, TILE), lambda i: (0, i))
    return pl.pallas_call(
        expert_kernel,
        grid=(hidden_width // TILE,),
        in_specs=[
            FLAGS,
            whole((slots, width)),
            wide,
            tall,
            whole((capacity, slots)),
            whole((slots, capacity)),
            whole((width, experts)),
            pl.BlockSpec((1, width, TILE), lambda i: (0, 0, i)),
        ],
        out_specs=[wide, wide, tall, tall, whole((slots, width))]
        + [whole((capacity, experts)), whole((capacity, 1))],
        out_shape=[
            low_shape(capacity, width),
            low_shape(capacity, width),
            low_shape(capacity, hidden_width),
            low_shape(capacity, hidden_width),
            low_shape(slots, width),
            low_shape(capacity, experts),
            wide_shape(capacity, 1),
        ],
        scratch_shapes=[
            pltpu.VMEM((capacity, width), F32),
            pltpu.VMEM((capacity, experts), F32),
            pltpu.VMEM((capacity, 1), F32),
        ],
        compiler_params=params(),
        cost_estimate=cost(8 * capacity * width * hidden_width, 8 * width * hidden_width),
    )(flags, arrived, cot, back, compact, expand, router, expert_in)


def owner_backward_kernel(
    flags_ref,
    returned_ref,
    to_tokens_ref,
    cotangent_ref,
    middle_ref,
    gain_ref,
    weight_ref,
    grad_middle_ref,
    grad_branch_ref,
    mine_ref,
    sent_ref,
    grad_gain_ref,
):
    half_rows = mine_ref.shape[0]
    middle = middle_ref[...]
    inverse = lax.rsqrt(jnp.mean(middle * middle, axis=1, keepdims=True) + EPSILON)
    normed = middle * inverse
    grad_second = dot(to_tokens_ref[...], returned_ref[...])
    grouped = (grad_second * normed).reshape(-1, GAIN_ROWS, grad_second.shape[1])
    grad_gain_ref[...] = jnp.sum(grouped, axis=0).astype(BF)
    scaled = grad_second * gain_ref[...]
    grad_middle = cotangent_ref[...].astype(F32) + inverse * (
        scaled - normed * jnp.mean(scaled * normed, axis=1, keepdims=True)
    )
    grad_middle_ref[...] = grad_middle
    grad_branch = grad_middle.astype(BF)
    grad_branch_ref[...] = grad_branch
    weight = weight_ref[:, : middle.shape[1]]
    grad_mixed = dot_nt(grad_branch, weight).astype(BF)
    for core in range(2):

        @pl.when(flags_ref[CORE] == core)
        def _(core=core):
            mine_ref[...] = grad_mixed[core * half_rows : (core + 1) * half_rows]
            sent_ref[...] = grad_mixed[(1 - core) * half_rows : (2 - core) * half_rows]


def owner_backward(flags, returned, to_tokens, cotangent, middle, gain, full_extra):
    rows, width = cotangent.shape
    shapes = [
        wide_shape(rows, width),
        low_shape(rows, width),
        low_shape(rows // 2, width),
        low_shape(rows // 2, width),
        low_shape(GAIN_ROWS, width),
    ]
    operands = [returned, to_tokens, cotangent, middle, gain, full_extra]
    return one_step(owner_backward_kernel, flags, operands, shapes)


GAIN_ROWS = 16


def deal_rows(flags_ref, total, keep_ref, send_ref, rows):
    core = flags_ref[CORE]
    for m in range(total.shape[0] // (2 * rows)):
        place = 2 * (flags_ref[PLACE] ^ m)
        keep_ref[m * rows : (m + 1) * rows, :] = total[
            pl.ds(pl.multiple_of((place + core) * rows, 8), rows), :
        ]
        send_ref[m * rows : (m + 1) * rows, :] = total[
            pl.ds(pl.multiple_of((place + 1 - core) * rows, 8), rows), :
        ].astype(BF)


def dealt(width, columns):
    return [wide_shape(width // 2, columns), low_shape(width // 2, columns)]


def weight_grads_kernel(
    rows,
    flags_ref,
    normed_ref,
    query_ref,
    near_ref,
    got_ref,
    mixed_ref,
    branch_ref,
    router_ref,
    gain_ref,
    projected_ref,
    keep_ref,
    send_ref,
    total,
):
    part = query_ref.shape[1]
    width, experts = router_ref.shape
    extra = total.shape[1] - 3 * part - width
    projected_ref[:, :part] = query_ref[...]
    for index in range(2):
        both = near_ref[index].astype(F32) + got_ref[index].astype(F32)
        projected_ref[:, (index + 1) * part : (index + 2) * part] = both.astype(BF)
    total[:, : 3 * part] = dot_tn(normed_ref[...], projected_ref[...])
    total[:, 3 * part : 3 * part + width] = dot_tn(mixed_ref[...], branch_ref[...])
    gain = dot_tn(gain_ref[...], jnp.ones((GAIN_ROWS, extra), BF))
    router = router_ref[...]
    router = jnp.concatenate([router, jnp.zeros((width, extra - experts), F32)], axis=1)
    lanes = lax.broadcasted_iota(jnp.int32, (1, extra), 1)
    total[:, 3 * part + width :] = jnp.where(lanes == experts, gain, router)
    deal_rows(flags_ref, total, keep_ref, send_ref, rows)


def weight_grads(flags, operands, rows):
    work_rows, width = operands[0].shape
    part = operands[1].shape[1]
    experts = operands[6].shape[1]
    columns = 3 * part + width + experts + 1
    columns += -columns % 128
    return one_step(
        functools.partial(weight_grads_kernel, rows),
        flags,
        operands,
        [low_shape(work_rows, 3 * part)] + dealt(width, columns),
        [pltpu.VMEM((width, columns), F32)],
        VMEM_BYTES,
    )


def all_to_all(array):
    return lax.all_to_all(array, AXES, split_axis=0, concat_axis=0, tiled=True)


def on_device(
    inputs,
    norm_one,
    w_query,
    w_key,
    w_value,
    w_output,
    norm_two,
    w_router,
    expert_in,
    expert_out,
    routes,
    cotangent,
):
    links = Links()
    level, core = links.level, links.core
    device = links.group * links.levels + level
    devices = links.groups * links.levels
    rows, width = inputs.shape
    half_rows = rows // 2
    half_width = width // 2
    experts = w_router.shape[1]
    own_rows = norm_one.shape[0]
    most = 2 * rows // experts
    capacity = 5 * rows // 4
    blocks = links.levels

    same = (level >> 1) ^ core
    flags = jnp.stack([core, level & 1, same, device, links.group >> 1]).astype(jnp.int32)

    mine = pick(core, inputs[:half_rows], inputs[half_rows:])
    got = links.swap_core(pick(core, inputs[half_rows:], inputs[:half_rows]))
    kept, cross = pack(
        flags,
        [w_query, w_key, w_value, w_output, w_router, routes.reshape(1, rows)]
        + [norm_one.reshape(1, own_rows), norm_two.reshape(1, own_rows)],
    )
    level_block = gather_levels(links, [kept, cross, kept, cross])
    level_rows = level_block.shape[0]
    got = gate(got, kept, cross)
    near, far = pick(same, mine, got), pick(same, got, mine)
    near_first = links.swap_level(near, 1)
    far_first = links.swap_level(far, 2)
    far_second = links.swap_level(far_first, 1)
    level_weights = level_block[:, : 3 * half_width]
    own_blocks = gather_groups(links, level_weights)
    chosen = gate(routes, level_block)[:, 0]
    picked = (chosen[:, None] == jnp.arange(experts, dtype=jnp.int32)[None, :]).astype(jnp.int32)
    rank = jnp.sum((jnp.cumsum(picked, axis=0) - picked) * picked, axis=1)
    place = chosen * most + rank
    slot_index = jnp.arange(experts * most, dtype=jnp.int32)
    to_slots = (slot_index[:, None] == place[None, :]).astype(BF)
    to_tokens = (place[:, None] == slot_index[None, :]).astype(BF)
    cot_slots = dot(to_slots, cotangent).astype(BF).reshape(experts, most, width)

    own_blocks = tie(*own_blocks, near_first, far_first, cot_slots)[:-3]
    other_blocks = [links.swap_core(part) for part in own_blocks]

    source = jnp.concatenate([near, near_first, far_first, far_second], axis=0).astype(F32)
    normed_work = (
        source * lax.rsqrt(jnp.mean(source * source, axis=-1, keepdims=True) + EPSILON)
    ).astype(BF)
    own_extra = gather_groups(links, gate(level_block[:, 3 * half_width :], *own_blocks))
    if level_rows % 16 == 0:
        queries, pair, weights = project(flags, normed_work, own_blocks, other_blocks)
    else:
        weights = in_order(links, own_blocks, other_blocks)
        projected = dot(normed_work, weights).astype(BF)
        queries, pair = projected[:, :half_width], projected[:, half_width:]
    pair_far = links.swap_core(pair)
    cot_arrived = all_to_all(gate(cot_slots, *own_blocks)).reshape(-1, width)
    *mixed_parts, attention_weights, inverse = attention_forward(queries, pair, pair_far)
    mixed_parts = tie(*mixed_parts, cot_arrived, *own_extra)[:4]

    own_extra = tie(*own_extra, *mixed_parts)[: len(own_extra)]
    other_extra = links.swap_core(jnp.concatenate(own_extra, axis=0))
    if level_rows % 16 == 0:
        full_extra, gain_two = assemble(flags, [*own_extra, other_extra], 2 * experts)
    else:
        other_parts = [
            other_extra[m * level_rows : (m + 1) * level_rows] for m in range(len(own_extra))
        ]
        full_extra = in_order(links, own_extra, other_parts)
        gain_two = full_extra[:, width + 2 * experts].astype(F32)[None]
    full_router = full_extra[:, width : width + experts]
    last_part = gate(mixed_parts[1], gain_two)
    back = [links.swap_level(mixed_parts[2], 2), links.swap_level(mixed_parts[3], 3)]
    back = tie(links.swap_level(last_part, 1), *back)
    tallies = full_extra[::own_rows, width + experts : width + 2 * experts].astype(F32)
    mine_only = (jnp.arange(experts, dtype=jnp.int32) == device).astype(F32)[None, :]
    counts = jnp.sum(tallies * mine_only, axis=1).astype(jnp.int32)
    offsets = jnp.cumsum(counts) - counts
    within = jnp.arange(most, dtype=jnp.int32)[None, :]
    slot_grid = offsets[:, None] + within
    usable = (within < counts[:, None]) & (slot_grid < capacity)
    slot_flat = jnp.where(usable, slot_grid, -1).reshape(-1)
    held_index = jnp.arange(capacity, dtype=jnp.int32)
    compact = (held_index[:, None] == slot_flat[None, :]).astype(BF)
    expand = (slot_flat[:, None] == held_index[None, :]).astype(BF)

    mixed_mine, mixed_sent = mixed_route(flags, [mixed_parts[0], *back])
    mixed_low, middle, second_slots = owner_forward(
        flags, mixed_mine, links.swap_core(mixed_sent), inputs, full_extra, gain_two, to_slots
    )
    arrived = all_to_all(second_slots.reshape(experts, most, width)).reshape(-1, width)

    cot_held, cot_back = cotangent_layer(gate(cot_arrived, second_slots), compact, expert_out)
    held, grad_result, hidden, grad_inner, grad_back, grad_logits, gate_rows = expert_layer(
        flags,
        gate(arrived, cot_back),
        cot_held,
        cot_back,
        compact,
        expand,
        full_router,
        expert_in,
    )
    grad_returned = all_to_all(grad_back.reshape(experts, most, width)).reshape(-1, width)
    grad_router = dot_tn(held, grad_logits)
    grad_weight_out = dot_tn(hidden, grad_result)
    grad_weight_in = dot_tn(held, grad_inner)
    result = dot(hidden, expert_out[0]).astype(BF).astype(F32)
    taken_back = dot(expand, (gate_rows * result).astype(BF)).astype(BF)
    grad_returned = gate(
        grad_returned, grad_weight_in, grad_weight_out, grad_router, taken_back, to_tokens
    )

    grad_middle, grad_branch, grad_mine, grad_sent, gain_rows = owner_backward(
        flags, grad_returned, to_tokens, cotangent, middle, gain_two, full_extra
    )
    routed = grad_route(flags, grad_mine, links.swap_core(grad_sent))
    got = [links.swap_level(routed[b], b) for b in (1, 2, 3)]

    got = tie(*got)
    taken_back = gate(taken_back, *got).reshape(experts, most, width)
    taken_arrived = all_to_all(taken_back).reshape(-1, width)
    grad_queries, grad_near, grad_far = attention_backward(
        queries,
        pair,
        pair_far,
        attention_weights,
        inverse,
        [routed[0], *got],
        mixed_parts,
    )
    got_pair = links.swap_core(grad_far)
    grad_projected, keep, send = weight_grads(
        flags,
        [normed_work, grad_queries, grad_near, got_pair]
        + [mixed_low, grad_branch, grad_router, gain_rows],
        level_rows,
    )
    grad_first_work = dot_nt(grad_projected, weights).astype(BF)
    core_sum = reduce_cores(links, keep, gate(send, taken_arrived))
    core_sum = gate(core_sum, grad_first_work)
    group_sum = reduce_groups(
        links, [core_sum[m * level_rows : (m + 1) * level_rows] for m in range(links.groups // 2)]
    )
    parts = gate(grad_first_work, core_sum).reshape(blocks, half_rows, width)
    back = tie(*[links.swap_level(parts[b], b) for b in (1, 2, 3)])
    back = tie(*back, group_sum)[:-1]
    near = (parts[0].astype(F32) + back[0].astype(F32)).astype(BF)
    far = (back[1].astype(F32) + back[2].astype(F32)).astype(BF)
    grad_first = workers_to_owner(links, near, far).astype(F32)
    source_own = inputs.astype(F32)
    inverse_one = lax.rsqrt(jnp.mean(source_own * source_own, axis=-1, keepdims=True) + EPSILON)
    normed_one = source_own * inverse_one
    grad_input = grad_middle + inverse_one * (
        grad_first - normed_one * jnp.mean(grad_first * normed_one, axis=-1, keepdims=True)
    )
    output = (middle + dot(to_tokens, taken_arrived)).astype(BF)

    sums = reduce_levels(links, gate(group_sum, *back), grad_input)
    *grad_weights, grad_w_output, grad_w_router, grad_norm_one, grad_norm_two = finish(
        flags,
        [*sums, w_query, w_key, w_value, norm_one.reshape(1, own_rows)],
        experts,
    )
    return (
        output,
        grad_input,
        grad_norm_one.reshape(own_rows),
        grad_weights[0],
        grad_weights[1],
        grad_weights[2],
        grad_w_output,
        grad_norm_two.reshape(own_rows),
        grad_w_router,
        grad_weight_in[None],
        grad_weight_out[None],
    )


def solution(mesh):
    return jax.shard_map(
        on_device,
        mesh=mesh,
        in_specs=(
            P(AXES, None),
            P(AXES),
            P(AXES, None),
            P(AXES, None),
            P(AXES, None),
            P(AXES, None),
            P(AXES),
            P(AXES, None),
            P(AXES, None, None),
            P(AXES, None, None),
            P(AXES, None),
            P(AXES, None),
        ),
        out_specs=(
            P(AXES, None),
            P(AXES, None),
            P(AXES),
            P(AXES, None),
            P(AXES, None),
            P(AXES, None),
            P(AXES, None),
            P(AXES),
            P(AXES, None),
            P(AXES, None, None),
            P(AXES, None, None),
        ),
        check_vma=False,
    )
```
